32 devices in a mesh: row: 2 (over y), col: 16 (over z, x, core).
Axes of the slice: x: 2, y: 2, z: 4, core: 2. Of those that a mesh axis runs over, the one named last changes fastest.
Arguments:
- latent: bfloat16 [2, 128, 128, 320], P(None, 'row', 'col'), may hold values from -28 to 28
- timestep: int32 [2], replicated, may hold values from 0 to 999
- group_norm_gain: float32 [320], replicated, may hold values from 0.5 to 1.5
- group_norm_bias: float32 [320], replicated, may hold values from -0.5 to 0.5
- conv_w: bfloat16 [3, 3, 320, 320], replicated, may hold values from -0.109375 to 0.109375
- conv_b: float32 [320], replicated, may hold values from -0.5 to 0.5
- embed_in: bfloat16 [320, 1280], replicated, may hold values from -0.3125 to 0.3125
- embed_out: bfloat16 [1280, 1280], replicated, may hold values from -0.15625 to 0.15625
- time_w: bfloat16 [1280, 320], replicated, may hold values from -0.15625 to 0.15625
- cotangent: bfloat16 [2, 128, 128, 320], P(None, 'row', 'col'), may hold values from -6 to 6
Outputs:
- block_out: bfloat16 [2, 128, 128, 320], P(None, 'row', 'col')
- input_grad: float32 [2, 128, 128, 320], P(None, 'row', 'col')
- conv_w_grad: float32 [320, 3, 3, 320], P('row')
- gain_grad: float32 [320], replicated
- bias_grad: float32 [320], replicated
- conv_b_grad: float32 [320], replicated
- time_w_grad: float32 [1280, 320], replicated
The draws below stay inside these ranges and needn't reach their ends.
All inputs are finite; a program needn't handle non-finite values.
Results may differ from the reference program's by a relative error of at most 0.0055.
Values may be sent and summed in bfloat16 or wider, within the bound.
No kernel may reach another device: no remote copies, remote signals or barrier semaphores. Data moves between devices by JAX's collectives and lax.ppermute only.
A program may use at most 128 MiB of HBM per device.

```python
import math
import jax
import jax.numpy as jnp
from jax import lax

C = 320
NORM_GROUPS = 32
TF = 320
TE = 1280
BATCH = 2
H = 128
W = 128


def draw_latent(key, part):
    base = jnp.clip(jax.random.normal(key, (BATCH, H, W, C), jnp.float32), -6.0, 6.0)
    row_count = jnp.arange(H, dtype=jnp.float32) / H
    column_count = jnp.arange(W, dtype=jnp.float32) / W
    spread = 3.0 ** (0.5 * row_count[:, None] + 0.5 * column_count[None, :])
    return (base * spread[None, :, :, None]).astype(jnp.bfloat16)


def level_of(key, dims, shards, least, largest):
    gain, own = 1.0, jax.random.fold_in(key, 6)
    for dim, parts in shards:
        steps = jnp.exp(jax.random.uniform(jax.random.fold_in(own, dim), (parts,), jnp.float32, least / len(shards), largest / len(shards)))
        gain = gain * jnp.repeat(steps, dims[dim] // parts).reshape([-1 if axis == dim else 1 for axis in range(len(dims))])
    return gain


def scatter_about(stream_key, extent, deviation, most, pieces=(), kind=jnp.bfloat16):
    drawn = deviation * jax.random.normal(stream_key, extent, jnp.float32)
    if pieces:
        drawn = drawn * level_of(stream_key, extent, pieces, -0.22, 0.18)
    return jnp.clip(drawn, -most, most).astype(kind)


def setup_inputs(seed: int = 0) -> dict:
    arg_keys = jax.random.split(jax.random.key(seed), 11)
    latent = draw_latent(jax.random.fold_in(arg_keys[10], 71), 0)
    timestep = jax.random.randint(arg_keys[1], (BATCH,), 0, 1000).astype(jnp.int32)
    group_norm_gain = jnp.clip(1.0 + 0.1 * jax.random.normal(arg_keys[2], (C,), jnp.float32), 0.5, 1.5)
    group_norm_bias = jnp.clip(jax.random.uniform(arg_keys[3], (C,), jnp.float32, -0.5, 0.5), -0.5, 0.5)
    conv_w = scatter_about(arg_keys[4], (3, 3, C, C), (9 * C) ** -0.5, 0.109375)
    conv_b = jnp.clip(jax.random.uniform(arg_keys[5], (C,), jnp.float32, -0.5, 0.5), -0.5, 0.5)
    embed_in = scatter_about(arg_keys[6], (TF, TE), TF ** -0.5, 0.3125)
    embed_out = scatter_about(arg_keys[7], (TE, TE), TE ** -0.5, 0.15625)
    time_w = scatter_about(arg_keys[8], (TE, C), TE ** -0.5, 0.15625)
    cotangent = scatter_about(arg_keys[9], (BATCH, H, W, C), 1.0, 6.0, ((1, 2), (2, 16)))
    return dict(latent=latent, timestep=timestep, group_norm_gain=group_norm_gain, group_norm_bias=group_norm_bias, conv_w=conv_w, conv_b=conv_b, embed_in=embed_in, embed_out=embed_out, time_w=time_w, cotangent=cotangent)


EPS = 1e-05

def embed(timestep, embed_in, embed_out):
    half = TF // 2
    freqs = jnp.exp(-math.log(10000.0) * jnp.arange(half, dtype=jnp.float32) / half)
    angles = timestep.astype(jnp.float32)[:, None] * freqs[None, :]
    sinus = jnp.concatenate([jnp.cos(angles), jnp.sin(angles)], axis=1).astype(jnp.bfloat16)
    first_hidden = jax.nn.silu(jnp.dot(sinus, embed_in, preferred_element_type=jnp.float32)).astype(jnp.bfloat16)
    return jax.nn.silu(jnp.dot(first_hidden, embed_out, preferred_element_type=jnp.float32)).astype(jnp.bfloat16)

def one_image(latent_img, temb_row, cot_img, group_norm_gain, group_norm_bias, conv_w, conv_b):
    row_count, column_count, channel_count = latent_img.shape
    channels_per_group = channel_count // NORM_GROUPS
    count = row_count * column_count * channels_per_group
    x = latent_img.astype(jnp.float32)
    grouped = x.reshape(row_count, column_count, NORM_GROUPS, channels_per_group)
    mean = lax.optimization_barrier(jnp.sum(grouped, axis=(0, 1, 3))) / count
    group_centered = grouped - mean[None, None, :, None]
    var = lax.optimization_barrier(jnp.sum(group_centered * group_centered, axis=(0, 1, 3))) / count
    inverse_deviation = lax.rsqrt(var + EPS)
    input_standardized = (group_centered * inverse_deviation[None, None, :, None]).reshape(row_count, column_count, channel_count)
    normed_output = input_standardized * group_norm_gain + group_norm_bias
    acts = jax.nn.silu(normed_output).astype(jnp.bfloat16)
    padded = jnp.pad(acts.astype(jnp.float32), ((1, 1), (1, 1), (0, 0)))
    weights = conv_w.astype(jnp.float32)
    conv = jnp.zeros((row_count, column_count, channel_count), jnp.float32)
    for kh in range(3):
        for kw in range(3):
            conv = conv + jnp.einsum('hwc,cd->hwd', padded[kh:kh + row_count, kw:kw + column_count], weights[kh, kw])
    block_out = (x + conv + conv_b + temb_row).astype(jnp.bfloat16)
    grad = cot_img.astype(jnp.float32)
    gpad = jnp.pad(grad, ((1, 1), (1, 1), (0, 0)))
    dacts = jnp.zeros((row_count, column_count, channel_count), jnp.float32)
    terms = []
    for kh in range(3):
        for kw in range(3):
            dacts = dacts + jnp.einsum('hwd,cd->hwc', gpad[2 - kh:2 - kh + row_count, 2 - kw:2 - kw + column_count], weights[kh, kw])
            terms.append(jnp.einsum('hwc,hwd->dc', padded[kh:kh + row_count, kw:kw + column_count], grad))
    wterm = jnp.stack(terms, axis=1).reshape(channel_count, 3, 3, channel_count)
    sig = jax.nn.sigmoid(normed_output)
    normed_gradient = dacts * sig * (1.0 + normed_output * (1.0 - sig))
    first = lax.optimization_barrier(jnp.sum(normed_gradient, axis=(0, 1)))
    second_moment = lax.optimization_barrier(jnp.sum(normed_gradient * input_standardized, axis=(0, 1)))
    gsum = lax.optimization_barrier(jnp.sum(grad, axis=(0, 1)))
    m_one = lax.optimization_barrier(jnp.sum((group_norm_gain * first).reshape(NORM_GROUPS, channels_per_group), axis=1)) / count
    m_two = lax.optimization_barrier(jnp.sum((group_norm_gain * second_moment).reshape(NORM_GROUPS, channels_per_group), axis=1)) / count
    dxhat = (normed_gradient * group_norm_gain).reshape(row_count, column_count, NORM_GROUPS, channels_per_group)
    input_grouped = input_standardized.reshape(row_count, column_count, NORM_GROUPS, channels_per_group)
    dx = inverse_deviation[None, None, :, None] * (dxhat - m_one[None, None, :, None] - input_grouped * m_two[None, None, :, None])
    input_grad = grad + dx.reshape(row_count, column_count, channel_count)
    return (block_out, input_grad, wterm, first, second_moment, gsum)

def reference(latent, timestep, group_norm_gain, group_norm_bias, conv_w, conv_b, embed_in, embed_out, time_w, cotangent):
    emb = embed(timestep, embed_in, embed_out)
    temb = jnp.dot(emb, time_w, preferred_element_type=jnp.float32)

    def step(items):
        return one_image(items[0], items[1], items[2], group_norm_gain, group_norm_bias, conv_w, conv_b)
    block_out, input_grad, wterm, first, second_moment, gsum = lax.map(step, (latent, temb, cotangent))
    scale = 1.0 / math.sqrt(BATCH * H * W)
    conv_w_grad = lax.optimization_barrier(jnp.sum(wterm, axis=0)) * scale
    gain_grad = lax.optimization_barrier(jnp.sum(second_moment, axis=0)) * scale
    bias_grad = lax.optimization_barrier(jnp.sum(first, axis=0)) * scale
    conv_b_grad = lax.optimization_barrier(jnp.sum(gsum, axis=0)) * scale
    time_w_grad = jnp.dot(emb.astype(jnp.float32).T, gsum) * scale
    return (block_out, input_grad, conv_w_grad, gain_grad, bias_grad, conv_b_grad, time_w_grad)
```

```python
import functools
import math

import jax
import jax.numpy as jnp
from jax import lax
from jax.experimental import pallas as pl
from jax.experimental.pallas import tpu as pltpu
from jax.sharding import PartitionSpec as P

NORM_GROUPS = 32
EPS = 1e-05
LANES = 128
F32 = jnp.float32
BF16 = jnp.bfloat16
AXES = ("row", "col")
VMEM_LIMIT = 48 * 1024 * 1024
HI = lax.Precision.HIGHEST


def iota(shape, dim):
    return lax.broadcasted_iota(jnp.int32, shape, dim)


def call(body, out_shape, scratch=(), flops=0, transcendentals=0, nbytes=4_000_000):
    return pl.pallas_call(
        body,
        out_shape=out_shape,
        scratch_shapes=list(scratch),
        compiler_params=pltpu.CompilerParams(vmem_limit_bytes=VMEM_LIMIT),
        cost_estimate=pl.CostEstimate(
            flops=flops, bytes_accessed=nbytes, transcendentals=transcendentals
        ),
    )


def group_matrix(channels, lanes):
    size = channels // NORM_GROUPS
    group = iota((channels, lanes), 1) & (NORM_GROUPS - 1)
    channel = iota((channels, lanes), 0)
    return jnp.where((channel >= group * size) & (channel < (group + 1) * size), 1.0, 0.0).astype(F32)


def group_sums(rows):
    lanes = LANES
    g = group_matrix(rows.shape[1], lanes)
    keep = iota((8, lanes), 1) < NORM_GROUPS
    s = jnp.dot(rows, g, precision=HI, preferred_element_type=F32)
    s = jnp.where(keep, s, 0.0)
    return lax.dot_general(
        s, g, (((1,), (1,)), ((), ())), precision=HI, preferred_element_type=F32
    )


def stack_rows(rows, channels):
    r = iota((8, channels), 0)
    out = jnp.zeros((8, channels), F32)
    for k, v in enumerate(rows):
        out = out + jnp.where(r == k, v, 0.0)
    return out


def stats_kernel(batch, x_ref, pay_ref):
    n, channels = x_ref.shape
    per = n // batch
    step = 64
    rows = []
    for b in range(batch):

        def add(i, c, b=b):
            start = pl.multiple_of(b * per + i * step, 16)
            v = x_ref[pl.ds(start, step), :].astype(F32).reshape(step // 8, 8, channels)
            return c[0] + jnp.sum(v, axis=0), c[1] + jnp.sum(v * v, axis=0)

        zero = jnp.zeros((8, channels), F32)
        s, q = lax.fori_loop(0, per // step, add, (zero, zero))
        rows.append((jnp.sum(s, axis=0, keepdims=True), jnp.sum(q, axis=0, keepdims=True)))
    stacked = stack_rows([r[0] for r in rows] + [r[1] for r in rows], channels)
    lanes = pay_ref.shape[-1]
    res = jnp.dot(
        stacked, group_matrix(channels, lanes), precision=HI, preferred_element_type=F32
    )
    first = iota((8, lanes), 0) * NORM_GROUPS
    lane = iota((8, lanes), 1)
    mine = (lane >= first) & (lane < first + NORM_GROUPS)
    row = jnp.sum(jnp.where(mine, res, 0.0), axis=0, keepdims=True)
    pay_ref[...] = jnp.broadcast_to(row[None], pay_ref.shape)


def affine_rows(st_ref, gain_ref, bias_ref, batch, count):
    channels = gain_ref.shape[-1]
    lanes = st_ref.shape[-1]
    total = jnp.sum(st_ref[...], axis=0)
    first = iota((8, lanes), 0) * NORM_GROUPS
    lane = iota((8, lanes), 1)
    mine = (lane >= first) & (lane < first + NORM_GROUPS)
    spread = jnp.where(mine, total, 0.0)
    sums = lax.dot_general(
        spread,
        group_matrix(channels, lanes),
        (((1,), (1,)), ((), ())),
        precision=HI,
        preferred_element_type=F32,
    )
    gain, bias = gain_ref[...], bias_ref[...]
    a, s, r, t = [], [], [], []
    for b in range(batch):
        mean = sums[b : b + 1] / count
        var = sums[batch + b : batch + b + 1] / count - mean * mean
        inv = lax.rsqrt(var + EPS)
        r.append(inv)
        t.append(-mean * inv)
        a.append(inv * gain)
        s.append(bias - mean * inv * gain)
    return stack_rows(a + s + r + t, channels)


def put_shifted(ap, b, h, v, left, right):
    t, w, c = v.shape
    j = iota((t, w, c), 1)
    ap[0, b, pl.ds(h, t)] = jnp.where(j == 0, left, pltpu.roll(v, 1, 1))
    ap[1, b, pl.ds(h, t)] = v
    ap[2, b, pl.ds(h, t)] = jnp.where(j == w - 1, right, pltpu.roll(v, w - 1, 1))


def fill_acts(ap, aff, x_ref, xt_ref, xb_ref, xl_ref, xr_ref):
    _, batch, tall, w, c = ap.shape
    high = tall - 2
    ri, rn = lax.axis_index("row"), lax.axis_size("row")
    ci, cn = lax.axis_index("col"), lax.axis_size("col")
    up = jnp.where(ri == 0, 0.0, 1.0)
    down = jnp.where(ri == rn - 1, 0.0, 1.0)
    west = jnp.where(ci == 0, 0.0, 1.0)
    east = jnp.where(ci == cn - 1, 0.0, 1.0)

    def silu(v):
        return v / (1.0 + jnp.exp(-v))

    t = 8
    for b in range(batch):
        a = aff[b : b + 1].reshape(1, 1, c)
        s = aff[batch + b : batch + b + 1].reshape(1, 1, c)

        def act(x, a=a, s=s):
            return silu(x * a + s)

        def body(i, _, b=b, act=act):
            start = pl.multiple_of(b * high * w + i * t * w, 16)
            v = act(x_ref[pl.ds(start, t * w), :].astype(F32).reshape(t, w, c))
            h = i * t + 1
            put_shifted(
                ap, b, h, v, act(xl_ref[b, pl.ds(h, t)]) * west, act(xr_ref[b, pl.ds(h, t)]) * east
            )
            return 0

        lax.fori_loop(0, high // t, body, 0)
        for ref, h, edge in ((xt_ref, 0, up), (xb_ref, tall - 1, down)):
            put_shifted(
                ap,
                b,
                h,
                act(ref[b * w : (b + 1) * w, :].reshape(1, w, c)) * edge,
                act(xl_ref[b, h : h + 1]) * (west * edge),
                act(xr_ref[b, h : h + 1]) * (east * edge),
            )


def tap_rows(ap, b, kh, kw):
    _, _, tall, w, c = ap.shape
    return ap[kw, b, kh : kh + tall - 2].reshape((tall - 2) * w, c).astype(BF16)


def wgrad_kernel(batch, count, scale, relative, *refs):
    (st_ref, gain_ref, bias_ref, x_ref, g_ref, xt_ref, xb_ref, xl_ref, xr_ref) = refs[:9]
    aff_ref, keep_ref, send_ref = refs[9:12]
    ap, gt, gp, part = refs[12:]
    channels = x_ref.shape[1]
    n = x_ref.shape[0]
    aff = affine_rows(st_ref, gain_ref, bias_ref, batch, count)
    aff_ref[...] = aff
    wide = gt.shape[0]
    step = LANES
    for i in range(n // step):
        v = g_ref[i * step : (i + 1) * step, :].astype(F32)
        v = jnp.concatenate([v, jnp.zeros((step, wide - channels), F32)], axis=1)
        gt[:, i * step : (i + 1) * step] = jnp.transpose(v).astype(BF16)
    _, rows, pieces, share, width = send_ref.shape
    if relative:
        me = lax.axis_index("row") * 2 + (lax.axis_index("col") & 1)
        for q in range(2 * rows):
            other = (me ^ ((q % rows) * 2 + q // rows)) * share
            gp[q * share : (q + 1) * share, :] = gt[pl.ds(pl.multiple_of(other, 16), share), :]
    else:
        gp[...] = gt[:channels, :]
    fill_acts(ap, aff, x_ref, xt_ref, xb_ref, xl_ref, xr_ref)
    part[:, 9 * channels :] = jnp.zeros((channels, part.shape[1] - 9 * channels), F32)
    per = n // batch
    for kh in range(3):
        for kw in range(3):
            tap = kh * 3 + kw
            acc = jnp.zeros((channels, channels), F32)
            for b in range(batch):
                acc = acc + jnp.dot(
                    gp[:, b * per : (b + 1) * per],
                    tap_rows(ap, b, kh, kw),
                    preferred_element_type=F32,
                )
            part[:, tap * channels : (tap + 1) * channels] = acc * scale
    for r in range(rows):
        for p in range(pieces):
            lane = slice(p * width, (p + 1) * width)
            keep_ref[r, p] = part[r * share : (r + 1) * share, lane]
            low = (rows + r) * share
            send_ref[0, r, p] = part[low : low + share, lane].astype(BF16)


def back_kernel(batch, *refs):
    aff_ref, x_ref, g_ref, gt_ref, gb_ref, gl_ref, gr_ref, w_ref = refs[:8]
    dn_ref, sums_ref, ap = refs[8:]
    _, _, tall, w, c = ap.shape
    high = tall - 2
    per = high * w
    t = 8
    rows = []
    totals = []
    for b in range(batch):

        def body(i, tot, b=b):
            start = pl.multiple_of(b * per + i * t * w, 16)
            v = g_ref[pl.ds(start, t * w), :].astype(F32).reshape(t, w, c)
            h = i * t + 1
            put_shifted(ap, b, h, v, gl_ref[b, pl.ds(h, t)], gr_ref[b, pl.ds(h, t)])
            return tot + jnp.sum(v, axis=0)

        tot = lax.fori_loop(0, high // t, body, jnp.zeros((w, c), F32))
        totals.append(jnp.sum(tot, axis=0, keepdims=True))
        for ref, h in ((gt_ref, 0), (gb_ref, tall - 1)):
            put_shifted(
                ap,
                b,
                h,
                ref[b * w : (b + 1) * w, :].reshape(1, w, c),
                gl_ref[b, h : h + 1],
                gr_ref[b, h : h + 1],
            )
    for b in range(batch):
        acc = jnp.zeros((per, c), F32)
        for kh in range(3):
            for kw in range(3):
                acc = acc + lax.dot_general(
                    tap_rows(ap, b, 2 - kh, 2 - kw),
                    w_ref[kh * 3 + kw],
                    (((1,), (1,)), ((), ())),
                    preferred_element_type=F32,
                )
        dn_ref[b * per : (b + 1) * per, :] = acc
    aff = aff_ref[...]
    for b in range(batch):
        a, s, r, o = (aff[k * batch + b : k * batch + b + 1] for k in range(4))

        def body(i, carry, b=b, a=a, s=s, r=r, o=o):
            rows_here = pl.ds(pl.multiple_of(b * per + i * 64, 16), 64)
            x = x_ref[rows_here, :].astype(F32)
            normed = x * a + s
            sig = 1.0 / (1.0 + jnp.exp(-normed))
            dn = dn_ref[rows_here, :] * sig * (1.0 + normed * (1.0 - sig))
            dn_ref[rows_here, :] = dn
            xhat = x * r + o
            return (
                carry[0] + jnp.sum(dn.reshape(8, 8, c), axis=0),
                carry[1] + jnp.sum((dn * xhat).reshape(8, 8, c), axis=0),
            )

        zero = jnp.zeros((8, c), F32)
        rows.append(lax.fori_loop(0, per // 64, body, (zero, zero)))
    sums_ref[...] = stack_rows(
        [jnp.sum(v[0], axis=0, keepdims=True) for v in rows]
        + [jnp.sum(v[1], axis=0, keepdims=True) for v in rows]
        + totals,
        c,
    )


def conv_kernel(batch, *refs):
    aff_ref, x_ref, xt_ref, xb_ref, xl_ref, xr_ref, w_ref, cb_ref, temb_ref = refs[:9]
    out_ref, ap = refs[9:]
    _, _, tall, w, c = ap.shape
    per = (tall - 2) * w
    fill_acts(ap, aff_ref[...], x_ref, xt_ref, xb_ref, xl_ref, xr_ref)
    for b in range(batch):
        acc = jnp.zeros((per, c), F32)
        for kh in range(3):
            for kw in range(3):
                acc = acc + jnp.dot(
                    tap_rows(ap, b, kh, kw), w_ref[kh * 3 + kw], preferred_element_type=F32
                )
        here = slice(b * per, (b + 1) * per)
        out = x_ref[here, :].astype(F32) + acc + cb_ref[...] + temb_ref[b : b + 1, :]
        out_ref[here, :] = out.astype(BF16)


def input_kernel(batch, count, scale, *refs):
    aff_ref, red_ref, gain_ref, x_ref, g_ref, dn_ref = refs[:6]
    out_ref, gain_out, bias_out, cb_out = refs[6:]
    n, c = x_ref.shape
    per = n // batch
    red = red_ref[...]
    aff = aff_ref[...]
    gain = gain_ref[...]
    m = group_sums(red * gain) / count
    total = lambda k: sum(red[k * batch + b : k * batch + b + 1] for b in range(batch)) * scale
    bias_out[...] = total(0)
    gain_out[...] = total(1)
    cb_out[...] = total(2)
    for b in range(batch):
        a, r, o = (aff[k * batch + b : k * batch + b + 1] for k in (0, 2, 3))
        m1 = r * m[b : b + 1]
        m2 = r * m[batch + b : batch + b + 1]

        def body(i, _, b=b, a=a, r=r, o=o, m1=m1, m2=m2):
            here = pl.ds(pl.multiple_of(b * per + i * 64, 16), 64)
            xhat = x_ref[here, :].astype(F32) * r + o
            out_ref[here, :] = g_ref[here, :].astype(F32) + (dn_ref[here, :] * a - m1 - xhat * m2)
            return 0

        lax.fori_loop(0, per // 64, body, 0)


def assemble_kernel(nz, own_ref, z_ref, x_ref, core_ref, out_ref, full):
    share, width = own_ref.shape[-2:]
    c = out_ref.shape[-1]
    col = lax.axis_index("col")
    core, xb, z = col & 1, (col >> 1) & 1, col >> 2

    def put(k, core, xb, z):
        row = pl.multiple_of(core * share, 16)
        lane = pl.multiple_of((xb * nz + z) * width, LANES)
        full[pl.ds(row, share), pl.ds(lane, width)] = k.astype(F32)

    put(own_ref[0], core, xb, z)
    for k in range(1, nz):
        put(z_ref[k - 1], core, xb, z ^ k)
    for k in range(nz):
        put(x_ref[k], core, 1 - xb, z ^ k)
    for half in range(2):
        for k in range(nz):
            put(core_ref[half * nz + k], 1 - core, xb ^ half, z ^ k)
    for tap in range(out_ref.shape[0]):
        out_ref[tap] = full[:, tap * c : (tap + 1) * c]


def embed(timestep, embed_in, embed_out):
    half = embed_in.shape[0] // 2
    freqs = jnp.exp(-math.log(10000.0) * jnp.arange(half, dtype=F32) / half)
    angles = timestep.astype(F32)[:, None] * freqs[None, :]
    sinus = jnp.concatenate([jnp.cos(angles), jnp.sin(angles)], axis=1).astype(BF16)
    first_hidden = jax.nn.silu(jnp.dot(sinus, embed_in, preferred_element_type=F32)).astype(BF16)
    return jax.nn.silu(jnp.dot(first_hidden, embed_out, preferred_element_type=F32)).astype(BF16)


def partner(value, bit):
    size = lax.axis_size("row") * lax.axis_size("col")
    return lax.ppermute(value, AXES, [(i, i ^ bit) for i in range(size)])


def halo(rows_last, rows_first, axis):
    devices = lax.axis_size(axis)
    up = [(i, i + 1) for i in range(devices - 1)]
    down = [(j, i) for i, j in up]
    return lax.ppermute(rows_last, axis, up), lax.ppermute(rows_first, axis, down)


def plus(*values):
    total = values[0].astype(F32)
    for v in values[1:]:
        total = total + v.astype(F32)
    return total


def reduce_weights(keep, send, nz):
    rows, pieces, share, width = keep.shape
    cols = lax.axis_size("col")
    col = lax.axis_index("col")
    xb, z = (col >> 1) & 1, col >> 2
    held = plus(keep, partner(send, 1)).reshape(rows, 2, nz, share, width)
    pick = lambda v, i, dim: lax.dynamic_index_in_dim(v, i, dim, keepdims=False)
    half = nz // 2
    a, b = held[:, :, :half], held[:, :, half:]
    a_in = partner(a[1].astype(BF16), cols)
    b_in = partner(pick(b, 1 - xb, 1).astype(BF16), 2)
    a = plus(a[0], a_in)
    b = plus(pick(b, xb, 1), b_in)
    a_in = partner(pick(a, 1 - xb, 0).astype(BF16), 2)
    b_in = partner(b[1].astype(BF16), cols)
    held = jnp.concatenate([plus(pick(a, xb, 0), a_in), plus(b[0], b_in)], axis=0)
    got = [partner(pick(held, z ^ k, 0).astype(BF16), 4 * k) for k in range(1, nz)]
    own = plus(pick(held, z, 0), *got).astype(BF16)[None]
    zs = jnp.concatenate([partner(own, 4 * k) for k in range(1, nz)], axis=0)
    chip = jnp.concatenate([own, zs], axis=0)
    xs = partner(chip, 2)
    others = partner(jnp.concatenate([chip, xs], axis=0), 1)
    return own, zs, xs, others


def local(
    latent,
    timestep,
    group_norm_gain,
    group_norm_bias,
    conv_w,
    conv_b,
    embed_in,
    embed_out,
    time_w,
    cotangent,
):
    batch, high, wide, channels = latent.shape
    rows, cols = lax.axis_size("row"), lax.axis_size("col")
    devices = rows * cols
    n = batch * high * wide
    count = high * rows * wide * cols * (channels // NORM_GROUPS)
    scale = 1.0 / math.sqrt(batch * high * rows * wide * cols)
    x2 = latent.reshape(n, channels)
    g2 = cotangent.reshape(n, channels)
    gain = group_norm_gain.reshape(1, channels)
    bias = group_norm_bias.reshape(1, channels)
    w9 = conv_w.reshape(9, channels, channels)

    lanes = -(-2 * batch * NORM_GROUPS // LANES) * LANES
    pay = call(
        functools.partial(stats_kernel, batch),
        jax.ShapeDtypeStruct((devices, 1, lanes), F32),
        flops=4 * n * channels,
    )(x2)
    stats = lax.all_to_all(pay, AXES, 0, 0)

    top, bottom = halo(
        jnp.concatenate([latent[:, -1:], cotangent[:, -1:]], axis=0),
        jnp.concatenate([latent[:, :1], cotangent[:, :1]], axis=0),
        "row",
    )
    tall = jnp.concatenate([top, jnp.concatenate([latent, cotangent], axis=0), bottom], axis=1)
    left, right = halo(tall[:, :, -1:], tall[:, :, :1], "col")
    top, bottom, left, right = (v.astype(F32) for v in (top, bottom, left, right))
    flat = lambda v: v.reshape(batch * wide, channels)
    xt, gt = flat(top[:batch]), flat(top[batch:])
    xb, gb = flat(bottom[:batch]), flat(bottom[batch:])
    xl, gl = left[:batch], left[batch:]
    xr, gr = right[:batch], right[batch:]

    shifted = pltpu.VMEM((3, batch, high + 2, wide, channels), F32)
    nz = cols // 4
    share = channels // (2 * rows)
    relative = rows == 2 and nz >= 2 and share % 16 == 0
    pieces = cols // 2 if relative else 1
    width = -(-9 * channels // (LANES * pieces)) * LANES
    padded = -(-channels // LANES) * LANES
    conv_flops = 2 * 9 * n * channels * channels
    if not relative:
        share = channels // 2
    keep_rows = rows if relative else 1
    aff, keep, send = call(
        functools.partial(wgrad_kernel, batch, count, scale, relative),
        (
            jax.ShapeDtypeStruct((8, channels), F32),
            jax.ShapeDtypeStruct((keep_rows, pieces, share, width), F32),
            jax.ShapeDtypeStruct((1, keep_rows, pieces, share, width), BF16),
        ),
        scratch=(
            shifted,
            pltpu.VMEM((padded, n), BF16),
            pltpu.VMEM((channels, n), BF16),
            pltpu.VMEM((channels, pieces * width), F32),
        ),
        flops=conv_flops,
    )(stats, gain, bias, x2, g2, xt, xb, xl, xr)

    dn, sums = call(
        functools.partial(back_kernel, batch),
        (
            jax.ShapeDtypeStruct((n, channels), F32),
            jax.ShapeDtypeStruct((8, channels), F32),
        ),
        scratch=(shifted,),
        flops=conv_flops,
    )(aff, x2, g2, gt, gb, gl, gr, w9)

    if relative:
        own, zs, xs, others = reduce_weights(keep, send[0], nz)
        grad = call(
            functools.partial(assemble_kernel, nz),
            jax.ShapeDtypeStruct((9, 2 * share, channels), F32),
            scratch=(pltpu.VMEM((2 * share, pieces * width), F32),),
        )(own, zs, xs, others)
    else:
        both = jnp.concatenate([keep[0, 0], send[0, 0, 0].astype(F32)], axis=0)
        both = lax.psum(both[:, : 9 * channels], AXES)
        mine = channels // rows
        grad = lax.dynamic_slice_in_dim(both, lax.axis_index("row") * mine, mine, 0)
        grad = jnp.transpose(grad.reshape(mine, 9, channels), (1, 0, 2))
    conv_w_grad = jnp.transpose(grad.reshape(3, 3, channels // rows, channels), (2, 0, 1, 3))

    bit = 1
    while bit < devices:
        sums = sums + partner(sums, bit)
        bit *= 2
    emb = embed(timestep, embed_in, embed_out)
    temb = jnp.dot(emb, time_w, preferred_element_type=F32)
    block_out = call(
        functools.partial(conv_kernel, batch),
        jax.ShapeDtypeStruct((n, channels), BF16),
        scratch=(shifted,),
        flops=conv_flops,
    )(aff, x2, xt, xb, xl, xr, w9, conv_b.reshape(1, channels), temb)

    vector = jax.ShapeDtypeStruct((1, channels), F32)
    input_grad, gain_grad, bias_grad, conv_b_grad = call(
        functools.partial(input_kernel, batch, count, scale),
        (jax.ShapeDtypeStruct((n, channels), F32), vector, vector, vector),
        flops=8 * n * channels,
    )(aff, sums, gain, x2, g2, dn)
    gsum = sums[2 * batch : 3 * batch]
    time_w_grad = jnp.dot(emb.astype(F32).T, gsum) * scale
    return (
        block_out.reshape(latent.shape),
        input_grad.reshape(latent.shape),
        conv_w_grad,
        gain_grad.reshape(channels),
        bias_grad.reshape(channels),
        conv_b_grad.reshape(channels),
        time_w_grad,
    )


def solution(mesh):
    return jax.shard_map(
        local,
        mesh=mesh,
        in_specs=(
            P(None, "row", "col", None),
            P(),
            P(),
            P(),
            P(),
            P(),
            P(),
            P(),
            P(),
            P(None, "row", "col", None),
        ),
        out_specs=(
            P(None, "row", "col", None),
            P(None, "row", "col", None),
            P("row", None, None, None),
            P(),
            P(),
            P(),
            P(),
        ),
        check_vma=False,
    )
```

```python
import functools
import math

import jax
import jax.numpy as jnp
from jax import lax
from jax.experimental import pallas as pl
from jax.experimental.pallas import tpu as pltpu
from jax.sharding import PartitionSpec as P

NORM_GROUPS = 32
EPS = 1e-05
LANES = 128
F32 = jnp.float32
BF16 = jnp.bfloat16
AXES = ("row", "col")
VMEM_LIMIT = 32 * 1024 * 1024
HI = lax.Precision.HIGHEST


def iota(shape, dim):
    return lax.broadcasted_iota(jnp.int32, shape, dim)


def call(body, out_shape, operands, after=(), scratch=(), flops=0, nbytes=2_000_000):
    used, waits = len(operands), len(after)

    def kernel(*refs):
        body(*refs[:used], *refs[used + waits :])

    vmem = pl.BlockSpec(memory_space=pltpu.VMEM)
    return pl.pallas_call(
        kernel,
        out_shape=out_shape,
        in_specs=[vmem] * used + [pl.BlockSpec(memory_space=pl.ANY)] * waits,
        out_specs=jax.tree.map(lambda _: vmem, out_shape),
        scratch_shapes=list(scratch),
        compiler_params=pltpu.CompilerParams(vmem_limit_bytes=VMEM_LIMIT),
        cost_estimate=pl.CostEstimate(flops=flops, bytes_accessed=nbytes, transcendentals=0),
    )(*operands, *after)


def group_matrix(channels, lanes):
    size = channels // NORM_GROUPS
    group = iota((channels, lanes), 1) & (NORM_GROUPS - 1)
    channel = iota((channels, lanes), 0)
    return jnp.where((channel >= group * size) & (channel < (group + 1) * size), 1.0, 0.0).astype(F32)


def group_sums(rows):
    lanes = LANES
    g = group_matrix(rows.shape[1], lanes)
    keep = iota((8, lanes), 1) < NORM_GROUPS
    s = jnp.dot(rows, g, precision=HI, preferred_element_type=F32)
    s = jnp.where(keep, s, 0.0)
    return lax.dot_general(
        s, g, (((1,), (1,)), ((), ())), precision=HI, preferred_element_type=F32
    )


def stack_rows(rows, channels):
    r = iota((8, channels), 0)
    out = jnp.zeros((8, channels), F32)
    for k, v in enumerate(rows):
        out = out + jnp.where(r == k, v, 0.0)
    return out


def stats_kernel(batch, w, rows, x_ref, g_ref, pay_ref, west_ref, east_ref, *edge_refs):
    n, channels = x_ref.shape
    per = n // batch
    step = 64
    t = step // w
    sums = []
    for k, ref in enumerate((x_ref, g_ref)):
        for b in range(batch):

            def add(i, c, b=b, k=k, ref=ref):
                start = pl.multiple_of(b * per + i * step, 16)
                v = ref[pl.ds(start, step), :].astype(F32).reshape(t, w, channels)
                west_ref[k * batch + b, pl.ds(i * t, t)] = v[:, :1]
                east_ref[k * batch + b, pl.ds(i * t, t)] = v[:, w - 1 :]
                if k:
                    return c
                return c[0] + jnp.sum(v, axis=0), c[1] + jnp.sum(v * v, axis=0)

            zero = jnp.zeros((w, channels), F32)
            s, q = lax.fori_loop(0, per // step, add, (zero, zero))
            if not k:
                sums.append((jnp.sum(s, axis=0, keepdims=True), jnp.sum(q, axis=0, keepdims=True)))
            last = ref[(b + 1) * per - 16 : (b + 1) * per, :].astype(F32)[16 - w :]
            first = ref[b * per : b * per + 16, :].astype(F32)[:w]
            if rows == 2:
                edges = (jnp.where(lax.axis_index("row") == 0, last, first),)
            else:
                edges = (last, first)
            for e, v in enumerate(edges):
                line, corner_w, corner_e = edge_refs[3 * e : 3 * e + 3]
                at = k * batch + b
                line[at * w : (at + 1) * w, :] = v
                corner_w[at] = v[:1]
                corner_e[at] = v[w - 1 :]
    stacked = stack_rows([r[0] for r in sums] + [r[1] for r in sums], channels)
    lanes = pay_ref.shape[-1]
    res = jnp.dot(
        stacked, group_matrix(channels, lanes), precision=HI, preferred_element_type=F32
    )
    first = iota((8, lanes), 0) * NORM_GROUPS
    lane = iota((8, lanes), 1)
    mine = (lane >= first) & (lane < first + NORM_GROUPS)
    row = jnp.sum(jnp.where(mine, res, 0.0), axis=0, keepdims=True)
    pay_ref[...] = jnp.broadcast_to(row[None], pay_ref.shape)


def affine_rows(st_ref, gain_ref, bias_ref, batch, count):
    channels = gain_ref.shape[-1]
    lanes = st_ref.shape[-1]
    total = jnp.sum(st_ref[...], axis=0)
    first = iota((8, lanes), 0) * NORM_GROUPS
    lane = iota((8, lanes), 1)
    mine = (lane >= first) & (lane < first + NORM_GROUPS)
    spread = jnp.where(mine, total, 0.0)
    sums = lax.dot_general(
        spread,
        group_matrix(channels, lanes),
        (((1,), (1,)), ((), ())),
        precision=HI,
        preferred_element_type=F32,
    )
    gain, bias = gain_ref[...].reshape(1, channels), bias_ref[...].reshape(1, channels)
    a, s, r, t = [], [], [], []
    for b in range(batch):
        mean = sums[b : b + 1] / count
        var = sums[batch + b : batch + b + 1] / count - mean * mean
        inv = lax.rsqrt(var + EPS)
        r.append(inv)
        t.append(-mean * inv)
        a.append(inv * gain)
        s.append(bias - mean * inv * gain)
    return stack_rows(a + s + r + t, channels)


def put_shifted(ap, b, h, v, left, right):
    t, w, c = v.shape
    j = iota((t, w, c), 1)
    ap[0, b, pl.ds(h, t)] = jnp.where(j == 0, left, pltpu.roll(v, 1, 1))
    ap[1, b, pl.ds(h, t)] = v
    ap[2, b, pl.ds(h, t)] = jnp.where(j == w - 1, right, pltpu.roll(v, w - 1, 1))


def edge_masks():
    ri, rn = lax.axis_index("row"), lax.axis_size("row")
    ci, cn = lax.axis_index("col"), lax.axis_size("col")
    flags = (ri == 0, ri == rn - 1, ci == 0, ci == cn - 1)
    return tuple(jnp.where(f, 0.0, 1.0) for f in flags)


def fill(ap, part, batch, fn, src_ref, halo, visit=None):
    _, _, tall, w, c = ap.shape
    high = tall - 2
    up, down, west, east = edge_masks()
    left, right, top, top_w, top_e, low, low_w, low_e = halo
    t = 8
    first = part * batch
    for b in range(batch):

        def body(i, carry, b=b):
            start = pl.multiple_of(b * high * w + i * t * w, 16)
            v = src_ref[pl.ds(start, t * w), :].astype(F32).reshape(t, w, c)
            h = i * t
            put_shifted(
                ap,
                b,
                h + 1,
                fn(b, v),
                fn(b, left[first + b, pl.ds(h, t)]) * west,
                fn(b, right[first + b, pl.ds(h, t)]) * east,
            )
            return carry if visit is None else visit(carry, v)

        out = lax.fori_loop(0, high // t, body, jnp.zeros((w, c), F32))
        if visit is not None:
            yield out
        for line, wc, ec, h, edge in (
            (top, top_w, top_e, 0, up),
            (low, low_w, low_e, tall - 1, down),
        ):
            at = first + b
            put_shifted(
                ap,
                b,
                h,
                fn(b, line[at * w : (at + 1) * w, :].reshape(1, w, c)) * edge,
                fn(b, wc[at : at + 1]) * (west * edge),
                fn(b, ec[at : at + 1]) * (east * edge),
            )


def fill_acts(ap, aff, batch, x_ref, halo):
    c = ap.shape[-1]

    def act(b, x):
        v = x * aff[b : b + 1].reshape(1, 1, c) + aff[batch + b : batch + b + 1].reshape(1, 1, c)
        return v / (1.0 + jnp.exp(-v))

    for _ in fill(ap, 0, batch, act, x_ref, halo):
        pass


def tap_rows(ap, b, kh, kw):
    _, _, tall, w, c = ap.shape
    return ap[kw, b, kh : kh + tall - 2].reshape((tall - 2) * w, c).astype(BF16)


def wgrad_kernel(batch, count, scale, relative, *refs):
    st_ref, gain_ref, bias_ref, x_ref, g_ref = refs[:5]
    halo = refs[5:13]
    aff_ref, keep_ref, send_ref = refs[13:16]
    ap, gt, gp, part = refs[16:]
    channels = x_ref.shape[1]
    n = x_ref.shape[0]
    aff = affine_rows(st_ref, gain_ref, bias_ref, batch, count)
    aff_ref[...] = aff
    wide = gt.shape[0]
    step = LANES
    for i in range(n // step):
        v = g_ref[i * step : (i + 1) * step, :].astype(F32)
        v = jnp.concatenate([v, jnp.zeros((step, wide - channels), F32)], axis=1)
        gt[:, i * step : (i + 1) * step] = jnp.transpose(v).astype(BF16)
    _, rows, pieces, share, width = send_ref.shape
    if relative:
        me = lax.axis_index("row") * 2 + (lax.axis_index("col") & 1)
        for q in range(2 * rows):
            other = (me ^ ((q % rows) * 2 + q // rows)) * share
            gp[q * share : (q + 1) * share, :] = gt[pl.ds(pl.multiple_of(other, 16), share), :]
    else:
        gp[...] = gt[:channels, :]
    fill_acts(ap, aff, batch, x_ref, halo)
    part[:, 9 * channels :] = jnp.zeros((channels, part.shape[1] - 9 * channels), F32)
    per = n // batch
    for kh in range(3):
        for kw in range(3):
            tap = kh * 3 + kw
            acc = jnp.zeros((channels, channels), F32)
            for b in range(batch):
                acc = acc + jnp.dot(
                    gp[:, b * per : (b + 1) * per],
                    tap_rows(ap, b, kh, kw),
                    preferred_element_type=F32,
                )
            part[:, tap * channels : (tap + 1) * channels] = acc * scale
    for r in range(rows):
        for p in range(pieces):
            lane = slice(p * width, (p + 1) * width)
            keep_ref[r, p] = part[r * share : (r + 1) * share, lane]
            low = (rows + r) * share
            send_ref[0, r, p] = part[low : low + share, lane].astype(BF16)


def back_kernel(batch, *refs):
    aff_ref, x_ref, g_ref = refs[:3]
    halo = refs[3:11]
    w_ref, dn_ref, sums_ref, ap = refs[11:]
    _, _, tall, w, c = ap.shape
    per = (tall - 2) * w
    rows = []
    totals = fill(
        ap, 1, batch, lambda b, v: v, g_ref, halo, lambda tot, v: tot + jnp.sum(v, axis=0)
    )
    totals = [jnp.sum(v, axis=0, keepdims=True) for v in totals]
    for b in range(batch):
        acc = jnp.zeros((per, c), F32)
        for kh in range(3):
            for kw in range(3):
                acc = acc + lax.dot_general(
                    tap_rows(ap, b, 2 - kh, 2 - kw),
                    w_ref[kh * 3 + kw],
                    (((1,), (1,)), ((), ())),
                    preferred_element_type=F32,
                )
        dn_ref[b * per : (b + 1) * per, :] = acc
    aff = aff_ref[...]
    for b in range(batch):
        a, s, r, o = (aff[k * batch + b : k * batch + b + 1] for k in range(4))

        def body(i, carry, b=b, a=a, s=s, r=r, o=o):
            rows_here = pl.ds(pl.multiple_of(b * per + i * 64, 16), 64)
            x = x_ref[rows_here, :].astype(F32)
            normed = x * a + s
            sig = 1.0 / (1.0 + jnp.exp(-normed))
            dn = dn_ref[rows_here, :] * sig * (1.0 + normed * (1.0 - sig))
            dn_ref[rows_here, :] = dn
            xhat = x * r + o
            return (
                carry[0] + jnp.sum(dn.reshape(8, 8, c), axis=0),
                carry[1] + jnp.sum((dn * xhat).reshape(8, 8, c), axis=0),
            )

        zero = jnp.zeros((8, c), F32)
        rows.append(lax.fori_loop(0, per // 64, body, (zero, zero)))
    sums_ref[...] = stack_rows(
        [jnp.sum(v[0], axis=0, keepdims=True) for v in rows]
        + [jnp.sum(v[1], axis=0, keepdims=True) for v in rows]
        + totals,
        c,
    )


def conv_kernel(batch, *refs):
    aff_ref, x_ref = refs[:2]
    halo = refs[2:10]
    w_ref, cb_ref, temb_ref, out_ref, ap = refs[10:]
    _, _, tall, w, c = ap.shape
    per = (tall - 2) * w
    fill_acts(ap, aff_ref[...], batch, x_ref, halo)
    bias = cb_ref[...].reshape(1, c)
    for b in range(batch):
        acc = jnp.zeros((per, c), F32)
        for kh in range(3):
            for kw in range(3):
                acc = acc + jnp.dot(
                    tap_rows(ap, b, kh, kw), w_ref[kh * 3 + kw], preferred_element_type=F32
                )
        here = slice(b * per, (b + 1) * per)
        out = x_ref[here, :].astype(F32) + acc + bias + temb_ref[b : b + 1, :]
        out_ref[here, :] = out.astype(BF16)


def input_kernel(batch, count, scale, *refs):
    aff_ref, red_ref, gain_ref, x_ref, g_ref, dn_ref, emb_ref = refs[:7]
    out_ref, gain_out, bias_out, cb_out, tw_out = refs[7:]
    n, c = x_ref.shape
    per = n // batch
    red = red_ref[...]
    aff = aff_ref[...]
    gain = gain_ref[...].reshape(1, c)
    m = group_sums(red * gain) / count
    total = lambda k: sum(red[k * batch + b : k * batch + b + 1] for b in range(batch)) * scale
    bias_out[...] = total(0).reshape(c)
    gain_out[...] = total(1).reshape(c)
    cb_out[...] = total(2).reshape(c)
    rest = red[2 * batch : 3 * batch] * scale
    parts = []
    for _ in range(3):
        parts.append(rest.astype(BF16))
        rest = rest - parts[-1].astype(F32)
    emb = emb_ref[...]
    tw_out[...] = sum(
        lax.dot_general(p, emb, (((0,), (0,)), ((), ())), preferred_element_type=F32)
        for p in reversed(parts)
    )
    for b in range(batch):
        a, r, o = (aff[k * batch + b : k * batch + b + 1] for k in (0, 2, 3))
        m1 = r * m[b : b + 1]
        m2 = r * m[batch + b : batch + b + 1]

        def body(i, _, b=b, a=a, r=r, o=o, m1=m1, m2=m2):
            here = pl.ds(pl.multiple_of(b * per + i * 64, 16), 64)
            xhat = x_ref[here, :].astype(F32) * r + o
            out_ref[here, :] = g_ref[here, :].astype(F32) + (dn_ref[here, :] * a - m1 - xhat * m2)
            return 0

        lax.fori_loop(0, per // 64, body, 0)


def place():
    col = lax.axis_index("col")
    return col & 1, (col >> 1) & 1, col >> 2


def step_one(nz, keep_ref, got_ref, a_send, a_keep, b_send, b_keep):
    _, xb, _ = place()
    half = nz // 2
    total = lambda r, p: keep_ref[r, p] + got_ref[r, p].astype(F32)
    for x in range(2):
        for z in range(half):
            p = x * nz + z
            a_send[x, z] = total(1, p).astype(BF16)
            a_keep[x, z] = total(0, p)
    for r in range(2):
        for z in range(half):
            b_send[r, z] = total(r, (1 - xb) * nz + half + z).astype(BF16)
            b_keep[r, z] = total(r, xb * nz + half + z)


def step_two(nz, a_got, a_keep, b_got, b_keep, a_send, a_next, b_send, b_next):
    _, xb, _ = place()
    for z in range(nz // 2):
        a_send[z] = (a_keep[1 - xb, z] + a_got[1 - xb, z].astype(F32)).astype(BF16)
        a_next[z] = a_keep[xb, z] + a_got[xb, z].astype(F32)
        b_send[z] = (b_keep[1, z] + b_got[1, z].astype(F32)).astype(BF16)
        b_next[z] = b_keep[0, z] + b_got[0, z].astype(F32)


def step_three(nz, a_got, a_keep, b_got, b_keep, own_ref, *refs):
    sends, held = refs[: nz - 1], refs[nz - 1]
    _, _, zb = place()
    half = nz // 2
    for z in range(half):
        held[z] = a_keep[z] + a_got[z].astype(F32)
        held[half + z] = b_keep[z] + b_got[z].astype(F32)
    own_ref[...] = held[zb]
    for k in range(1, nz):
        sends[k - 1][...] = held[zb ^ k].astype(BF16)


def step_four(own_ref, *refs):
    total = own_ref[...]
    for g in refs[:-1]:
        total = total + g[...].astype(F32)
    refs[-1][...] = total.astype(BF16)


def step_five(nz, *refs):
    out = refs[-1]
    width = refs[0].shape[-1]
    _, xb, zb = place()
    for k, ref in enumerate(refs[:-1]):
        p = (xb ^ (k % 2)) * nz + (zb ^ (k // 2))
        out[:, pl.ds(pl.multiple_of(p * width, LANES), width)] = ref[...]


def step_six(mine_ref, other_ref, out_ref, full):
    core, _, _ = place()
    share = mine_ref.shape[0]
    c = out_ref.shape[-1]
    full[pl.ds(pl.multiple_of(core * share, 16), share), :] = mine_ref[...].astype(F32)
    full[pl.ds(pl.multiple_of((1 - core) * share, 16), share), :] = other_ref[...].astype(F32)
    for tap in range(out_ref.shape[0]):
        out_ref[tap] = full[:, tap * c : (tap + 1) * c]


def embed(timestep, embed_in, embed_out):
    half = embed_in.shape[0] // 2
    freqs = jnp.exp(-math.log(10000.0) * jnp.arange(half, dtype=F32) / half)
    angles = timestep.astype(F32)[:, None] * freqs[None, :]
    sinus = jnp.concatenate([jnp.cos(angles), jnp.sin(angles)], axis=1).astype(BF16)
    first_hidden = jax.nn.silu(jnp.dot(sinus, embed_in, preferred_element_type=F32)).astype(BF16)
    return jax.nn.silu(jnp.dot(first_hidden, embed_out, preferred_element_type=F32)).astype(BF16)


def partner(value, bit):
    size = lax.axis_size("row") * lax.axis_size("col")
    return lax.ppermute(value, AXES, [(i, i ^ bit) for i in range(size)])


def shift(value, down, right):
    rows, cols = lax.axis_size("row"), lax.axis_size("col")
    pairs = []
    for r in range(rows):
        for c in range(cols):
            to = (r + down, c + right)
            if 0 <= to[0] < rows and 0 <= to[1] < cols:
                pairs.append((r * cols + c, to[0] * cols + to[1]))
    return lax.ppermute(value, AXES, pairs)


def swap(value, right):
    cols = lax.axis_size("col")
    pairs = []
    for r in range(2):
        for c in range(cols):
            if 0 <= c + right < cols:
                pairs.append((r * cols + c, (1 - r) * cols + c + right))
    return lax.ppermute(value, AXES, pairs)


def local(
    latent,
    timestep,
    group_norm_gain,
    group_norm_bias,
    conv_w,
    conv_b,
    embed_in,
    embed_out,
    time_w,
    cotangent,
):
    batch, high, wide, channels = latent.shape
    rows, cols = lax.axis_size("row"), lax.axis_size("col")
    devices = rows * cols
    n = batch * high * wide
    count = high * rows * wide * cols * (channels // NORM_GROUPS)
    scale = 1.0 / math.sqrt(batch * high * rows * wide * cols)
    x2 = latent.reshape(n, channels)
    g2 = cotangent.reshape(n, channels)
    w9 = conv_w.reshape(9, channels, channels)
    of = jax.ShapeDtypeStruct

    lanes = -(-2 * batch * NORM_GROUPS // LANES) * LANES
    column = of((2 * batch, high, 1, channels), F32)
    edge = (
        of((2 * batch * wide, channels), F32),
        of((2 * batch, 1, channels), F32),
        of((2 * batch, 1, channels), F32),
    )
    pay, west, east, *edges = call(
        functools.partial(stats_kernel, batch, wide, rows),
        (of((devices, 1, lanes), F32), column, column, *(edge * (1 if rows == 2 else 2))),
        (x2, g2),
    )
    left, right = shift(east, 0, 1), shift(west, 0, -1)
    if rows == 2:
        line, corner_w, corner_e = edges
        top = (swap(line, 0), swap(corner_e, 1), swap(corner_w, -1))
        low = top
    else:
        line, corner_w, corner_e = edges[:3]
        top = (shift(line, 1, 0), shift(corner_e, 1, 1), shift(corner_w, 1, -1))
        line, corner_w, corner_e = edges[3:]
        low = (shift(line, -1, 0), shift(corner_e, -1, 1), shift(corner_w, -1, -1))
    stats = lax.all_to_all(pay, AXES, 0, 0)
    halo = (left, right, *top, *low)

    shifted = pltpu.VMEM((3, batch, high + 2, wide, channels), F32)
    nz = cols // 4
    share = channels // (2 * rows)
    relative = rows == 2 and nz >= 2 and share % 16 == 0
    pieces = cols // 2 if relative else 1
    width = -(-9 * channels // (LANES * pieces)) * LANES
    padded = -(-channels // LANES) * LANES
    conv_flops = 2 * 9 * n * channels * channels
    if not relative:
        share = channels // 2
    keep_rows = rows if relative else 1
    aff, keep, send = call(
        functools.partial(wgrad_kernel, batch, count, scale, relative),
        (
            of((8, channels), F32),
            of((keep_rows, pieces, share, width), F32),
            of((1, keep_rows, pieces, share, width), BF16),
        ),
        (stats, group_norm_gain, group_norm_bias, x2, g2, *halo),
        scratch=(
            shifted,
            pltpu.VMEM((padded, n), BF16),
            pltpu.VMEM((channels, n), BF16),
            pltpu.VMEM((channels, pieces * width), F32),
        ),
        flops=conv_flops,
    )

    if relative:
        half = nz // 2
        many = lambda k, dtype: of((*k, share, width), dtype)
        got = partner(send[0], 1)
        a_send, a_keep, b_send, b_keep = call(
            functools.partial(step_one, nz),
            (many((2, half), BF16), many((2, half), F32)) * 2,
            (keep, got),
        )
        a_got, b_got = partner(a_send, cols), partner(b_send, 2)
        first = (a_send, b_send)
    else:
        first = ()

    dn, sums = call(
        functools.partial(back_kernel, batch),
        (of((n, channels), F32), of((8, channels), F32)),
        (aff, x2, g2, *halo, w9),
        after=first,
        scratch=(shifted,),
        flops=conv_flops,
    )
    emb = embed(timestep, embed_in, embed_out)
    temb = jnp.dot(emb, time_w, preferred_element_type=F32)

    if relative:
        a_send, a_keep, b_send, b_keep = call(
            functools.partial(step_two, nz),
            (many((half,), BF16), many((half,), F32)) * 2,
            (a_got, a_keep, b_got, b_keep),
            after=(sums,),
        )
        a_got, b_got = partner(a_send, 2), partner(b_send, cols)
        own, *sends = call(
            functools.partial(step_three, nz),
            (many((), F32), *[many((), BF16)] * (nz - 1)),
            (a_got, a_keep, b_got, b_keep),
            scratch=(pltpu.VMEM((nz, share, width), F32),),
        )
        gots = [partner(v, 4 * (k + 1)) for k, v in enumerate(sends)]
        second = tuple(sends)
    else:
        second = ()

    block_out = call(
        functools.partial(conv_kernel, batch),
        of((n, channels), BF16),
        (aff, x2, *halo, w9, conv_b, temb),
        after=second,
        scratch=(shifted,),
        flops=conv_flops,
    )
    bit = 1
    while bit < devices:
        sums = sums + partner(sums, bit)
        bit *= 2

    if relative:
        own = call(step_four, many((), BF16), (own, *gots), after=(block_out,))
        others = [partner(own, 2 * k) for k in range(1, pieces)]
        third = (own,)
    else:
        third = ()

    vector = of((channels,), F32)
    input_grad, gain_grad, bias_grad, conv_b_grad, time_grad = call(
        functools.partial(input_kernel, batch, count, scale),
        (of((n, channels), F32), vector, vector, vector, of((channels, emb.shape[1]), F32)),
        (aff, sums, group_norm_gain, x2, g2, dn, emb),
        after=third,
        flops=8 * n * channels,
    )

    if relative:
        mine = call(
            functools.partial(step_five, nz),
            of((share, pieces * width), BF16),
            (own, *others),
            after=(input_grad,),
        )
        grad = call(
            step_six,
            of((9, 2 * share, channels), F32),
            (mine, partner(mine, 1)),
            scratch=(pltpu.VMEM((2 * share, pieces * width), F32),),
        )
    else:
        both = jnp.concatenate([keep[0, 0], send[0, 0, 0].astype(F32)], axis=0)
        both = lax.psum(both[:, : 9 * channels], AXES)
        mine = channels // rows
        grad = lax.dynamic_slice_in_dim(both, lax.axis_index("row") * mine, mine, 0)
        grad = jnp.transpose(grad.reshape(mine, 9, channels), (1, 0, 2))
    conv_w_grad = jnp.transpose(grad.reshape(3, 3, channels // rows, channels), (2, 0, 1, 3))
    return (
        block_out.reshape(latent.shape),
        input_grad.reshape(latent.shape),
        conv_w_grad,
        gain_grad,
        bias_grad,
        conv_b_grad,
        time_grad.T,
    )


def solution(mesh):
    return jax.shard_map(
        local,
        mesh=mesh,
        in_specs=(
            P(None, "row", "col", None),
            P(),
            P(),
            P(),
            P(),
            P(),
            P(),
            P(),
            P(),
            P(None, "row", "col", None),
        ),
        out_specs=(
            P(None, "row", "col", None),
            P(None, "row", "col", None),
            P("row", None, None, None),
            P(),
            P(),
            P(),
            P(),
        ),
        check_vma=False,
    )
```

```python
import functools
import math

import jax
import jax.numpy as jnp
from jax import lax
from jax.experimental import pallas as pl
from jax.experimental.pallas import tpu as pltpu
from jax.sharding import PartitionSpec as P

NORM_GROUPS = 32
EPS = 1e-05
LANES = 128
F32 = jnp.float32
BF16 = jnp.bfloat16
AXES = ("row", "col")
VMEM_LIMIT = 20 * 1024 * 1024
HI = lax.Precision.HIGHEST


def iota(shape, dim):
    return lax.broadcasted_iota(jnp.int32, shape, dim)


def call(body, out_shape, operands, far=(), after=(), scratch=(), flops=0, nbytes=2_000_000):
    count, used, waits = len(far), len(operands), len(after)

    def kernel(*refs):
        ins = refs[:count]
        rest = refs[count : count + used] + refs[count + used + waits :]
        if not count:
            return body(*rest)
        holds, sems = rest[-1 - count : -1], rest[-1]
        copies = [
            pltpu.make_async_copy(ins[i], holds[i], sems.at[i]) for i in range(count)
        ]
        for c in copies:
            c.start()

        def loader(i):
            def load():
                copies[i].wait()
                return holds[i]

            return load

        body(*[loader(i) for i in range(count)], *rest[: -1 - count])

    vmem = pl.BlockSpec(memory_space=pltpu.VMEM)
    scratch = list(scratch)
    if count:
        scratch += [pltpu.VMEM(v.shape, v.dtype) for v in far]
        scratch.append(pltpu.SemaphoreType.DMA((count,)))
    return pl.pallas_call(
        kernel,
        out_shape=out_shape,
        in_specs=[pl.BlockSpec(memory_space=pltpu.HBM)] * count
        + [vmem] * used
        + [pl.BlockSpec(memory_space=pl.ANY)] * waits,
        out_specs=jax.tree.map(lambda _: vmem, out_shape),
        scratch_shapes=scratch,
        compiler_params=pltpu.CompilerParams(vmem_limit_bytes=VMEM_LIMIT),
        cost_estimate=pl.CostEstimate(flops=flops, bytes_accessed=nbytes, transcendentals=0),
    )(*far, *operands, *after)


def group_matrix(channels, lanes):
    size = channels // NORM_GROUPS
    group = iota((channels, lanes), 1) & (NORM_GROUPS - 1)
    channel = iota((channels, lanes), 0)
    return jnp.where((channel >= group * size) & (channel < (group + 1) * size), 1.0, 0.0).astype(F32)


def group_sums(rows):
    lanes = LANES
    g = group_matrix(rows.shape[1], lanes)
    keep = iota((8, lanes), 1) < NORM_GROUPS
    s = jnp.dot(rows, g, precision=HI, preferred_element_type=F32)
    s = jnp.where(keep, s, 0.0)
    return lax.dot_general(
        s, g, (((1,), (1,)), ((), ())), precision=HI, preferred_element_type=F32
    )


def stack_rows(rows, channels):
    r = iota((8, channels), 0)
    out = jnp.zeros((8, channels), F32)
    for k, v in enumerate(rows):
        out = out + jnp.where(r == k, v, 0.0)
    return out


def stats_kernel(batch, w, x_load, g_load, top_ref, low_ref, pay_ref, west_ref, east_ref):
    sums = []
    step = 64
    t = step // w
    top, low = top_ref[...].astype(F32), low_ref[...].astype(F32)
    for k, load in enumerate((x_load, g_load)):
        ref = load()
        n, channels = ref.shape
        per = n // batch
        high = per // w
        for b in range(batch):
            at = k * batch + b

            def add(i, c, b=b, k=k, ref=ref, at=at):
                start = pl.multiple_of(b * per + i * step, 16)
                v = ref[pl.ds(start, step), :].astype(F32).reshape(t, w, channels)
                west_ref[at, pl.ds(i * t + 1, t)] = v[:, :1]
                east_ref[at, pl.ds(i * t + 1, t)] = v[:, w - 1 :]
                if k:
                    return c
                return c[0] + jnp.sum(v, axis=0), c[1] + jnp.sum(v * v, axis=0)

            zero = jnp.zeros((w, channels), F32)
            s, q = lax.fori_loop(0, per // step, add, (zero, zero))
            if not k:
                sums.append((jnp.sum(s, axis=0, keepdims=True), jnp.sum(q, axis=0, keepdims=True)))
            for v, h in ((top, 0), (low, high + 1)):
                west_ref[at, h] = v[at * w : at * w + 1]
                east_ref[at, h] = v[(at + 1) * w - 1 : (at + 1) * w]
    stacked = stack_rows([r[0] for r in sums] + [r[1] for r in sums], channels)
    lanes = pay_ref.shape[-1]
    res = jnp.dot(
        stacked, group_matrix(channels, lanes), precision=HI, preferred_element_type=F32
    )
    first = iota((8, lanes), 0) * NORM_GROUPS
    lane = iota((8, lanes), 1)
    mine = (lane >= first) & (lane < first + NORM_GROUPS)
    row = jnp.sum(jnp.where(mine, res, 0.0), axis=0, keepdims=True)
    pay_ref[...] = jnp.broadcast_to(row[None], pay_ref.shape)


def affine_rows(st_ref, gain_ref, bias_ref, batch, count):
    channels = gain_ref.shape[-1]
    lanes = st_ref.shape[-1]
    total = jnp.sum(st_ref[...], axis=0)
    first = iota((8, lanes), 0) * NORM_GROUPS
    lane = iota((8, lanes), 1)
    mine = (lane >= first) & (lane < first + NORM_GROUPS)
    spread = jnp.where(mine, total, 0.0)
    sums = lax.dot_general(
        spread,
        group_matrix(channels, lanes),
        (((1,), (1,)), ((), ())),
        precision=HI,
        preferred_element_type=F32,
    )
    gain, bias = gain_ref[...].reshape(1, channels), bias_ref[...].reshape(1, channels)
    a, s, r, t = [], [], [], []
    for b in range(batch):
        mean = sums[b : b + 1] / count
        var = sums[batch + b : batch + b + 1] / count - mean * mean
        inv = lax.rsqrt(var + EPS)
        r.append(inv)
        t.append(-mean * inv)
        a.append(inv * gain)
        s.append(bias - mean * inv * gain)
    return stack_rows(a + s + r + t, channels)


def put_shifted(ap, b, h, v, left, right):
    t, w, c = v.shape
    j = iota((t, w, c), 1)
    ap[0, b, pl.ds(h, t)] = jnp.where(j == 0, left, pltpu.roll(v, 1, 1))
    ap[1, b, pl.ds(h, t)] = v
    ap[2, b, pl.ds(h, t)] = jnp.where(j == w - 1, right, pltpu.roll(v, w - 1, 1))


def edge_masks():
    ri, rn = lax.axis_index("row"), lax.axis_size("row")
    ci, cn = lax.axis_index("col"), lax.axis_size("col")
    flags = (ri == 0, ri == rn - 1, ci == 0, ci == cn - 1)
    return tuple(jnp.where(f, 0.0, 1.0) for f in flags)


def fill(ap, part, batch, fn, src_ref, halo, visit=None):
    _, _, tall, w, c = ap.shape
    high = tall - 2
    up, down, west, east = edge_masks()
    left, right, top, low = halo
    top, low = top[...].astype(F32), low[...].astype(F32)
    t = 8
    first = part * batch
    for b in range(batch):

        def body(i, carry, b=b):
            start = pl.multiple_of(b * high * w + i * t * w, 16)
            v = src_ref[pl.ds(start, t * w), :].astype(F32).reshape(t, w, c)
            h = i * t
            put_shifted(
                ap,
                b,
                h + 1,
                fn(b, v),
                fn(b, left[first + b, pl.ds(h + 1, t)]) * west,
                fn(b, right[first + b, pl.ds(h + 1, t)]) * east,
            )
            return carry if visit is None else visit(carry, v)

        out = lax.fori_loop(0, high // t, body, jnp.zeros((w, c), F32))
        if visit is not None:
            yield out
        for line, h, edge in ((top, 0, up), (low, tall - 1, down)):
            at = first + b
            put_shifted(
                ap,
                b,
                h,
                fn(b, line[at * w : (at + 1) * w].reshape(1, w, c)) * edge,
                fn(b, left[at, h : h + 1]) * (west * edge),
                fn(b, right[at, h : h + 1]) * (east * edge),
            )


def fill_acts(ap, aff, batch, x_ref, halo):
    c = ap.shape[-1]

    def act(b, x):
        v = x * aff[b : b + 1].reshape(1, 1, c) + aff[batch + b : batch + b + 1].reshape(1, 1, c)
        return v / (1.0 + jnp.exp(-v))

    for _ in fill(ap, 0, batch, act, x_ref, halo):
        pass


def tap_rows(ap, b, kh, kw):
    _, _, tall, w, c = ap.shape
    return ap[kw, b, kh : kh + tall - 2].reshape((tall - 2) * w, c).astype(BF16)


def wgrad_kernel(batch, count, scale, relative, *refs):
    x_load, g_load, gain_load, bias_load, st_ref = refs[:5]
    halo = refs[5:9]
    aff_ref, keep_ref, send_ref = refs[9:12]
    ap, gt, gp, part = refs[12:]
    gain_ref, bias_ref = gain_load(), bias_load()
    x_ref, g_ref = x_load(), g_load()
    channels = x_ref.shape[1]
    n = x_ref.shape[0]
    aff = affine_rows(st_ref, gain_ref, bias_ref, batch, count)
    aff_ref[...] = aff
    wide = gt.shape[0]
    step = LANES
    for i in range(n // step):
        v = g_ref[i * step : (i + 1) * step, :].astype(F32)
        v = jnp.concatenate([v, jnp.zeros((step, wide - channels), F32)], axis=1)
        gt[:, i * step : (i + 1) * step] = jnp.transpose(v).astype(BF16)
    _, rows, pieces, share, width = send_ref.shape
    if relative:
        me = lax.axis_index("row") * 2 + (lax.axis_index("col") & 1)
        for q in range(2 * rows):
            other = (me ^ ((q % rows) * 2 + q // rows)) * share
            gp[q * share : (q + 1) * share, :] = gt[pl.ds(pl.multiple_of(other, 16), share), :]
    else:
        gp[...] = gt[:channels, :]
    fill_acts(ap, aff, batch, x_ref, halo)
    part[:, 9 * channels :] = jnp.zeros((channels, part.shape[1] - 9 * channels), F32)
    per = n // batch
    for kh in range(3):
        for kw in range(3):
            tap = kh * 3 + kw
            acc = jnp.zeros((channels, channels), F32)
            for b in range(batch):
                acc = acc + jnp.dot(
                    gp[:, b * per : (b + 1) * per],
                    tap_rows(ap, b, kh, kw),
                    preferred_element_type=F32,
                )
            part[:, tap * channels : (tap + 1) * channels] = acc * scale
    for r in range(rows):
        for p in range(pieces):
            lane = slice(p * width, (p + 1) * width)
            keep_ref[r, p] = part[r * share : (r + 1) * share, lane]
            low = (rows + r) * share
            send_ref[0, r, p] = part[low : low + share, lane].astype(BF16)


def back_kernel(batch, *refs):
    g_load, w_load, x_load, aff_ref = refs[:4]
    halo = refs[4:8]
    dn_ref, sums_ref, ap = refs[8:]
    g_ref = g_load()
    _, _, tall, w, c = ap.shape
    per = (tall - 2) * w
    rows = []
    totals = fill(
        ap, 1, batch, lambda b, v: v, g_ref, halo, lambda tot, v: tot + jnp.sum(v, axis=0)
    )
    totals = [jnp.sum(v, axis=0, keepdims=True) for v in totals]
    w_ref = w_load()
    for b in range(batch):
        acc = jnp.zeros((per, c), F32)
        for kh in range(3):
            for kw in range(3):
                acc = acc + lax.dot_general(
                    tap_rows(ap, b, 2 - kh, 2 - kw),
                    w_ref[kh * 3 + kw],
                    (((1,), (1,)), ((), ())),
                    preferred_element_type=F32,
                )
        dn_ref[b * per : (b + 1) * per, :] = acc
    aff = aff_ref[...]
    x_ref = x_load()
    for b in range(batch):
        a, s, r, o = (aff[k * batch + b : k * batch + b + 1] for k in range(4))

        def body(i, carry, b=b, a=a, s=s, r=r, o=o):
            rows_here = pl.ds(pl.multiple_of(b * per + i * 64, 16), 64)
            x = x_ref[rows_here, :].astype(F32)
            normed = x * a + s
            sig = 1.0 / (1.0 + jnp.exp(-normed))
            dn = dn_ref[rows_here, :] * sig * (1.0 + normed * (1.0 - sig))
            dn_ref[rows_here, :] = dn
            xhat = x * r + o
            return (
                carry[0] + jnp.sum(dn.reshape(8, 8, c), axis=0),
                carry[1] + jnp.sum((dn * xhat).reshape(8, 8, c), axis=0),
            )

        zero = jnp.zeros((8, c), F32)
        rows.append(lax.fori_loop(0, per // 64, body, (zero, zero)))
    sums_ref[...] = stack_rows(
        [jnp.sum(v[0], axis=0, keepdims=True) for v in rows]
        + [jnp.sum(v[1], axis=0, keepdims=True) for v in rows]
        + totals,
        c,
    )


def conv_kernel(batch, *refs):
    x_load, w_load, cb_load, aff_ref = refs[:4]
    halo = refs[4:8]
    temb_ref, out_ref, done_ref, ap = refs[8:]
    x_ref = x_load()
    done_ref[...] = jnp.zeros_like(done_ref)
    _, _, tall, w, c = ap.shape
    per = (tall - 2) * w
    fill_acts(ap, aff_ref[...], batch, x_ref, halo)
    w_ref = w_load()
    bias = cb_load()[...].reshape(1, c)
    for b in range(batch):
        acc = jnp.zeros((per, c), F32)
        for kh in range(3):
            for kw in range(3):
                acc = acc + jnp.dot(
                    tap_rows(ap, b, kh, kw), w_ref[kh * 3 + kw], preferred_element_type=F32
                )
        here = slice(b * per, (b + 1) * per)
        out = x_ref[here, :].astype(F32) + acc + bias + temb_ref[b : b + 1, :]
        out_ref[here, :] = out.astype(BF16)


def input_kernel(batch, count, scale, *refs):
    x_load, g_load, dn_load, gain_load, aff_ref, part_ref, other_ref, emb_ref = refs[:8]
    out_ref, gain_out, bias_out, cb_out, tw_out, done_ref = refs[8:]
    done_ref[...] = jnp.zeros_like(done_ref)
    gain_ref = gain_load()
    n, c = out_ref.shape
    per = n // batch
    red = part_ref[...] + other_ref[...]
    aff = aff_ref[...]
    gain = gain_ref[...].reshape(1, c)
    m = group_sums(red * gain) / count
    total = lambda k: sum(red[k * batch + b : k * batch + b + 1] for b in range(batch)) * scale
    bias_out[...] = total(0).reshape(c)
    gain_out[...] = total(1).reshape(c)
    cb_out[...] = total(2).reshape(c)
    rest = red[2 * batch : 3 * batch] * scale
    parts = []
    for _ in range(3):
        parts.append(rest.astype(BF16))
        rest = rest - parts[-1].astype(F32)
    emb = emb_ref[...]
    tw_out[...] = sum(
        lax.dot_general(p, emb, (((0,), (0,)), ((), ())), preferred_element_type=F32)
        for p in reversed(parts)
    )
    x_ref, g_ref, dn_ref = x_load(), g_load(), dn_load()
    for b in range(batch):
        a, r, o = (aff[k * batch + b : k * batch + b + 1] for k in (0, 2, 3))
        m1 = r * m[b : b + 1]
        m2 = r * m[batch + b : batch + b + 1]

        def body(i, _, b=b, a=a, r=r, o=o, m1=m1, m2=m2):
            here = pl.ds(pl.multiple_of(b * per + i * 64, 16), 64)
            xhat = x_ref[here, :].astype(F32) * r + o
            out_ref[here, :] = g_ref[here, :].astype(F32) + (dn_ref[here, :] * a - m1 - xhat * m2)
            return 0

        lax.fori_loop(0, per // 64, body, 0)


def place():
    col = lax.axis_index("col")
    return col & 1, (col >> 1) & 1, col >> 2


def step_one(nz, keep_ref, got_ref, a_send, a_keep, b_send, b_keep):
    _, xb, _ = place()
    half = nz // 2
    total = lambda r, p: keep_ref[r, p] + got_ref[r, p].astype(F32)
    for x in range(2):
        for z in range(half):
            p = x * nz + z
            a_send[x, z] = total(1, p).astype(BF16)
            a_keep[x, z] = total(0, p)
    for r in range(2):
        for z in range(half):
            b_send[r, z] = total(r, (1 - xb) * nz + half + z).astype(BF16)
            b_keep[r, z] = total(r, xb * nz + half + z)


def step_two(nz, a_got, a_keep, b_got, b_keep, s, s_got, a_send, a_next, b_send, b_next, s_next):
    _, xb, _ = place()
    s_next[...] = s[...] + s_got[...]
    for z in range(nz // 2):
        a_send[z] = (a_keep[1 - xb, z] + a_got[1 - xb, z].astype(F32)).astype(BF16)
        a_next[z] = a_keep[xb, z] + a_got[xb, z].astype(F32)
        b_send[z] = (b_keep[1, z] + b_got[1, z].astype(F32)).astype(BF16)
        b_next[z] = b_keep[0, z] + b_got[0, z].astype(F32)


def step_three(nz, a_got, a_keep, b_got, b_keep, s, s_got, own_ref, s_next, *refs):
    s_next[...] = s[...] + s_got[...]
    sends, held = refs[: nz - 1], refs[nz - 1]
    _, _, zb = place()
    half = nz // 2
    for z in range(half):
        held[z] = a_keep[z] + a_got[z].astype(F32)
        held[half + z] = b_keep[z] + b_got[z].astype(F32)
    own_ref[...] = held[zb]
    for k in range(1, nz):
        sends[k - 1][...] = held[zb ^ k].astype(BF16)


def step_four(nz, own_ref, s, *refs):
    total, sums = own_ref[...], s[...]
    for k in range(nz - 1):
        total = total + refs[k][...].astype(F32)
        sums = sums + refs[nz - 1 + k][...]
    refs[-2][...] = total.astype(BF16)
    refs[-1][...] = sums


def step_five(nz, *refs):
    out = refs[-1]
    width = refs[0].shape[-1]
    _, xb, zb = place()
    for k, ref in enumerate(refs[:-1]):
        p = (xb ^ (k % 2)) * nz + (zb ^ (k // 2))
        out[:, pl.ds(pl.multiple_of(p * width, LANES), width)] = ref[...]


def step_six(mine_ref, other_ref, out_ref, full):
    core, _, _ = place()
    share = mine_ref.shape[0]
    c = out_ref.shape[-1]
    full[pl.ds(pl.multiple_of(core * share, 16), share), :] = mine_ref[...].astype(F32)
    full[pl.ds(pl.multiple_of((1 - core) * share, 16), share), :] = other_ref[...].astype(F32)
    for tap in range(out_ref.shape[0]):
        out_ref[tap] = full[:, tap * c : (tap + 1) * c]


def embed(timestep, embed_in, embed_out):
    half = embed_in.shape[0] // 2
    freqs = jnp.exp(-math.log(10000.0) * jnp.arange(half, dtype=F32) / half)
    angles = timestep.astype(F32)[:, None] * freqs[None, :]
    sinus = jnp.concatenate([jnp.cos(angles), jnp.sin(angles)], axis=1).astype(BF16)
    first_hidden = jax.nn.silu(jnp.dot(sinus, embed_in, preferred_element_type=F32)).astype(BF16)
    return jax.nn.silu(jnp.dot(first_hidden, embed_out, preferred_element_type=F32)).astype(BF16)


def partner(value, bit):
    size = lax.axis_size("row") * lax.axis_size("col")
    return lax.ppermute(value, AXES, [(i, i ^ bit) for i in range(size)])


def shift(value, down, right):
    rows, cols = lax.axis_size("row"), lax.axis_size("col")
    pairs = []
    for r in range(rows):
        for c in range(cols):
            to = (r + down, c + right)
            if 0 <= to[0] < rows and 0 <= to[1] < cols:
                pairs.append((r * cols + c, to[0] * cols + to[1]))
    return lax.ppermute(value, AXES, pairs)


def swap(value):
    return partner(value, lax.axis_size("col"))


def local(
    latent,
    timestep,
    group_norm_gain,
    group_norm_bias,
    conv_w,
    conv_b,
    embed_in,
    embed_out,
    time_w,
    cotangent,
):
    batch, high, wide, channels = latent.shape
    rows, cols = lax.axis_size("row"), lax.axis_size("col")
    devices = rows * cols
    n = batch * high * wide
    count = high * rows * wide * cols * (channels // NORM_GROUPS)
    scale = 1.0 / math.sqrt(batch * high * rows * wide * cols)
    x2 = latent.reshape(n, channels)
    g2 = cotangent.reshape(n, channels)
    w9 = conv_w.reshape(9, channels, channels)
    of = jax.ShapeDtypeStruct

    lanes = -(-2 * batch * NORM_GROUPS // LANES) * LANES
    column = of((2 * batch, high + 2, 1, channels), F32)
    row = lax.axis_index("row")

    def edge(at):
        lines = [lax.dynamic_slice_in_dim(v, at, 1, 1) for v in (latent, cotangent)]
        return jnp.concatenate(lines, axis=0).reshape(2 * batch * wide, channels)

    if rows == 2:
        top = swap(edge(jnp.where(row == 0, high - 1, 0)))
        low = top
    else:
        top, low = shift(edge(high - 1), 1, 0), shift(edge(0), -1, 0)
    pay, west, east = call(
        functools.partial(stats_kernel, batch, wide),
        (of((devices, 1, lanes), F32), column, column),
        (top, low),
        far=(x2, g2),
    )
    left, right = shift(east, 0, 1), shift(west, 0, -1)
    stats = lax.all_to_all(pay, AXES, 0, 0)
    halo = (left, right, top, low)

    shifted = pltpu.VMEM((3, batch, high + 2, wide, channels), F32)
    nz = cols // 4
    share = channels // (2 * rows)
    relative = rows == 2 and nz >= 2 and share % 16 == 0
    pieces = cols // 2 if relative else 1
    width = -(-9 * channels // (LANES * pieces)) * LANES
    padded = -(-channels // LANES) * LANES
    conv_flops = 2 * 9 * n * channels * channels
    if not relative:
        share = channels // 2
    keep_rows = rows if relative else 1
    aff, keep, send = call(
        functools.partial(wgrad_kernel, batch, count, scale, relative),
        (
            of((8, channels), F32),
            of((keep_rows, pieces, share, width), F32),
            of((1, keep_rows, pieces, share, width), BF16),
        ),
        (stats, *halo),
        far=(x2, g2, group_norm_gain, group_norm_bias),
        scratch=(
            shifted,
            pltpu.VMEM((padded, n), BF16),
            pltpu.VMEM((channels, n), BF16),
            pltpu.VMEM((channels, pieces * width), F32),
        ),
        flops=conv_flops,
    )

    if relative:
        half = nz // 2
        many = lambda k, dtype: of((*k, share, width), dtype)
        got = partner(send[0], 1)
        a_send, a_keep, b_send, b_keep = call(
            functools.partial(step_one, nz),
            (many((2, half), BF16), many((2, half), F32)) * 2,
            (keep, got),
        )
        a_got, b_got = partner(a_send, cols), partner(b_send, 2)
        first = (a_send, b_send)
    else:
        first = ()

    dn, sums = call(
        functools.partial(back_kernel, batch),
        (of((n, channels), F32), of((8, channels), F32)),
        (aff, *halo),
        far=(g2, w9, x2),
        after=first,
        scratch=(shifted,),
        flops=conv_flops,
    )
    emb = embed(timestep, embed_in, embed_out)
    temb = jnp.dot(emb, time_w, preferred_element_type=F32)

    if relative:
        s_shape = of(sums.shape, F32)
        a_send, a_keep, b_send, b_keep, sums = call(
            functools.partial(step_two, nz),
            (many((half,), BF16), many((half,), F32)) * 2 + (s_shape,),
            (a_got, a_keep, b_got, b_keep, sums, partner(sums, 1)),
        )
        a_got, b_got = partner(a_send, 2), partner(b_send, cols)
        own, sums, *sends = call(
            functools.partial(step_three, nz),
            (many((), F32), s_shape, *[many((), BF16)] * (nz - 1)),
            (a_got, a_keep, b_got, b_keep, sums, partner(sums, 2)),
            scratch=(pltpu.VMEM((nz, share, width), F32),),
        )
        gots = [partner(v, 4 * (k + 1)) for k, v in enumerate(sends)]
        gots += [partner(sums, 4 * k) for k in range(1, nz)]
        second = tuple(sends)
    else:
        second = ()

    token = of((8, LANES), F32)
    block_out, done = call(
        functools.partial(conv_kernel, batch),
        (of((n, channels), BF16), token),
        (aff, *halo, temb),
        far=(x2, w9, conv_b),
        after=second,
        scratch=(shifted,),
        flops=conv_flops,
    )

    if relative:
        own, sums = call(
            functools.partial(step_four, nz),
            (many((), BF16), s_shape),
            (own, sums, *gots),
            after=(done,),
        )
        others = [partner(own, 2 * k) for k in range(1, pieces)]
        third = (own,)
    else:
        bit = 1
        while 2 * bit < devices:
            sums = sums + partner(sums, bit)
            bit *= 2
        third = ()

    vector = of((channels,), F32)
    input_grad, gain_grad, bias_grad, conv_b_grad, time_grad, done = call(
        functools.partial(input_kernel, batch, count, scale),
        (of((n, channels), F32), *[vector] * 3, of((channels, emb.shape[1]), F32), token),
        (aff, sums, partner(sums, cols if relative else bit), emb),
        far=(x2, g2, dn, group_norm_gain),
        after=third,
        flops=8 * n * channels,
    )

    if relative:
        mine = call(
            functools.partial(step_five, nz),
            of((share, pieces * width), BF16),
            (own, *others),
            after=(done,),
        )
        grad = call(
            step_six,
            of((9, 2 * share, channels), F32),
            (mine, partner(mine, 1)),
            scratch=(pltpu.VMEM((2 * share, pieces * width), F32),),
        )
    else:
        both = jnp.concatenate([keep[0, 0], send[0, 0, 0].astype(F32)], axis=0)
        both = lax.psum(both[:, : 9 * channels], AXES)
        mine = channels // rows
        grad = lax.dynamic_slice_in_dim(both, lax.axis_index("row") * mine, mine, 0)
        grad = jnp.transpose(grad.reshape(mine, 9, channels), (1, 0, 2))
    conv_w_grad = jnp.transpose(grad.reshape(3, 3, channels // rows, channels), (2, 0, 1, 3))
    return (
        block_out.reshape(latent.shape),
        input_grad.reshape(latent.shape),
        conv_w_grad,
        gain_grad,
        bias_grad,
        conv_b_grad,
        time_grad.T,
    )


def solution(mesh):
    return jax.shard_map(
        local,
        mesh=mesh,
        in_specs=(
            P(None, "row", "col", None),
            P(),
            P(),
            P(),
            P(),
            P(),
            P(),
            P(),
            P(),
            P(None, "row", "col", None),
        ),
        out_specs=(
            P(None, "row", "col", None),
            P(None, "row", "col", None),
            P("row", None, None, None),
            P(),
            P(),
            P(),
            P(),
        ),
        check_vma=False,
    )
```

```python
import functools
import math

import jax
import jax.numpy as jnp
from jax import lax
from jax.experimental import pallas as pl
from jax.experimental.pallas import tpu as pltpu
from jax.sharding import PartitionSpec as P

NORM_GROUPS = 32
EPS = 1e-05
LANES = 128
F32 = jnp.float32
BF16 = jnp.bfloat16
AXES = ("row", "col")
VMEM_LIMIT = 64 * 1024 * 1024
HI = lax.Precision.HIGHEST


def iota(shape, dim):
    return lax.broadcasted_iota(jnp.int32, shape, dim)


def call(body, out_shape, operands, far=(), after=(), scratch=(), flops=0, nbytes=2_000_000):
    outs, tree = jax.tree.flatten(out_shape)
    ins = (*far, *operands)
    waits, own = len(after), len(scratch)

    def kernel(*refs):
        src, refs = refs[: len(ins)], refs[len(ins) + waits :]
        dst, refs = refs[: len(outs)], refs[len(outs) :]
        mine, refs = refs[:own], refs[own:]
        held, refs = refs[: len(ins)], refs[len(ins) :]
        made, (sem_in, sem_out) = refs[: len(outs)], refs[len(outs) :]
        copies = [pltpu.make_async_copy(a, b, sem_in.at[i]) for i, (a, b) in enumerate(zip(src, held))]
        for c in (*copies[len(far) :], *copies[: len(far)]):
            c.start()

        def loader(i):
            def load():
                copies[i].wait()
                return held[i]

            return load

        for c in copies[len(far) :]:
            c.wait()
        body(*[loader(i) for i in range(len(far))], *held[len(far) :], *made, *mine)
        copies = [pltpu.make_async_copy(a, b, sem_out.at[i]) for i, (a, b) in enumerate(zip(made, dst))]
        for c in copies:
            c.start()
        for c in copies:
            c.wait()

    hbm = pl.BlockSpec(memory_space=pltpu.HBM)
    results = pl.pallas_call(
        kernel,
        out_shape=tuple(outs),
        in_specs=[hbm] * len(ins) + [pl.BlockSpec(memory_space=pl.ANY)] * waits,
        out_specs=(hbm,) * len(outs),
        scratch_shapes=[
            *scratch,
            *[pltpu.VMEM(v.shape, v.dtype) for v in ins],
            *[pltpu.VMEM(v.shape, v.dtype) for v in outs],
            pltpu.SemaphoreType.DMA((max(len(ins), 1),)),
            pltpu.SemaphoreType.DMA((len(outs),)),
        ],
        compiler_params=pltpu.CompilerParams(vmem_limit_bytes=VMEM_LIMIT),
        cost_estimate=pl.CostEstimate(flops=flops, bytes_accessed=nbytes, transcendentals=0),
    )(*ins, *after)
    return jax.tree.unflatten(tree, results)


def group_matrix(channels, lanes):
    size = channels // NORM_GROUPS
    group = iota((channels, lanes), 1) & (NORM_GROUPS - 1)
    channel = iota((channels, lanes), 0)
    return jnp.where((channel >= group * size) & (channel < (group + 1) * size), 1.0, 0.0).astype(F32)


def group_sums(rows):
    lanes = LANES
    g = group_matrix(rows.shape[1], lanes)
    keep = iota((8, lanes), 1) < NORM_GROUPS
    s = jnp.dot(rows, g, precision=HI, preferred_element_type=F32)
    s = jnp.where(keep, s, 0.0)
    return lax.dot_general(
        s, g, (((1,), (1,)), ((), ())), precision=HI, preferred_element_type=F32
    )


def stack_rows(rows, channels):
    r = iota((8, channels), 0)
    out = jnp.zeros((8, channels), F32)
    for k, v in enumerate(rows):
        out = out + jnp.where(r == k, v, 0.0)
    return out


def stats_kernel(batch, w, x_load, g_load, top_ref, low_ref, pay_ref, west_ref, east_ref):
    sums = []
    step = 64
    t = step // w
    top, low = top_ref[...].astype(F32), low_ref[...].astype(F32)
    for k, load in enumerate((x_load, g_load)):
        ref = load()
        n, channels = ref.shape
        per = n // batch
        high = per // w
        for b in range(batch):
            at = k * batch + b

            def add(i, c, b=b, k=k, ref=ref, at=at):
                start = pl.multiple_of(b * per + i * step, 16)
                v = ref[pl.ds(start, step), :].astype(F32).reshape(t, w, channels)
                west_ref[at, pl.ds(i * t + 1, t)] = v[:, :1]
                east_ref[at, pl.ds(i * t + 1, t)] = v[:, w - 1 :]
                if k:
                    return c
                return c[0] + jnp.sum(v, axis=0), c[1] + jnp.sum(v * v, axis=0)

            zero = jnp.zeros((w, channels), F32)
            s, q = lax.fori_loop(0, per // step, add, (zero, zero))
            if not k:
                sums.append((jnp.sum(s, axis=0, keepdims=True), jnp.sum(q, axis=0, keepdims=True)))
            for v, h in ((top, 0), (low, high + 1)):
                west_ref[at, h] = v[at * w : at * w + 1]
                east_ref[at, h] = v[(at + 1) * w - 1 : (at + 1) * w]
    stacked = stack_rows([r[0] for r in sums] + [r[1] for r in sums], channels)
    lanes = pay_ref.shape[-1]
    res = jnp.dot(
        stacked, group_matrix(channels, lanes), precision=HI, preferred_element_type=F32
    )
    first = iota((8, lanes), 0) * NORM_GROUPS
    lane = iota((8, lanes), 1)
    mine = (lane >= first) & (lane < first + NORM_GROUPS)
    row = jnp.sum(jnp.where(mine, res, 0.0), axis=0, keepdims=True)
    pay_ref[...] = jnp.broadcast_to(row[None], pay_ref.shape)


def affine_rows(st_ref, gain_ref, bias_ref, batch, count):
    channels = gain_ref.shape[-1]
    lanes = st_ref.shape[-1]
    total = jnp.sum(st_ref[...], axis=0)
    first = iota((8, lanes), 0) * NORM_GROUPS
    lane = iota((8, lanes), 1)
    mine = (lane >= first) & (lane < first + NORM_GROUPS)
    spread = jnp.where(mine, total, 0.0)
    sums = lax.dot_general(
        spread,
        group_matrix(channels, lanes),
        (((1,), (1,)), ((), ())),
        precision=HI,
        preferred_element_type=F32,
    )
    gain, bias = gain_ref[...].reshape(1, channels), bias_ref[...].reshape(1, channels)
    a, s, r, t = [], [], [], []
    for b in range(batch):
        mean = sums[b : b + 1] / count
        var = sums[batch + b : batch + b + 1] / count - mean * mean
        inv = lax.rsqrt(var + EPS)
        r.append(inv)
        t.append(-mean * inv)
        a.append(inv * gain)
        s.append(bias - mean * inv * gain)
    return stack_rows(a + s + r + t, channels)


def put_shifted(ap, b, h, v, left, right):
    t, w, c = v.shape
    j = iota((t, w, c), 1)
    ap[0, b, pl.ds(h, t)] = jnp.where(j == 0, left, pltpu.roll(v, 1, 1))
    ap[1, b, pl.ds(h, t)] = v
    ap[2, b, pl.ds(h, t)] = jnp.where(j == w - 1, right, pltpu.roll(v, w - 1, 1))


def edge_masks():
    ri, rn = lax.axis_index("row"), lax.axis_size("row")
    ci, cn = lax.axis_index("col"), lax.axis_size("col")
    flags = (ri == 0, ri == rn - 1, ci == 0, ci == cn - 1)
    return tuple(jnp.where(f, 0.0, 1.0) for f in flags)


def fill(ap, part, batch, fn, src_ref, halo, visit=None):
    _, _, tall, w, c = ap.shape
    high = tall - 2
    up, down, west, east = edge_masks()
    left, right, top, low = halo
    top, low = top[...].astype(F32), low[...].astype(F32)
    t = 8
    first = part * batch
    for b in range(batch):

        def body(i, carry, b=b):
            start = pl.multiple_of(b * high * w + i * t * w, 16)
            v = src_ref[pl.ds(start, t * w), :].astype(F32).reshape(t, w, c)
            h = i * t
            put_shifted(
                ap,
                b,
                h + 1,
                fn(b, v),
                fn(b, left[first + b, pl.ds(h + 1, t)]) * west,
                fn(b, right[first + b, pl.ds(h + 1, t)]) * east,
            )
            return carry if visit is None else visit(carry, v)

        out = lax.fori_loop(0, high // t, body, jnp.zeros((w, c), F32))
        if visit is not None:
            yield out
        for line, h, edge in ((top, 0, up), (low, tall - 1, down)):
            at = first + b
            put_shifted(
                ap,
                b,
                h,
                fn(b, line[at * w : (at + 1) * w].reshape(1, w, c)) * edge,
                fn(b, left[at, h : h + 1]) * (west * edge),
                fn(b, right[at, h : h + 1]) * (east * edge),
            )


def fill_acts(ap, aff, batch, x_ref, halo):
    c = ap.shape[-1]

    def act(b, x):
        v = x * aff[b : b + 1].reshape(1, 1, c) + aff[batch + b : batch + b + 1].reshape(1, 1, c)
        return v / (1.0 + jnp.exp(-v))

    for _ in fill(ap, 0, batch, act, x_ref, halo):
        pass


def tap_rows(ap, b, kh, kw):
    _, _, tall, w, c = ap.shape
    return ap[kw, b, kh : kh + tall - 2].reshape((tall - 2) * w, c).astype(BF16)


def dacts_kernel(batch, relative, share, *refs):
    g_load, w_load = refs[:2]
    halo = refs[2:6]
    da_ref, gsum_ref, gp_ref, ap, gt = refs[6:]
    g_ref = g_load()
    n, c = g_ref.shape
    _, _, tall, w, _ = ap.shape
    per = (tall - 2) * w
    totals = fill(
        ap, 1, batch, lambda b, v: v, g_ref, halo, lambda tot, v: tot + jnp.sum(v, axis=0)
    )
    totals = [jnp.sum(v, axis=0, keepdims=True) for v in totals]
    gsum_ref[...] = stack_rows([jnp.zeros((1, c), F32)] * (2 * batch) + totals, c)
    w_ref = w_load()
    for b in range(batch):
        acc = jnp.zeros((per, c), F32)
        for kh in range(3):
            for kw in range(3):
                acc = acc + lax.dot_general(
                    tap_rows(ap, b, 2 - kh, 2 - kw),
                    w_ref[kh * 3 + kw],
                    (((1,), (1,)), ((), ())),
                    preferred_element_type=F32,
                )
        da_ref[b * per : (b + 1) * per, :] = acc
    wide = gt.shape[0]
    step = LANES
    for i in range(n // step):
        v = g_ref[i * step : (i + 1) * step, :].astype(F32)
        v = jnp.concatenate([v, jnp.zeros((step, wide - c), F32)], axis=1)
        gt[:, i * step : (i + 1) * step] = jnp.transpose(v).astype(BF16)
    if relative:
        me = lax.axis_index("row") * 2 + (lax.axis_index("col") & 1)
        for q in range(4):
            other = (me ^ ((q % 2) * 2 + q // 2)) * share
            gp_ref[q * share : (q + 1) * share, :] = gt[pl.ds(pl.multiple_of(other, 16), share), :]
    else:
        gp_ref[...] = gt[:c, :]


def wgrad_kernel(batch, count, scale, *refs):
    x_load, gp_load, gain_ref, bias_ref, st_ref = refs[:5]
    halo = refs[5:9]
    aff_ref, keep_ref, send_ref = refs[9:12]
    ap, part = refs[12:]
    aff = affine_rows(st_ref, gain_ref, bias_ref, batch, count)
    aff_ref[...] = aff
    x_ref = x_load()
    n, channels = x_ref.shape
    _, rows, pieces, share, width = send_ref.shape
    fill_acts(ap, aff, batch, x_ref, halo)
    part[:, 9 * channels :] = jnp.zeros((channels, part.shape[1] - 9 * channels), F32)
    per = n // batch
    gp = gp_load()
    for kh in range(3):
        for kw in range(3):
            tap = kh * 3 + kw
            acc = jnp.zeros((channels, channels), F32)
            for b in range(batch):
                acc = acc + jnp.dot(
                    gp[:, b * per : (b + 1) * per],
                    tap_rows(ap, b, kh, kw),
                    preferred_element_type=F32,
                )
            part[:, tap * channels : (tap + 1) * channels] = acc * scale
    for r in range(rows):
        for p in range(pieces):
            lane = slice(p * width, (p + 1) * width)
            keep_ref[r, p] = part[r * share : (r + 1) * share, lane]
            low = (rows + r) * share
            send_ref[0, r, p] = part[low : low + share, lane].astype(BF16)


def back_kernel(batch, *refs):
    x_load, da_load, aff_ref, gsum_ref, dn_ref, sums_ref = refs
    n, c = dn_ref.shape
    per = n // batch
    rows = []
    aff = aff_ref[...]
    x_ref, da_ref = x_load(), da_load()
    for b in range(batch):
        a, s, r, o = (aff[k * batch + b : k * batch + b + 1] for k in range(4))

        def body(i, carry, b=b, a=a, s=s, r=r, o=o):
            rows_here = pl.ds(pl.multiple_of(b * per + i * 64, 16), 64)
            x = x_ref[rows_here, :].astype(F32)
            normed = x * a + s
            sig = 1.0 / (1.0 + jnp.exp(-normed))
            dn = da_ref[rows_here, :] * sig * (1.0 + normed * (1.0 - sig))
            dn_ref[rows_here, :] = dn
            xhat = x * r + o
            return (
                carry[0] + jnp.sum(dn.reshape(8, 8, c), axis=0),
                carry[1] + jnp.sum((dn * xhat).reshape(8, 8, c), axis=0),
            )

        zero = jnp.zeros((8, c), F32)
        rows.append(lax.fori_loop(0, per // 64, body, (zero, zero)))
    sums_ref[...] = gsum_ref[...] + stack_rows(
        [jnp.sum(v[0], axis=0, keepdims=True) for v in rows]
        + [jnp.sum(v[1], axis=0, keepdims=True) for v in rows],
        c,
    )


def conv_kernel(batch, *refs):
    x_load, w_load, cb_load, aff_ref = refs[:4]
    halo = refs[4:8]
    temb_ref, out_ref, done_ref, ap = refs[8:]
    x_ref = x_load()
    done_ref[...] = jnp.zeros_like(done_ref)
    _, _, tall, w, c = ap.shape
    per = (tall - 2) * w
    fill_acts(ap, aff_ref[...], batch, x_ref, halo)
    w_ref = w_load()
    bias = cb_load()[...].reshape(1, c)
    for b in range(batch):
        acc = jnp.zeros((per, c), F32)
        for kh in range(3):
            for kw in range(3):
                acc = acc + jnp.dot(
                    tap_rows(ap, b, kh, kw), w_ref[kh * 3 + kw], preferred_element_type=F32
                )
        here = slice(b * per, (b + 1) * per)
        out = x_ref[here, :].astype(F32) + acc + bias + temb_ref[b : b + 1, :]
        out_ref[here, :] = out.astype(BF16)


def input_kernel(batch, count, scale, *refs):
    x_load, g_load, dn_load, gain_load, aff_ref, part_ref, other_ref, emb_ref = refs[:8]
    out_ref, gain_out, bias_out, cb_out, tw_out, done_ref = refs[8:]
    done_ref[...] = jnp.zeros_like(done_ref)
    gain_ref = gain_load()
    n, c = out_ref.shape
    per = n // batch
    red = part_ref[...] + other_ref[...]
    aff = aff_ref[...]
    gain = gain_ref[...].reshape(1, c)
    m = group_sums(red * gain) / count
    total = lambda k: sum(red[k * batch + b : k * batch + b + 1] for b in range(batch)) * scale
    bias_out[...] = total(0).reshape(c)
    gain_out[...] = total(1).reshape(c)
    cb_out[...] = total(2).reshape(c)
    rest = red[2 * batch : 3 * batch] * scale
    parts = []
    for _ in range(3):
        parts.append(rest.astype(BF16))
        rest = rest - parts[-1].astype(F32)
    emb = emb_ref[...]
    tw_out[...] = sum(
        lax.dot_general(p, emb, (((0,), (0,)), ((), ())), preferred_element_type=F32)
        for p in reversed(parts)
    )
    x_ref, g_ref, dn_ref = x_load(), g_load(), dn_load()
    for b in range(batch):
        a, r, o = (aff[k * batch + b : k * batch + b + 1] for k in (0, 2, 3))
        m1 = r * m[b : b + 1]
        m2 = r * m[batch + b : batch + b + 1]

        def body(i, _, b=b, a=a, r=r, o=o, m1=m1, m2=m2):
            here = pl.ds(pl.multiple_of(b * per + i * 64, 16), 64)
            xhat = x_ref[here, :].astype(F32) * r + o
            out_ref[here, :] = g_ref[here, :].astype(F32) + (dn_ref[here, :] * a - m1 - xhat * m2)
            return 0

        lax.fori_loop(0, per // 64, body, 0)


def place():
    col = lax.axis_index("col")
    return col & 1, (col >> 1) & 1, col >> 2


def step_one(nz, keep_ref, got_ref, a_send, a_keep, b_send, b_keep):
    _, xb, _ = place()
    half = nz // 2
    total = lambda r, p: keep_ref[r, p] + got_ref[r, p].astype(F32)
    for x in range(2):
        for z in range(half):
            p = x * nz + z
            a_send[x, z] = total(1, p).astype(BF16)
            a_keep[x, z] = total(0, p)
    for r in range(2):
        for z in range(half):
            b_send[r, z] = total(r, (1 - xb) * nz + half + z).astype(BF16)
            b_keep[r, z] = total(r, xb * nz + half + z)


def step_two(nz, a_got, a_keep, b_got, b_keep, s, s_got, a_send, a_next, b_send, b_next, s_next):
    _, xb, _ = place()
    s_next[...] = s[...] + s_got[...]
    for z in range(nz // 2):
        a_send[z] = (a_keep[1 - xb, z] + a_got[1 - xb, z].astype(F32)).astype(BF16)
        a_next[z] = a_keep[xb, z] + a_got[xb, z].astype(F32)
        b_send[z] = (b_keep[1, z] + b_got[1, z].astype(F32)).astype(BF16)
        b_next[z] = b_keep[0, z] + b_got[0, z].astype(F32)


def step_three(nz, a_got, a_keep, b_got, b_keep, s, s_got, own_ref, s_next, *refs):
    s_next[...] = s[...] + s_got[...]
    sends, held = refs[: nz - 1], refs[nz - 1]
    _, _, zb = place()
    half = nz // 2
    for z in range(half):
        held[z] = a_keep[z] + a_got[z].astype(F32)
        held[half + z] = b_keep[z] + b_got[z].astype(F32)
    own_ref[...] = held[zb]
    for k in range(1, nz):
        sends[k - 1][...] = held[zb ^ k].astype(BF16)


def step_four(nz, own_ref, s, *refs):
    total, sums = own_ref[...], s[...]
    for k in range(nz - 1):
        total = total + refs[k][...].astype(F32)
        sums = sums + refs[nz - 1 + k][...]
    refs[-2][...] = total.astype(BF16)
    refs[-1][...] = sums


def step_five(nz, *refs):
    out = refs[-1]
    width = refs[0].shape[-1]
    _, xb, zb = place()
    for k, ref in enumerate(refs[:-1]):
        p = (xb ^ (k % 2)) * nz + (zb ^ (k // 2))
        out[:, pl.ds(pl.multiple_of(p * width, LANES), width)] = ref[...]


def step_six(mine_ref, other_ref, out_ref, full):
    core, _, _ = place()
    share = mine_ref.shape[0]
    c = out_ref.shape[-1]
    full[pl.ds(pl.multiple_of(core * share, 16), share), :] = mine_ref[...].astype(F32)
    full[pl.ds(pl.multiple_of((1 - core) * share, 16), share), :] = other_ref[...].astype(F32)
    for tap in range(out_ref.shape[0]):
        out_ref[tap] = full[:, tap * c : (tap + 1) * c]


def embed(timestep, embed_in, embed_out):
    half = embed_in.shape[0] // 2
    freqs = jnp.exp(-math.log(10000.0) * jnp.arange(half, dtype=F32) / half)
    angles = timestep.astype(F32)[:, None] * freqs[None, :]
    sinus = jnp.concatenate([jnp.cos(angles), jnp.sin(angles)], axis=1).astype(BF16)
    first_hidden = jax.nn.silu(jnp.dot(sinus, embed_in, preferred_element_type=F32)).astype(BF16)
    return jax.nn.silu(jnp.dot(first_hidden, embed_out, preferred_element_type=F32)).astype(BF16)


def partner(value, bit):
    size = lax.axis_size("row") * lax.axis_size("col")
    return lax.ppermute(value, AXES, [(i, i ^ bit) for i in range(size)])


def shift(value, down, right):
    rows, cols = lax.axis_size("row"), lax.axis_size("col")
    pairs = []
    for r in range(rows):
        for c in range(cols):
            to = (r + down, c + right)
            if 0 <= to[0] < rows and 0 <= to[1] < cols:
                pairs.append((r * cols + c, to[0] * cols + to[1]))
    return lax.ppermute(value, AXES, pairs)


def swap(value):
    return partner(value, lax.axis_size("col"))


def local(
    latent,
    timestep,
    group_norm_gain,
    group_norm_bias,
    conv_w,
    conv_b,
    embed_in,
    embed_out,
    time_w,
    cotangent,
):
    batch, high, wide, channels = latent.shape
    rows, cols = lax.axis_size("row"), lax.axis_size("col")
    devices = rows * cols
    n = batch * high * wide
    count = high * rows * wide * cols * (channels // NORM_GROUPS)
    scale = 1.0 / math.sqrt(batch * high * rows * wide * cols)
    x2 = latent.reshape(n, channels)
    g2 = cotangent.reshape(n, channels)
    w9 = conv_w.reshape(9, channels, channels)
    of = jax.ShapeDtypeStruct

    lanes = -(-2 * batch * NORM_GROUPS // LANES) * LANES
    column = of((2 * batch, high + 2, 1, channels), F32)
    row = lax.axis_index("row")

    def edge(at):
        lines = [lax.dynamic_slice_in_dim(v, at, 1, 1) for v in (latent, cotangent)]
        return jnp.concatenate(lines, axis=0).reshape(2 * batch * wide, channels)

    if rows == 2:
        top = swap(edge(jnp.where(row == 0, high - 1, 0)))
        low = top
    else:
        top, low = shift(edge(high - 1), 1, 0), shift(edge(0), -1, 0)
    pay, west, east = call(
        functools.partial(stats_kernel, batch, wide),
        (of((devices, 1, lanes), F32), column, column),
        (top, low),
        far=(x2, g2),
    )
    left, right = shift(east, 0, 1), shift(west, 0, -1)
    stats = lax.all_to_all(pay, AXES, 0, 0)
    halo = (left, right, top, low)

    shifted = pltpu.VMEM((3, batch, high + 2, wide, channels), F32)
    nz = cols // 4
    share = channels // (2 * rows)
    relative = rows == 2 and nz >= 2 and share % 16 == 0
    pieces = cols // 2 if relative else 1
    width = -(-9 * channels // (LANES * pieces)) * LANES
    padded = -(-channels // LANES) * LANES
    conv_flops = 2 * 9 * n * channels * channels
    if not relative:
        share = channels // 2
    keep_rows = rows if relative else 1
    dacts, gsum, flipped = call(
        functools.partial(dacts_kernel, batch, relative, share),
        (of((n, channels), F32), of((8, channels), F32), of((channels, n), BF16)),
        halo,
        far=(g2, w9),
        scratch=(shifted, pltpu.VMEM((padded, n), BF16)),
        flops=conv_flops,
    )
    aff, keep, send = call(
        functools.partial(wgrad_kernel, batch, count, scale),
        (
            of((8, channels), F32),
            of((keep_rows, pieces, share, width), F32),
            of((1, keep_rows, pieces, share, width), BF16),
        ),
        (group_norm_gain, group_norm_bias, stats, *halo),
        far=(x2, flipped),
        scratch=(shifted, pltpu.VMEM((channels, pieces * width), F32)),
        flops=conv_flops,
    )

    if relative:
        half = nz // 2
        many = lambda k, dtype: of((*k, share, width), dtype)
        got = partner(send[0], 1)
        a_send, a_keep, b_send, b_keep = call(
            functools.partial(step_one, nz),
            (many((2, half), BF16), many((2, half), F32)) * 2,
            (keep, got),
        )
        a_got, b_got = partner(a_send, cols), partner(b_send, 2)
        first = (a_send, b_send)
    else:
        first = ()

    dn, sums = call(
        functools.partial(back_kernel, batch),
        (of((n, channels), F32), of((8, channels), F32)),
        (aff, gsum),
        far=(x2, dacts),
        after=first,
        flops=20 * n * channels,
    )
    emb = embed(timestep, embed_in, embed_out)
    temb = jnp.dot(emb, time_w, preferred_element_type=F32)

    if relative:
        s_shape = of(sums.shape, F32)
        a_send, a_keep, b_send, b_keep, sums = call(
            functools.partial(step_two, nz),
            (many((half,), BF16), many((half,), F32)) * 2 + (s_shape,),
            (a_got, a_keep, b_got, b_keep, sums, partner(sums, 1)),
        )
        a_got, b_got = partner(a_send, 2), partner(b_send, cols)
        own, sums, *sends = call(
            functools.partial(step_three, nz),
            (many((), F32), s_shape, *[many((), BF16)] * (nz - 1)),
            (a_got, a_keep, b_got, b_keep, sums, partner(sums, 2)),
            scratch=(pltpu.VMEM((nz, share, width), F32),),
        )
        gots = [partner(v, 4 * (k + 1)) for k, v in enumerate(sends)]
        gots += [partner(sums, 4 * k) for k in range(1, nz)]
        second = tuple(sends)
    else:
        second = ()

    token = of((8, LANES), F32)
    block_out, done = call(
        functools.partial(conv_kernel, batch),
        (of((n, channels), BF16), token),
        (aff, *halo, temb),
        far=(x2, w9, conv_b),
        after=second,
        scratch=(shifted,),
        flops=conv_flops,
    )

    if relative:
        own, sums = call(
            functools.partial(step_four, nz),
            (many((), BF16), s_shape),
            (own, sums, *gots),
            after=(done,),
        )
        others = [partner(own, 2 * k) for k in range(1, pieces)]
        third = (own,)
    else:
        bit = 1
        while 2 * bit < devices:
            sums = sums + partner(sums, bit)
            bit *= 2
        third = ()

    vector = of((channels,), F32)
    input_grad, gain_grad, bias_grad, conv_b_grad, time_grad, done = call(
        functools.partial(input_kernel, batch, count, scale),
        (of((n, channels), F32), *[vector] * 3, of((channels, emb.shape[1]), F32), token),
        (aff, sums, partner(sums, cols if relative else bit), emb),
        far=(x2, g2, dn, group_norm_gain),
        after=third,
        flops=8 * n * channels,
    )

    if relative:
        mine = call(
            functools.partial(step_five, nz),
            of((share, pieces * width), BF16),
            (own, *others),
            after=(done,),
        )
        grad = call(
            step_six,
            of((9, 2 * share, channels), F32),
            (mine, partner(mine, 1)),
            scratch=(pltpu.VMEM((2 * share, pieces * width), F32),),
        )
    else:
        both = jnp.concatenate([keep[0, 0], send[0, 0, 0].astype(F32)], axis=0)
        both = lax.psum(both[:, : 9 * channels], AXES)
        mine = channels // rows
        grad = lax.dynamic_slice_in_dim(both, lax.axis_index("row") * mine, mine, 0)
        grad = jnp.transpose(grad.reshape(mine, 9, channels), (1, 0, 2))
    conv_w_grad = jnp.transpose(grad.reshape(3, 3, channels // rows, channels), (2, 0, 1, 3))
    return (
        block_out.reshape(latent.shape),
        input_grad.reshape(latent.shape),
        conv_w_grad,
        gain_grad,
        bias_grad,
        conv_b_grad,
        time_grad.T,
    )


def solution(mesh):
    return jax.shard_map(
        local,
        mesh=mesh,
        in_specs=(
            P(None, "row", "col", None),
            P(),
            P(),
            P(),
            P(),
            P(),
            P(),
            P(),
            P(),
            P(None, "row", "col", None),
        ),
        out_specs=(
            P(None, "row", "col", None),
            P(None, "row", "col", None),
            P("row", None, None, None),
            P(),
            P(),
            P(),
            P(),
        ),
        check_vma=False,
    )
```

```python
import functools
import math

import jax
import jax.numpy as jnp
from jax import lax
from jax.experimental import pallas as pl
from jax.experimental.pallas import tpu as pltpu
from jax.sharding import PartitionSpec as P

NORM_GROUPS = 32
EPS = 1e-05
LANES = 128
F32 = jnp.float32
BF16 = jnp.bfloat16
AXES = ("row", "col")
HI = lax.Precision.HIGHEST


def iota(shape, dim):
    return lax.broadcasted_iota(jnp.int32, shape, dim)


def call(body, out_shape, operands, far=(), after=(), scratch=(), vmem=20, flops=0):
    count, used, waits = len(far), len(operands), len(after)

    def kernel(*refs):
        ins = refs[:count]
        rest = refs[count : count + used] + refs[count + used + waits :]
        if not count:
            return body(*rest)
        holds, sems = rest[-1 - count : -1], rest[-1]
        copies = [
            pltpu.make_async_copy(ins[i], holds[i], sems.at[i]) for i in range(count)
        ]
        for c in copies:
            c.start()

        def loader(i):
            def load():
                copies[i].wait()
                return holds[i]

            return load

        body(*[loader(i) for i in range(count)], *rest[: -1 - count])

    near = pl.BlockSpec(memory_space=pltpu.VMEM)
    scratch = list(scratch)
    if count:
        scratch += [pltpu.VMEM(v.shape, v.dtype) for v in far]
        scratch.append(pltpu.SemaphoreType.DMA((count,)))
    return pl.pallas_call(
        kernel,
        out_shape=out_shape,
        in_specs=[pl.BlockSpec(memory_space=pltpu.HBM)] * count
        + [near] * used
        + [near] * waits,
        out_specs=jax.tree.map(lambda _: near, out_shape),
        scratch_shapes=scratch,
        compiler_params=pltpu.CompilerParams(vmem_limit_bytes=vmem * 2**20),
        cost_estimate=pl.CostEstimate(flops=flops, bytes_accessed=2_000_000, transcendentals=0),
    )(*far, *operands, *after)


def group_matrix(channels, lanes):
    size = channels // NORM_GROUPS
    group = iota((channels, lanes), 1) & (NORM_GROUPS - 1)
    channel = iota((channels, lanes), 0)
    return jnp.where((channel >= group * size) & (channel < (group + 1) * size), 1.0, 0.0).astype(F32)


def group_sums(rows):
    lanes = LANES
    g = group_matrix(rows.shape[1], lanes)
    keep = iota((8, lanes), 1) < NORM_GROUPS
    s = jnp.dot(rows, g, precision=HI, preferred_element_type=F32)
    s = jnp.where(keep, s, 0.0)
    return lax.dot_general(
        s, g, (((1,), (1,)), ((), ())), precision=HI, preferred_element_type=F32
    )


def stack_rows(rows, channels):
    r = iota((8, channels), 0)
    out = jnp.zeros((8, channels), F32)
    for k, v in enumerate(rows):
        out = out + jnp.where(r == k, v, 0.0)
    return out


def stats_kernel(batch, w, x_load, g_load, top_ref, low_ref, pay_ref, west_ref, east_ref):
    sums = []
    step = 64
    t = step // w
    top, low = top_ref[...].astype(F32), low_ref[...].astype(F32)
    for k, load in enumerate((x_load, g_load)):
        ref = load()
        n, channels = ref.shape
        per = n // batch
        high = per // w
        for b in range(batch):
            at = k * batch + b

            def add(i, c, b=b, k=k, ref=ref, at=at):
                start = pl.multiple_of(b * per + i * step, 16)
                v = ref[pl.ds(start, step), :].astype(F32).reshape(t, w, channels)
                west_ref[at, pl.ds(i * t + 1, t)] = v[:, :1]
                east_ref[at, pl.ds(i * t + 1, t)] = v[:, w - 1 :]
                if k:
                    return c
                return c[0] + jnp.sum(v, axis=0), c[1] + jnp.sum(v * v, axis=0)

            zero = jnp.zeros((w, channels), F32)
            s, q = lax.fori_loop(0, per // step, add, (zero, zero))
            if not k:
                sums.append((jnp.sum(s, axis=0, keepdims=True), jnp.sum(q, axis=0, keepdims=True)))
            for v, h in ((top, 0), (low, high + 1)):
                west_ref[at, h] = v[at * w : at * w + 1]
                east_ref[at, h] = v[(at + 1) * w - 1 : (at + 1) * w]
    stacked = stack_rows([r[0] for r in sums] + [r[1] for r in sums], channels)
    lanes = pay_ref.shape[-1]
    res = jnp.dot(
        stacked, group_matrix(channels, lanes), precision=HI, preferred_element_type=F32
    )
    first = iota((8, lanes), 0) * NORM_GROUPS
    lane = iota((8, lanes), 1)
    mine = (lane >= first) & (lane < first + NORM_GROUPS)
    row = jnp.sum(jnp.where(mine, res, 0.0), axis=0, keepdims=True)
    pay_ref[...] = jnp.broadcast_to(row[None], pay_ref.shape)


def affine_rows(st_ref, gain_ref, bias_ref, batch, count):
    channels = gain_ref.shape[-1]
    lanes = st_ref.shape[-1]
    total = jnp.sum(st_ref[...], axis=0)
    first = iota((8, lanes), 0) * NORM_GROUPS
    lane = iota((8, lanes), 1)
    mine = (lane >= first) & (lane < first + NORM_GROUPS)
    spread = jnp.where(mine, total, 0.0)
    sums = lax.dot_general(
        spread,
        group_matrix(channels, lanes),
        (((1,), (1,)), ((), ())),
        precision=HI,
        preferred_element_type=F32,
    )
    gain, bias = gain_ref[...].reshape(1, channels), bias_ref[...].reshape(1, channels)
    a, s, r, t = [], [], [], []
    for b in range(batch):
        mean = sums[b : b + 1] / count
        var = sums[batch + b : batch + b + 1] / count - mean * mean
        inv = lax.rsqrt(var + EPS)
        r.append(inv)
        t.append(-mean * inv)
        a.append(inv * gain)
        s.append(bias - mean * inv * gain)
    return stack_rows(a + s + r + t, channels)


def put_shifted(ap, b, h, v, left, right):
    t, w, c = v.shape
    j = iota((t, w, c), 1)
    ap[0, b, pl.ds(h, t)] = jnp.where(j == 0, left, pltpu.roll(v, 1, 1))
    ap[1, b, pl.ds(h, t)] = v
    ap[2, b, pl.ds(h, t)] = jnp.where(j == w - 1, right, pltpu.roll(v, w - 1, 1))


def edge_masks():
    ri, rn = lax.axis_index("row"), lax.axis_size("row")
    ci, cn = lax.axis_index("col"), lax.axis_size("col")
    flags = (ri == 0, ri == rn - 1, ci == 0, ci == cn - 1)
    return tuple(jnp.where(f, 0.0, 1.0) for f in flags)


def fill(ap, part, batch, fn, src_ref, halo, visit=None):
    _, _, tall, w, c = ap.shape
    high = tall - 2
    up, down, west, east = edge_masks()
    left, right, top, low = halo
    top, low = top[...].astype(F32), low[...].astype(F32)
    t = 8
    first = part * batch
    for b in range(batch):

        def body(i, carry, b=b):
            start = pl.multiple_of(b * high * w + i * t * w, 16)
            v = src_ref[pl.ds(start, t * w), :].astype(F32).reshape(t, w, c)
            h = i * t
            put_shifted(
                ap,
                b,
                h + 1,
                fn(b, v),
                fn(b, left[first + b, pl.ds(h + 1, t)]) * west,
                fn(b, right[first + b, pl.ds(h + 1, t)]) * east,
            )
            return carry if visit is None else visit(carry, v)

        out = lax.fori_loop(0, high // t, body, jnp.zeros((w, c), F32))
        if visit is not None:
            yield out
        for line, h, edge in ((top, 0, up), (low, tall - 1, down)):
            at = first + b
            put_shifted(
                ap,
                b,
                h,
                fn(b, line[at * w : (at + 1) * w].reshape(1, w, c)) * edge,
                fn(b, left[at, h : h + 1]) * (west * edge),
                fn(b, right[at, h : h + 1]) * (east * edge),
            )


def fill_acts(ap, aff, batch, x_ref, halo):
    c = ap.shape[-1]

    def act(b, x):
        v = x * aff[b : b + 1].reshape(1, 1, c) + aff[batch + b : batch + b + 1].reshape(1, 1, c)
        return v / (1.0 + jnp.exp(-v))

    for _ in fill(ap, 0, batch, act, x_ref, halo):
        pass


def tap_rows(ap, b, kh, kw):
    _, _, tall, w, c = ap.shape
    return ap[kw, b, kh : kh + tall - 2].reshape((tall - 2) * w, c).astype(BF16)


def dacts_kernel(batch, relative, share, *refs):
    g_load, w_load = refs[:2]
    halo = refs[2:6]
    da_ref, gsum_ref, gp_ref, ap, gt = refs[6:]
    g_ref = g_load()
    n, c = g_ref.shape
    _, _, tall, w, _ = ap.shape
    per = (tall - 2) * w
    totals = fill(
        ap, 1, batch, lambda b, v: v, g_ref, halo, lambda tot, v: tot + jnp.sum(v, axis=0)
    )
    totals = [jnp.sum(v, axis=0, keepdims=True) for v in totals]
    gsum_ref[...] = stack_rows([jnp.zeros((1, c), F32)] * (2 * batch) + totals, c)
    w_ref = w_load()
    for b in range(batch):
        acc = jnp.zeros((per, c), F32)
        for kh in range(3):
            for kw in range(3):
                acc = acc + lax.dot_general(
                    tap_rows(ap, b, 2 - kh, 2 - kw),
                    w_ref[kh * 3 + kw],
                    (((1,), (1,)), ((), ())),
                    preferred_element_type=F32,
                )
        da_ref[b * per : (b + 1) * per, :] = acc
    wide = gt.shape[0]
    step = LANES
    for i in range(n // step):
        v = g_ref[i * step : (i + 1) * step, :].astype(F32)
        v = jnp.concatenate([v, jnp.zeros((step, wide - c), F32)], axis=1)
        gt[:, i * step : (i + 1) * step] = jnp.transpose(v).astype(BF16)
    if relative:
        me = lax.axis_index("row") * 2 + (lax.axis_index("col") & 1)
        for q in range(4):
            other = (me ^ ((q % 2) * 2 + q // 2)) * share
            gp_ref[q * share : (q + 1) * share, :] = gt[pl.ds(pl.multiple_of(other, 16), share), :]
    else:
        gp_ref[...] = gt[:c, :]


def wgrad_kernel(batch, count, scale, *refs):
    x_load, gp_load, gain_load, bias_load, st_ref = refs[:5]
    halo = refs[5:9]
    aff_ref, keep_ref, send_ref = refs[9:12]
    ap, part = refs[12:]
    aff = affine_rows(st_ref, gain_load(), bias_load(), batch, count)
    aff_ref[...] = aff
    x_ref = x_load()
    n, channels = x_ref.shape
    _, rows, pieces, share, width = send_ref.shape
    fill_acts(ap, aff, batch, x_ref, halo)
    part[:, 9 * channels :] = jnp.zeros((channels, part.shape[1] - 9 * channels), F32)
    per = n // batch
    gp = gp_load()
    for kh in range(3):
        for kw in range(3):
            tap = kh * 3 + kw
            acc = jnp.zeros((channels, channels), F32)
            for b in range(batch):
                acc = acc + jnp.dot(
                    gp[:, b * per : (b + 1) * per],
                    tap_rows(ap, b, kh, kw),
                    preferred_element_type=F32,
                )
            part[:, tap * channels : (tap + 1) * channels] = acc * scale
    for r in range(rows):
        for p in range(pieces):
            lane = slice(p * width, (p + 1) * width)
            keep_ref[r, p] = part[r * share : (r + 1) * share, lane]
            low = (rows + r) * share
            send_ref[0, r, p] = part[low : low + share, lane].astype(BF16)


def back_kernel(batch, *refs):
    x_load, da_load, aff_ref, gsum_ref, dn_ref, sums_ref = refs
    n, c = dn_ref.shape
    per = n // batch
    rows = []
    aff = aff_ref[...]
    x_ref, da_ref = x_load(), da_load()
    for b in range(batch):
        a, s, r, o = (aff[k * batch + b : k * batch + b + 1] for k in range(4))

        def body(i, carry, b=b, a=a, s=s, r=r, o=o):
            rows_here = pl.ds(pl.multiple_of(b * per + i * 64, 16), 64)
            x = x_ref[rows_here, :].astype(F32)
            normed = x * a + s
            sig = 1.0 / (1.0 + jnp.exp(-normed))
            dn = da_ref[rows_here, :] * sig * (1.0 + normed * (1.0 - sig))
            dn_ref[rows_here, :] = dn
            xhat = x * r + o
            return (
                carry[0] + jnp.sum(dn.reshape(8, 8, c), axis=0),
                carry[1] + jnp.sum((dn * xhat).reshape(8, 8, c), axis=0),
            )

        zero = jnp.zeros((8, c), F32)
        rows.append(lax.fori_loop(0, per // 64, body, (zero, zero)))
    sums_ref[...] = gsum_ref[...] + stack_rows(
        [jnp.sum(v[0], axis=0, keepdims=True) for v in rows]
        + [jnp.sum(v[1], axis=0, keepdims=True) for v in rows],
        c,
    )


def conv_kernel(batch, *refs):
    x_load, w_load, cb_load, aff_ref = refs[:4]
    halo = refs[4:8]
    temb_ref, out_ref, done_ref, ap = refs[8:]
    x_ref = x_load()
    done_ref[...] = jnp.zeros_like(done_ref)
    _, _, tall, w, c = ap.shape
    per = (tall - 2) * w
    fill_acts(ap, aff_ref[...], batch, x_ref, halo)
    w_ref = w_load()
    bias = cb_load()[...].reshape(1, c)
    for b in range(batch):
        acc = jnp.zeros((per, c), F32)
        for kh in range(3):
            for kw in range(3):
                acc = acc + jnp.dot(
                    tap_rows(ap, b, kh, kw), w_ref[kh * 3 + kw], preferred_element_type=F32
                )
        here = slice(b * per, (b + 1) * per)
        out = x_ref[here, :].astype(F32) + acc + bias + temb_ref[b : b + 1, :]
        out_ref[here, :] = out.astype(BF16)


def input_kernel(batch, count, scale, *refs):
    x_load, g_load, dn_load, gain_load, aff_ref, part_ref, other_ref, emb_ref = refs[:8]
    out_ref, gain_out, bias_out, cb_out, tw_out, done_ref = refs[8:]
    done_ref[...] = jnp.zeros_like(done_ref)
    gain_ref = gain_load()
    n, c = out_ref.shape
    per = n // batch
    red = part_ref[...] + other_ref[...]
    aff = aff_ref[...]
    gain = gain_ref[...].reshape(1, c)
    m = group_sums(red * gain) / count
    total = lambda k: sum(red[k * batch + b : k * batch + b + 1] for b in range(batch)) * scale
    bias_out[...] = total(0).reshape(c)
    gain_out[...] = total(1).reshape(c)
    cb_out[...] = total(2).reshape(c)
    rest = red[2 * batch : 3 * batch] * scale
    parts = []
    for _ in range(3):
        parts.append(rest.astype(BF16))
        rest = rest - parts[-1].astype(F32)
    emb = emb_ref[...]
    tw_out[...] = sum(
        lax.dot_general(p, emb, (((0,), (0,)), ((), ())), preferred_element_type=F32)
        for p in reversed(parts)
    )
    x_ref, g_ref, dn_ref = x_load(), g_load(), dn_load()
    for b in range(batch):
        a, r, o = (aff[k * batch + b : k * batch + b + 1] for k in (0, 2, 3))
        m1 = r * m[b : b + 1]
        m2 = r * m[batch + b : batch + b + 1]

        def body(i, _, b=b, a=a, r=r, o=o, m1=m1, m2=m2):
            here = pl.ds(pl.multiple_of(b * per + i * 64, 16), 64)
            xhat = x_ref[here, :].astype(F32) * r + o
            out_ref[here, :] = g_ref[here, :].astype(F32) + (dn_ref[here, :] * a - m1 - xhat * m2)
            return 0

        lax.fori_loop(0, per // 64, body, 0)


def place():
    col = lax.axis_index("col")
    return col & 1, (col >> 1) & 1, col >> 2


def step_one(nz, keep_ref, got_ref, a_send, a_keep, b_send, b_keep, done_ref):
    _, xb, _ = place()
    half = nz // 2
    done_ref[...] = jnp.zeros_like(done_ref)
    total = lambda r, p: keep_ref[r, p] + got_ref[r, p].astype(F32)
    for x in range(2):
        for z in range(half):
            p = x * nz + z
            a_send[x, z] = total(1, p).astype(BF16)
            a_keep[x, z] = total(0, p)
    for r in range(2):
        for z in range(half):
            b_send[r, z] = total(r, (1 - xb) * nz + half + z).astype(BF16)
            b_keep[r, z] = total(r, xb * nz + half + z)


def step_two(nz, a_got, a_keep, b_got, b_keep, s, s_got, a_send, a_next, b_send, b_next, s_next):
    _, xb, _ = place()
    s_next[...] = s[...] + s_got[...]
    for z in range(nz // 2):
        a_send[z] = (a_keep[1 - xb, z] + a_got[1 - xb, z].astype(F32)).astype(BF16)
        a_next[z] = a_keep[xb, z] + a_got[xb, z].astype(F32)
        b_send[z] = (b_keep[1, z] + b_got[1, z].astype(F32)).astype(BF16)
        b_next[z] = b_keep[0, z] + b_got[0, z].astype(F32)


def step_three(nz, a_got, a_keep, b_got, b_keep, s, s_got, own_ref, s_next, *refs):
    s_next[...] = s[...] + s_got[...]
    sends, held = refs[: nz - 1], refs[nz - 1]
    _, _, zb = place()
    half = nz // 2
    for z in range(half):
        held[z] = a_keep[z] + a_got[z].astype(F32)
        held[half + z] = b_keep[z] + b_got[z].astype(F32)
    own_ref[...] = held[zb]
    for k in range(1, nz):
        sends[k - 1][...] = held[zb ^ k].astype(BF16)


def step_four(nz, own_ref, s, *refs):
    total, sums = own_ref[...], s[...]
    for k in range(nz - 1):
        total = total + refs[k][...].astype(F32)
        sums = sums + refs[nz - 1 + k][...]
    refs[-2][...] = total.astype(BF16)
    refs[-1][...] = sums


def step_five(nz, *refs):
    out = refs[-1]
    width = refs[0].shape[-1]
    _, xb, zb = place()
    for k, ref in enumerate(refs[:-1]):
        p = (xb ^ (k % 2)) * nz + (zb ^ (k // 2))
        out[:, pl.ds(pl.multiple_of(p * width, LANES), width)] = ref[...]


def step_six(mine_ref, other_ref, out_ref, full):
    core, _, _ = place()
    share = mine_ref.shape[0]
    c = out_ref.shape[-1]
    full[pl.ds(pl.multiple_of(core * share, 16), share), :] = mine_ref[...].astype(F32)
    full[pl.ds(pl.multiple_of((1 - core) * share, 16), share), :] = other_ref[...].astype(F32)
    for tap in range(out_ref.shape[0]):
        out_ref[tap] = full[:, tap * c : (tap + 1) * c]


def embed(timestep, embed_in, embed_out):
    half = embed_in.shape[0] // 2
    freqs = jnp.exp(-math.log(10000.0) * jnp.arange(half, dtype=F32) / half)
    angles = timestep.astype(F32)[:, None] * freqs[None, :]
    sinus = jnp.concatenate([jnp.cos(angles), jnp.sin(angles)], axis=1).astype(BF16)
    first_hidden = jax.nn.silu(jnp.dot(sinus, embed_in, preferred_element_type=F32)).astype(BF16)
    return jax.nn.silu(jnp.dot(first_hidden, embed_out, preferred_element_type=F32)).astype(BF16)


def partner(value, bit):
    size = lax.axis_size("row") * lax.axis_size("col")
    return lax.ppermute(value, AXES, [(i, i ^ bit) for i in range(size)])


def shift(value, down, right):
    rows, cols = lax.axis_size("row"), lax.axis_size("col")
    pairs = []
    for r in range(rows):
        for c in range(cols):
            to = (r + down, c + right)
            if 0 <= to[0] < rows and 0 <= to[1] < cols:
                pairs.append((r * cols + c, to[0] * cols + to[1]))
    return lax.ppermute(value, AXES, pairs)


def swap(value):
    return partner(value, lax.axis_size("col"))


def local(
    latent,
    timestep,
    group_norm_gain,
    group_norm_bias,
    conv_w,
    conv_b,
    embed_in,
    embed_out,
    time_w,
    cotangent,
):
    batch, high, wide, channels = latent.shape
    rows, cols = lax.axis_size("row"), lax.axis_size("col")
    devices = rows * cols
    n = batch * high * wide
    count = high * rows * wide * cols * (channels // NORM_GROUPS)
    scale = 1.0 / math.sqrt(batch * high * rows * wide * cols)
    x2 = latent.reshape(n, channels)
    g2 = cotangent.reshape(n, channels)
    w9 = conv_w.reshape(9, channels, channels)
    of = jax.ShapeDtypeStruct

    lanes = -(-2 * batch * NORM_GROUPS // LANES) * LANES
    column = of((2 * batch, high + 2, 1, channels), F32)
    row = lax.axis_index("row")

    def edge(at):
        lines = [lax.dynamic_slice_in_dim(v, at, 1, 1) for v in (latent, cotangent)]
        return jnp.concatenate(lines, axis=0).reshape(2 * batch * wide, channels)

    if rows == 2:
        top = swap(edge(jnp.where(row == 0, high - 1, 0)))
        low = top
    else:
        top, low = shift(edge(high - 1), 1, 0), shift(edge(0), -1, 0)
    pay, west, east = call(
        functools.partial(stats_kernel, batch, wide),
        (of((devices, 1, lanes), F32), column, column),
        (top, low),
        far=(x2, g2),
        vmem=64,
    )
    left, right = shift(east, 0, 1), shift(west, 0, -1)
    stats = lax.all_to_all(pay, AXES, 0, 0)
    halo = (left, right, top, low)

    shifted = pltpu.VMEM((3, batch, high + 2, wide, channels), F32)
    nz = cols // 4
    share = channels // (2 * rows)
    relative = rows == 2 and nz >= 2 and share % 16 == 0
    pieces = cols // 2 if relative else 1
    width = -(-9 * channels // (LANES * pieces)) * LANES
    padded = -(-channels // LANES) * LANES
    conv_flops = 2 * 9 * n * channels * channels
    if not relative:
        share = channels // 2
    keep_rows = rows if relative else 1
    dacts, gsum, flipped = call(
        functools.partial(dacts_kernel, batch, relative, share),
        (of((n, channels), F32), of((8, channels), F32), of((channels, n), BF16)),
        halo,
        far=(g2, w9),
        vmem=64,
        scratch=(shifted, pltpu.VMEM((padded, n), BF16)),
        flops=conv_flops,
    )
    aff, keep, send = call(
        functools.partial(wgrad_kernel, batch, count, scale),
        (
            of((8, channels), F32),
            of((keep_rows, pieces, share, width), F32),
            of((1, keep_rows, pieces, share, width), BF16),
        ),
        (stats, *halo),
        far=(x2, flipped, group_norm_gain, group_norm_bias),
        vmem=56,
        scratch=(shifted, pltpu.VMEM((channels, pieces * width), F32)),
        flops=conv_flops,
    )

    token = of((8, LANES), F32)
    if relative:
        half = nz // 2
        many = lambda k, dtype: of((*k, share, width), dtype)
        got = partner(send[0], 1)
        a_send, a_keep, b_send, b_keep, done = call(
            functools.partial(step_one, nz),
            (many((2, half), BF16), many((2, half), F32)) * 2 + (token,),
            (keep, got),
        )
        a_got, b_got = partner(a_send, cols), partner(b_send, 2)
        first = (done,)
    else:
        first = ()

    dn, sums = call(
        functools.partial(back_kernel, batch),
        (of((n, channels), F32), of((8, channels), F32)),
        (aff, gsum),
        far=(x2, dacts),
        vmem=58,
        after=first,
        flops=20 * n * channels,
    )
    emb = embed(timestep, embed_in, embed_out)
    temb = jnp.dot(emb, time_w, preferred_element_type=F32)

    block_out, done = call(
        functools.partial(conv_kernel, batch),
        (of((n, channels), BF16), token),
        (aff, *halo, temb),
        far=(x2, w9, conv_b),
        after=(sums,),
        vmem=58,
        scratch=(shifted,),
        flops=conv_flops,
    )

    if relative:
        s_shape = of(sums.shape, F32)
        a_send, a_keep, b_send, b_keep, sums = call(
            functools.partial(step_two, nz),
            (many((half,), BF16), many((half,), F32)) * 2 + (s_shape,),
            (a_got, a_keep, b_got, b_keep, sums, partner(sums, 1)),
            after=(done,),
        )
        a_got, b_got = partner(a_send, 2), partner(b_send, cols)
        own, sums, *sends = call(
            functools.partial(step_three, nz),
            (many((), F32), s_shape, *[many((), BF16)] * (nz - 1)),
            (a_got, a_keep, b_got, b_keep, sums, partner(sums, 2)),
            scratch=(pltpu.VMEM((nz, share, width), F32),),
        )
        gots = [partner(v, 4 * (k + 1)) for k, v in enumerate(sends)]
        gots += [partner(sums, 4 * k) for k in range(1, nz)]

    if relative:
        own, sums = call(
            functools.partial(step_four, nz),
            (many((), BF16), s_shape),
            (own, sums, *gots),
        )
        others = [partner(own, 2 * k) for k in range(1, pieces)]
    else:
        bit = 1
        while 2 * bit < devices:
            sums = sums + partner(sums, bit)
            bit *= 2

    vector = of((channels,), F32)
    input_grad, gain_grad, bias_grad, conv_b_grad, time_grad, done = call(
        functools.partial(input_kernel, batch, count, scale),
        (of((n, channels), F32), *[vector] * 3, of((channels, emb.shape[1]), F32), token),
        (aff, sums, partner(sums, cols if relative else bit), emb),
        far=(x2, g2, dn, group_norm_gain),
        vmem=60,
        flops=8 * n * channels,
    )

    if relative:
        mine = call(
            functools.partial(step_five, nz),
            of((share, pieces * width), BF16),
            (own, *others),
            after=(done,),
        )
        grad = call(
            step_six,
            of((9, 2 * share, channels), F32),
            (mine, partner(mine, 1)),
            scratch=(pltpu.VMEM((2 * share, pieces * width), F32),),
        )
    else:
        both = jnp.concatenate([keep[0, 0], send[0, 0, 0].astype(F32)], axis=0)
        both = lax.psum(both[:, : 9 * channels], AXES)
        mine = channels // rows
        grad = lax.dynamic_slice_in_dim(both, lax.axis_index("row") * mine, mine, 0)
        grad = jnp.transpose(grad.reshape(mine, 9, channels), (1, 0, 2))
    conv_w_grad = jnp.transpose(grad.reshape(3, 3, channels // rows, channels), (2, 0, 1, 3))
    return (
        block_out.reshape(latent.shape),
        input_grad.reshape(latent.shape),
        conv_w_grad,
        gain_grad,
        bias_grad,
        conv_b_grad,
        time_grad.T,
    )


def solution(mesh):
    return jax.shard_map(
        local,
        mesh=mesh,
        in_specs=(
            P(None, "row", "col", None),
            P(),
            P(),
            P(),
            P(),
            P(),
            P(),
            P(),
            P(),
            P(None, "row", "col", None),
        ),
        out_specs=(
            P(None, "row", "col", None),
            P(None, "row", "col", None),
            P("row", None, None, None),
            P(),
            P(),
            P(),
            P(),
        ),
        check_vma=False,
    )
```

```python
import functools
import math

import jax
import jax.numpy as jnp
from jax import lax
from jax.experimental import pallas as pl
from jax.experimental.pallas import tpu as pltpu
from jax.sharding import PartitionSpec as P

NORM_GROUPS = 32
EPS = 1e-05
LANES = 128
F32 = jnp.float32
BF16 = jnp.bfloat16
AXES = ("row", "col")
HI = lax.Precision.HIGHEST


def iota(shape, dim):
    return lax.broadcasted_iota(jnp.int32, shape, dim)


def call(body, out_shape, operands, far=(), after=(), scratch=(), vmem=20, flops=0):
    count, used, waits = len(far), len(operands), len(after)

    def kernel(*refs):
        ins = refs[:count]
        rest = refs[count : count + used] + refs[count + used + waits :]
        if not count:
            return body(*rest)
        holds, sems = rest[-1 - count : -1], rest[-1]
        copies = [
            pltpu.make_async_copy(ins[i], holds[i], sems.at[i]) for i in range(count)
        ]
        for c in copies:
            c.start()

        def loader(i):
            def load():
                copies[i].wait()
                return holds[i]

            return load

        body(*[loader(i) for i in range(count)], *rest[: -1 - count])

    near = pl.BlockSpec(memory_space=pltpu.VMEM)
    scratch = list(scratch)
    if count:
        scratch += [pltpu.VMEM(v.shape, v.dtype) for v in far]
        scratch.append(pltpu.SemaphoreType.DMA((count,)))
    return pl.pallas_call(
        kernel,
        out_shape=out_shape,
        in_specs=[pl.BlockSpec(memory_space=pltpu.HBM)] * count
        + [near] * used
        + [near] * waits,
        out_specs=jax.tree.map(lambda _: near, out_shape),
        scratch_shapes=scratch,
        compiler_params=pltpu.CompilerParams(vmem_limit_bytes=vmem * 2**20),
        cost_estimate=pl.CostEstimate(flops=flops, bytes_accessed=2_000_000, transcendentals=0),
    )(*far, *operands, *after)


def call_far(body, out_shape, operands, far=(), after=(), scratch=(), vmem=58, flops=0):
    outs, tree = jax.tree.flatten(out_shape)
    ins = (*far, *operands)
    waits, own = len(after), len(scratch)
    slots = len(outs) + 4

    def kernel(*refs):
        src, refs = refs[: len(ins)], refs[len(ins) + waits :]
        dst, refs = refs[: len(outs)], refs[len(outs) :]
        mine, refs = refs[:own], refs[own:]
        held, refs = refs[: len(ins)], refs[len(ins) :]
        made, (sem_in, sem_out) = refs[: len(outs)], refs[len(outs) :]
        copies = [pltpu.make_async_copy(a, b, sem_in.at[i]) for i, (a, b) in enumerate(zip(src, held))]
        for c in (*copies[len(far) :], *copies[: len(far)]):
            c.start()

        def loader(i):
            def load():
                copies[i].wait()
                return held[i]

            return load

        sent = {}

        def emit(i, start=None, size=None):
            a, b = made[i], dst[i]
            if start is not None:
                a, b = a.at[pl.ds(start, size)], b.at[pl.ds(start, size)]
            c = pltpu.make_async_copy(a, b, sem_out.at[sum(map(len, sent.values()))])
            c.start()
            sent.setdefault(i, []).append(c)

        for c in copies[len(far) :]:
            c.wait()
        body(emit, *[loader(i) for i in range(len(far))], *held[len(far) :], *made, *mine)
        for i in range(len(outs)):
            if i not in sent:
                emit(i)
        for parts in sent.values():
            for c in parts:
                c.wait()

    hbm = pl.BlockSpec(memory_space=pltpu.HBM)
    near = pl.BlockSpec(memory_space=pltpu.VMEM)
    results = pl.pallas_call(
        kernel,
        out_shape=tuple(outs),
        in_specs=[hbm] * len(ins) + [near] * waits,
        out_specs=(hbm,) * len(outs),
        scratch_shapes=[
            *scratch,
            *[pltpu.VMEM(v.shape, v.dtype) for v in ins],
            *[pltpu.VMEM(v.shape, v.dtype) for v in outs],
            pltpu.SemaphoreType.DMA((len(ins),)),
            pltpu.SemaphoreType.DMA((slots,)),
        ],
        compiler_params=pltpu.CompilerParams(vmem_limit_bytes=vmem * 2**20),
        cost_estimate=pl.CostEstimate(flops=flops, bytes_accessed=2_000_000, transcendentals=0),
    )(*ins, *after)
    return jax.tree.unflatten(tree, results)


def group_matrix(channels, lanes):
    size = channels // NORM_GROUPS
    group = iota((channels, lanes), 1) & (NORM_GROUPS - 1)
    channel = iota((channels, lanes), 0)
    return jnp.where((channel >= group * size) & (channel < (group + 1) * size), 1.0, 0.0).astype(F32)


def group_sums(rows):
    lanes = LANES
    g = group_matrix(rows.shape[1], lanes)
    keep = iota((8, lanes), 1) < NORM_GROUPS
    s = jnp.dot(rows, g, precision=HI, preferred_element_type=F32)
    s = jnp.where(keep, s, 0.0)
    return lax.dot_general(
        s, g, (((1,), (1,)), ((), ())), precision=HI, preferred_element_type=F32
    )


def stack_rows(rows, channels):
    r = iota((8, channels), 0)
    out = jnp.zeros((8, channels), F32)
    for k, v in enumerate(rows):
        out = out + jnp.where(r == k, v, 0.0)
    return out


def stats_kernel(batch, w, emit, x_load, g_load, top_ref, low_ref, pay_ref, west_ref, east_ref):
    sums = []
    step = 64
    t = step // w
    top, low = top_ref[...].astype(F32), low_ref[...].astype(F32)
    for k, load in enumerate((x_load, g_load)):
        ref = load()
        n, channels = ref.shape
        per = n // batch
        high = per // w
        for b in range(batch):
            at = k * batch + b

            def add(i, c, b=b, k=k, ref=ref, at=at):
                start = pl.multiple_of(b * per + i * step, 16)
                v = ref[pl.ds(start, step), :].astype(F32).reshape(t, w, channels)
                west_ref[at, pl.ds(i * t + 1, t)] = v[:, :1]
                east_ref[at, pl.ds(i * t + 1, t)] = v[:, w - 1 :]
                if k:
                    return c
                return c[0] + jnp.sum(v, axis=0), c[1] + jnp.sum(v * v, axis=0)

            zero = jnp.zeros((w, channels), F32)
            s, q = lax.fori_loop(0, per // step, add, (zero, zero))
            if not k:
                sums.append((jnp.sum(s, axis=0, keepdims=True), jnp.sum(q, axis=0, keepdims=True)))
            for v, h in ((top, 0), (low, high + 1)):
                west_ref[at, h] = v[at * w : at * w + 1]
                east_ref[at, h] = v[(at + 1) * w - 1 : (at + 1) * w]
    stacked = stack_rows([r[0] for r in sums] + [r[1] for r in sums], channels)
    lanes = pay_ref.shape[-1]
    res = jnp.dot(
        stacked, group_matrix(channels, lanes), precision=HI, preferred_element_type=F32
    )
    first = iota((8, lanes), 0) * NORM_GROUPS
    lane = iota((8, lanes), 1)
    mine = (lane >= first) & (lane < first + NORM_GROUPS)
    row = jnp.sum(jnp.where(mine, res, 0.0), axis=0, keepdims=True)
    pay_ref[...] = jnp.broadcast_to(row[None], pay_ref.shape)


def affine_rows(st_ref, gain_ref, bias_ref, batch, count):
    channels = gain_ref.shape[-1]
    lanes = st_ref.shape[-1]
    total = jnp.sum(st_ref[...], axis=0)
    first = iota((8, lanes), 0) * NORM_GROUPS
    lane = iota((8, lanes), 1)
    mine = (lane >= first) & (lane < first + NORM_GROUPS)
    spread = jnp.where(mine, total, 0.0)
    sums = lax.dot_general(
        spread,
        group_matrix(channels, lanes),
        (((1,), (1,)), ((), ())),
        precision=HI,
        preferred_element_type=F32,
    )
    gain, bias = gain_ref[...].reshape(1, channels), bias_ref[...].reshape(1, channels)
    a, s, r, t = [], [], [], []
    for b in range(batch):
        mean = sums[b : b + 1] / count
        var = sums[batch + b : batch + b + 1] / count - mean * mean
        inv = lax.rsqrt(var + EPS)
        r.append(inv)
        t.append(-mean * inv)
        a.append(inv * gain)
        s.append(bias - mean * inv * gain)
    return stack_rows(a + s + r + t, channels)


def put_shifted(ap, b, h, v, left, right):
    t, w, c = v.shape
    j = iota((t, w, c), 1)
    ap[0, b, pl.ds(h, t)] = jnp.where(j == 0, left, pltpu.roll(v, 1, 1))
    ap[1, b, pl.ds(h, t)] = v
    ap[2, b, pl.ds(h, t)] = jnp.where(j == w - 1, right, pltpu.roll(v, w - 1, 1))


def edge_masks():
    ri, rn = lax.axis_index("row"), lax.axis_size("row")
    ci, cn = lax.axis_index("col"), lax.axis_size("col")
    flags = (ri == 0, ri == rn - 1, ci == 0, ci == cn - 1)
    return tuple(jnp.where(f, 0.0, 1.0) for f in flags)


def fill(ap, part, batch, fn, src_ref, halo, visit=None):
    _, _, tall, w, c = ap.shape
    high = tall - 2
    up, down, west, east = edge_masks()
    left, right, top, low = halo
    top, low = top[...].astype(F32), low[...].astype(F32)
    t = 8
    first = part * batch
    for b in range(batch):

        def body(i, carry, b=b):
            start = pl.multiple_of(b * high * w + i * t * w, 16)
            v = src_ref[pl.ds(start, t * w), :].astype(F32).reshape(t, w, c)
            h = i * t
            put_shifted(
                ap,
                b,
                h + 1,
                fn(b, v),
                fn(b, left[first + b, pl.ds(h + 1, t)]) * west,
                fn(b, right[first + b, pl.ds(h + 1, t)]) * east,
            )
            return carry if visit is None else visit(carry, v)

        out = lax.fori_loop(0, high // t, body, jnp.zeros((w, c), F32))
        if visit is not None:
            yield out
        for line, h, edge in ((top, 0, up), (low, tall - 1, down)):
            at = first + b
            put_shifted(
                ap,
                b,
                h,
                fn(b, line[at * w : (at + 1) * w].reshape(1, w, c)) * edge,
                fn(b, left[at, h : h + 1]) * (west * edge),
                fn(b, right[at, h : h + 1]) * (east * edge),
            )


def fill_acts(ap, aff, batch, x_ref, halo):
    c = ap.shape[-1]

    def act(b, x):
        v = x * aff[b : b + 1].reshape(1, 1, c) + aff[batch + b : batch + b + 1].reshape(1, 1, c)
        return v / (1.0 + jnp.exp(-v))

    for _ in fill(ap, 0, batch, act, x_ref, halo):
        pass


def tap_rows(ap, b, kh, kw):
    _, _, tall, w, c = ap.shape
    return ap[kw, b, kh : kh + tall - 2].reshape((tall - 2) * w, c).astype(BF16)


def dacts_kernel(batch, relative, share, emit, *refs):
    g_load, w_load = refs[:2]
    halo = refs[2:6]
    da_ref, gsum_ref, gp_ref, ap, gt = refs[6:]
    g_ref = g_load()
    n, c = g_ref.shape
    _, _, tall, w, _ = ap.shape
    per = (tall - 2) * w
    totals = fill(
        ap, 1, batch, lambda b, v: v, g_ref, halo, lambda tot, v: tot + jnp.sum(v, axis=0)
    )
    totals = [jnp.sum(v, axis=0, keepdims=True) for v in totals]
    gsum_ref[...] = stack_rows([jnp.zeros((1, c), F32)] * (2 * batch) + totals, c)
    wide = gt.shape[0]
    step = LANES
    for i in range(n // step):
        v = g_ref[i * step : (i + 1) * step, :].astype(F32)
        v = jnp.concatenate([v, jnp.zeros((step, wide - c), F32)], axis=1)
        gt[:, i * step : (i + 1) * step] = jnp.transpose(v).astype(BF16)
    if relative:
        me = lax.axis_index("row") * 2 + (lax.axis_index("col") & 1)
        for q in range(4):
            other = (me ^ ((q % 2) * 2 + q // 2)) * share
            gp_ref[q * share : (q + 1) * share, :] = gt[pl.ds(pl.multiple_of(other, 16), share), :]
    else:
        gp_ref[...] = gt[:c, :]
    emit(1)
    emit(2)
    w_ref = w_load()
    for b in range(batch):
        acc = jnp.zeros((per, c), F32)
        for kh in range(3):
            for kw in range(3):
                acc = acc + lax.dot_general(
                    tap_rows(ap, b, 2 - kh, 2 - kw),
                    w_ref[kh * 3 + kw],
                    (((1,), (1,)), ((), ())),
                    preferred_element_type=F32,
                )
        da_ref[b * per : (b + 1) * per, :] = acc
        emit(0, b * per, per)


def wgrad_kernel(batch, count, scale, emit, *refs):
    x_load, gp_load, gain_load, bias_load, st_ref = refs[:5]
    halo = refs[5:9]
    aff_ref, keep_ref, send_ref = refs[9:12]
    ap, part = refs[12:]
    aff = affine_rows(st_ref, gain_load(), bias_load(), batch, count)
    aff_ref[...] = aff
    emit(0)
    x_ref = x_load()
    n, channels = x_ref.shape
    _, rows, pieces, share, width = send_ref.shape
    fill_acts(ap, aff, batch, x_ref, halo)
    part[:, 9 * channels :] = jnp.zeros((channels, part.shape[1] - 9 * channels), F32)
    per = n // batch
    gp = gp_load()
    for kh in range(3):
        for kw in range(3):
            tap = kh * 3 + kw
            acc = jnp.zeros((channels, channels), F32)
            for b in range(batch):
                acc = acc + jnp.dot(
                    gp[:, b * per : (b + 1) * per],
                    tap_rows(ap, b, kh, kw),
                    preferred_element_type=F32,
                )
            part[:, tap * channels : (tap + 1) * channels] = acc * scale
    for r in range(rows):
        for p in range(pieces):
            lane = slice(p * width, (p + 1) * width)
            low = (rows + r) * share
            send_ref[0, r, p] = part[low : low + share, lane].astype(BF16)
    emit(2)
    for r in range(rows):
        for p in range(pieces):
            lane = slice(p * width, (p + 1) * width)
            keep_ref[r, p] = part[r * share : (r + 1) * share, lane]
        emit(1, r, 1)


def back_kernel(batch, emit, *refs):
    x_load, da_load, aff_ref, gsum_ref, dn_ref, sums_ref = refs
    n, c = dn_ref.shape
    per = n // batch
    rows = []
    aff = aff_ref[...]
    x_ref, da_ref = x_load(), da_load()
    for b in range(batch):
        a, s, r, o = (aff[k * batch + b : k * batch + b + 1] for k in range(4))

        def body(i, carry, b=b, a=a, s=s, r=r, o=o):
            rows_here = pl.ds(pl.multiple_of(b * per + i * 64, 16), 64)
            x = x_ref[rows_here, :].astype(F32)
            normed = x * a + s
            sig = 1.0 / (1.0 + jnp.exp(-normed))
            dn = da_ref[rows_here, :] * sig * (1.0 + normed * (1.0 - sig))
            dn_ref[rows_here, :] = dn
            xhat = x * r + o
            return (
                carry[0] + jnp.sum(dn.reshape(8, 8, c), axis=0),
                carry[1] + jnp.sum((dn * xhat).reshape(8, 8, c), axis=0),
            )

        zero = jnp.zeros((8, c), F32)
        rows.append(lax.fori_loop(0, per // 64, body, (zero, zero)))
        emit(0, b * per, per)
    sums_ref[...] = gsum_ref[...] + stack_rows(
        [jnp.sum(v[0], axis=0, keepdims=True) for v in rows]
        + [jnp.sum(v[1], axis=0, keepdims=True) for v in rows],
        c,
    )


def conv_kernel(batch, emit, *refs):
    x_load, w_load, cb_load, aff_ref = refs[:4]
    halo = refs[4:8]
    temb_ref, out_ref, done_ref, ap = refs[8:]
    x_ref = x_load()
    done_ref[...] = jnp.zeros_like(done_ref)
    _, _, tall, w, c = ap.shape
    per = (tall - 2) * w
    fill_acts(ap, aff_ref[...], batch, x_ref, halo)
    w_ref = w_load()
    bias = cb_load()[...].reshape(1, c)
    for b in range(batch):
        acc = jnp.zeros((per, c), F32)
        for kh in range(3):
            for kw in range(3):
                acc = acc + jnp.dot(
                    tap_rows(ap, b, kh, kw), w_ref[kh * 3 + kw], preferred_element_type=F32
                )
        here = slice(b * per, (b + 1) * per)
        out = x_ref[here, :].astype(F32) + acc + bias + temb_ref[b : b + 1, :]
        out_ref[here, :] = out.astype(BF16)
        emit(0, b * per, per)


def input_kernel(batch, count, scale, emit, *refs):
    x_load, g_load, dn_load, gain_load, aff_ref, part_ref, other_ref, emb_ref = refs[:8]
    out_ref, gain_out, bias_out, cb_out, tw_out, done_ref = refs[8:]
    done_ref[...] = jnp.zeros_like(done_ref)
    gain_ref = gain_load()
    n, c = out_ref.shape
    per = n // batch
    red = part_ref[...] + other_ref[...]
    aff = aff_ref[...]
    gain = gain_ref[...].reshape(1, c)
    m = group_sums(red * gain) / count
    total = lambda k: sum(red[k * batch + b : k * batch + b + 1] for b in range(batch)) * scale
    bias_out[...] = total(0).reshape(c)
    gain_out[...] = total(1).reshape(c)
    cb_out[...] = total(2).reshape(c)
    rest = red[2 * batch : 3 * batch] * scale
    parts = []
    for _ in range(3):
        parts.append(rest.astype(BF16))
        rest = rest - parts[-1].astype(F32)
    emb = emb_ref[...]
    tw_out[...] = sum(
        lax.dot_general(p, emb, (((0,), (0,)), ((), ())), preferred_element_type=F32)
        for p in reversed(parts)
    )
    emit(4)
    x_ref, g_ref, dn_ref = x_load(), g_load(), dn_load()
    for b in range(batch):
        a, r, o = (aff[k * batch + b : k * batch + b + 1] for k in (0, 2, 3))
        m1 = r * m[b : b + 1]
        m2 = r * m[batch + b : batch + b + 1]

        def body(i, _, b=b, a=a, r=r, o=o, m1=m1, m2=m2):
            here = pl.ds(pl.multiple_of(b * per + i * 64, 16), 64)
            xhat = x_ref[here, :].astype(F32) * r + o
            out_ref[here, :] = g_ref[here, :].astype(F32) + (dn_ref[here, :] * a - m1 - xhat * m2)
            return 0

        lax.fori_loop(0, per // 64, body, 0)
        emit(0, b * per, per)


def place():
    col = lax.axis_index("col")
    return col & 1, (col >> 1) & 1, col >> 2


def step_one(nz, keep_ref, got_ref, a_send, a_keep, b_send, b_keep, done_ref):
    _, xb, _ = place()
    half = nz // 2
    done_ref[...] = jnp.zeros_like(done_ref)
    total = lambda r, p: keep_ref[r, p] + got_ref[r, p].astype(F32)
    for x in range(2):
        for z in range(half):
            p = x * nz + z
            a_send[x, z] = total(1, p).astype(BF16)
            a_keep[x, z] = total(0, p)
    for r in range(2):
        for z in range(half):
            b_send[r, z] = total(r, (1 - xb) * nz + half + z).astype(BF16)
            b_keep[r, z] = total(r, xb * nz + half + z)


def step_two(nz, a_got, a_keep, b_got, b_keep, s, s_got, a_send, a_next, b_send, b_next, s_next):
    _, xb, _ = place()
    s_next[...] = s[...] + s_got[...]
    for z in range(nz // 2):
        a_send[z] = (a_keep[1 - xb, z] + a_got[1 - xb, z].astype(F32)).astype(BF16)
        a_next[z] = a_keep[xb, z] + a_got[xb, z].astype(F32)
        b_send[z] = (b_keep[1, z] + b_got[1, z].astype(F32)).astype(BF16)
        b_next[z] = b_keep[0, z] + b_got[0, z].astype(F32)


def step_three(nz, a_got, a_keep, b_got, b_keep, s, s_got, own_ref, s_next, *refs):
    s_next[...] = s[...] + s_got[...]
    sends, held = refs[: nz - 1], refs[nz - 1]
    _, _, zb = place()
    half = nz // 2
    for z in range(half):
        held[z] = a_keep[z] + a_got[z].astype(F32)
        held[half + z] = b_keep[z] + b_got[z].astype(F32)
    own_ref[...] = held[zb]
    for k in range(1, nz):
        sends[k - 1][...] = held[zb ^ k].astype(BF16)


def step_four(nz, own_ref, s, *refs):
    total, sums = own_ref[...], s[...]
    for k in range(nz - 1):
        total = total + refs[k][...].astype(F32)
        sums = sums + refs[nz - 1 + k][...]
    refs[-2][...] = total.astype(BF16)
    refs[-1][...] = sums


def step_five(nz, *refs):
    out = refs[-1]
    width = refs[0].shape[-1]
    _, xb, zb = place()
    for k, ref in enumerate(refs[:-1]):
        p = (xb ^ (k % 2)) * nz + (zb ^ (k // 2))
        out[:, pl.ds(pl.multiple_of(p * width, LANES), width)] = ref[...]


def step_six(mine_ref, other_ref, out_ref, full):
    core, _, _ = place()
    share = mine_ref.shape[0]
    c = out_ref.shape[-1]
    full[pl.ds(pl.multiple_of(core * share, 16), share), :] = mine_ref[...].astype(F32)
    full[pl.ds(pl.multiple_of((1 - core) * share, 16), share), :] = other_ref[...].astype(F32)
    for tap in range(out_ref.shape[0]):
        out_ref[tap] = full[:, tap * c : (tap + 1) * c]


def embed(timestep, embed_in, embed_out):
    half = embed_in.shape[0] // 2
    freqs = jnp.exp(-math.log(10000.0) * jnp.arange(half, dtype=F32) / half)
    angles = timestep.astype(F32)[:, None] * freqs[None, :]
    sinus = jnp.concatenate([jnp.cos(angles), jnp.sin(angles)], axis=1).astype(BF16)
    first_hidden = jax.nn.silu(jnp.dot(sinus, embed_in, preferred_element_type=F32)).astype(BF16)
    return jax.nn.silu(jnp.dot(first_hidden, embed_out, preferred_element_type=F32)).astype(BF16)


def partner(value, bit):
    size = lax.axis_size("row") * lax.axis_size("col")
    return lax.ppermute(value, AXES, [(i, i ^ bit) for i in range(size)])


def shift(value, down, right):
    rows, cols = lax.axis_size("row"), lax.axis_size("col")
    pairs = []
    for r in range(rows):
        for c in range(cols):
            to = (r + down, c + right)
            if 0 <= to[0] < rows and 0 <= to[1] < cols:
                pairs.append((r * cols + c, to[0] * cols + to[1]))
    return lax.ppermute(value, AXES, pairs)


def swap(value):
    return partner(value, lax.axis_size("col"))


def local(
    latent,
    timestep,
    group_norm_gain,
    group_norm_bias,
    conv_w,
    conv_b,
    embed_in,
    embed_out,
    time_w,
    cotangent,
):
    batch, high, wide, channels = latent.shape
    rows, cols = lax.axis_size("row"), lax.axis_size("col")
    devices = rows * cols
    n = batch * high * wide
    count = high * rows * wide * cols * (channels // NORM_GROUPS)
    scale = 1.0 / math.sqrt(batch * high * rows * wide * cols)
    x2 = latent.reshape(n, channels)
    g2 = cotangent.reshape(n, channels)
    w9 = conv_w.reshape(9, channels, channels)
    of = jax.ShapeDtypeStruct

    lanes = -(-2 * batch * NORM_GROUPS // LANES) * LANES
    column = of((2 * batch, high + 2, 1, channels), F32)
    row = lax.axis_index("row")

    def edge(at):
        lines = [lax.dynamic_slice_in_dim(v, at, 1, 1) for v in (latent, cotangent)]
        return jnp.concatenate(lines, axis=0).reshape(2 * batch * wide, channels)

    if rows == 2:
        top = swap(edge(jnp.where(row == 0, high - 1, 0)))
        low = top
    else:
        top, low = shift(edge(high - 1), 1, 0), shift(edge(0), -1, 0)
    pay, west, east = call_far(
        functools.partial(stats_kernel, batch, wide),
        (of((devices, 1, lanes), F32), column, column),
        (top, low),
        far=(x2, g2),
        vmem=64,
    )
    left, right = shift(east, 0, 1), shift(west, 0, -1)
    stats = lax.all_to_all(pay, AXES, 0, 0)
    halo = (left, right, top, low)

    shifted = pltpu.VMEM((3, batch, high + 2, wide, channels), F32)
    nz = cols // 4
    share = channels // (2 * rows)
    relative = rows == 2 and nz >= 2 and share % 16 == 0
    pieces = cols // 2 if relative else 1
    width = -(-9 * channels // (LANES * pieces)) * LANES
    padded = -(-channels // LANES) * LANES
    conv_flops = 2 * 9 * n * channels * channels
    if not relative:
        share = channels // 2
    keep_rows = rows if relative else 1
    dacts, gsum, flipped = call_far(
        functools.partial(dacts_kernel, batch, relative, share),
        (of((n, channels), F32), of((8, channels), F32), of((channels, n), BF16)),
        halo,
        far=(g2, w9),
        vmem=64,
        scratch=(shifted, pltpu.VMEM((padded, n), BF16)),
        flops=conv_flops,
    )
    aff, keep, send = call_far(
        functools.partial(wgrad_kernel, batch, count, scale),
        (
            of((8, channels), F32),
            of((keep_rows, pieces, share, width), F32),
            of((1, keep_rows, pieces, share, width), BF16),
        ),
        (stats, *halo),
        far=(x2, flipped, group_norm_gain, group_norm_bias),
        vmem=56,
        scratch=(shifted, pltpu.VMEM((channels, pieces * width), F32)),
        flops=conv_flops,
    )

    token = of((8, LANES), F32)
    if relative:
        half = nz // 2
        many = lambda k, dtype: of((*k, share, width), dtype)
        got = partner(send[0], 1)
        a_send, a_keep, b_send, b_keep, done = call(
            functools.partial(step_one, nz),
            (many((2, half), BF16), many((2, half), F32)) * 2 + (token,),
            (keep, got),
        )
        a_got, b_got = partner(a_send, cols), partner(b_send, 2)
        first = (done,)
    else:
        first = ()

    dn, sums = call_far(
        functools.partial(back_kernel, batch),
        (of((n, channels), F32), of((8, channels), F32)),
        (aff, gsum),
        far=(x2, dacts),
        vmem=58,
        after=first,
        flops=20 * n * channels,
    )
    emb = embed(timestep, embed_in, embed_out)
    temb = jnp.dot(emb, time_w, preferred_element_type=F32)

    if relative:
        s_shape = of(sums.shape, F32)
        a_send, a_keep, b_send, b_keep, sums = call(
            functools.partial(step_two, nz),
            (many((half,), BF16), many((half,), F32)) * 2 + (s_shape,),
            (a_got, a_keep, b_got, b_keep, sums, partner(sums, 1)),
        )
        a_got, b_got = partner(a_send, 2), partner(b_send, cols)
        own, sums, *sends = call(
            functools.partial(step_three, nz),
            (many((), F32), s_shape, *[many((), BF16)] * (nz - 1)),
            (a_got, a_keep, b_got, b_keep, sums, partner(sums, 2)),
            scratch=(pltpu.VMEM((nz, share, width), F32),),
        )
        gots = [partner(v, 4 * (k + 1)) for k, v in enumerate(sends)]
        gots += [partner(sums, 4 * k) for k in range(1, nz)]
        second = (sums,)
    else:
        second = ()


    block_out, done = call_far(
        functools.partial(conv_kernel, batch),
        (of((n, channels), BF16), token),
        (aff, *halo, temb),
        far=(x2, w9, conv_b),
        after=second,
        vmem=58,
        scratch=(shifted,),
        flops=conv_flops,
    )

    if relative:
        own, sums = call(
            functools.partial(step_four, nz),
            (many((), BF16), s_shape),
            (own, sums, *gots),
            after=(done,),
        )
        others = [partner(own, 2 * k) for k in range(1, pieces)]
    else:
        bit = 1
        while 2 * bit < devices:
            sums = sums + partner(sums, bit)
            bit *= 2

    vector = of((channels,), F32)
    input_grad, gain_grad, bias_grad, conv_b_grad, time_grad, done = call_far(
        functools.partial(input_kernel, batch, count, scale),
        (of((n, channels), F32), *[vector] * 3, of((channels, emb.shape[1]), F32), token),
        (aff, sums, partner(sums, cols if relative else bit), emb),
        far=(x2, g2, dn, group_norm_gain),
        vmem=60,
        flops=8 * n * channels,
    )

    if relative:
        mine = call(
            functools.partial(step_five, nz),
            of((share, pieces * width), BF16),
            (own, *others),
            after=(done,),
        )
        grad = call(
            step_six,
            of((9, 2 * share, channels), F32),
            (mine, partner(mine, 1)),
            scratch=(pltpu.VMEM((2 * share, pieces * width), F32),),
        )
    else:
        both = jnp.concatenate([keep[0, 0], send[0, 0, 0].astype(F32)], axis=0)
        both = lax.psum(both[:, : 9 * channels], AXES)
        mine = channels // rows
        grad = lax.dynamic_slice_in_dim(both, lax.axis_index("row") * mine, mine, 0)
        grad = jnp.transpose(grad.reshape(mine, 9, channels), (1, 0, 2))
    conv_w_grad = jnp.transpose(grad.reshape(3, 3, channels // rows, channels), (2, 0, 1, 3))
    return (
        block_out.reshape(latent.shape),
        input_grad.reshape(latent.shape),
        conv_w_grad,
        gain_grad,
        bias_grad,
        conv_b_grad,
        time_grad.T,
    )


def solution(mesh):
    return jax.shard_map(
        local,
        mesh=mesh,
        in_specs=(
            P(None, "row", "col", None),
            P(),
            P(),
            P(),
            P(),
            P(),
            P(),
            P(),
            P(),
            P(None, "row", "col", None),
        ),
        out_specs=(
            P(None, "row", "col", None),
            P(None, "row", "col", None),
            P("row", None, None, None),
            P(),
            P(),
            P(),
            P(),
        ),
        check_vma=False,
    )
```

```python
import functools
import math

import jax
import jax.numpy as jnp
from jax import lax
from jax.experimental import pallas as pl
from jax.experimental.pallas import tpu as pltpu
from jax.sharding import PartitionSpec as P

NORM_GROUPS = 32
EPS = 1e-05
LANES = 128
F32 = jnp.float32
BF16 = jnp.bfloat16
AXES = ("row", "col")
HI = lax.Precision.HIGHEST


def iota(shape, dim):
    return lax.broadcasted_iota(jnp.int32, shape, dim)


def call(body, out_shape, operands, far=(), after=(), scratch=(), vmem=20, flops=0):
    count, used, waits = len(far), len(operands), len(after)

    def kernel(*refs):
        ins = refs[:count]
        rest = refs[count : count + used] + refs[count + used + waits :]
        if not count:
            return body(*rest)
        holds, sems = rest[-1 - count : -1], rest[-1]
        copies = [
            pltpu.make_async_copy(ins[i], holds[i], sems.at[i]) for i in range(count)
        ]
        for c in copies:
            c.start()

        def loader(i):
            def load():
                copies[i].wait()
                return holds[i]

            return load

        body(*[loader(i) for i in range(count)], *rest[: -1 - count])

    near = pl.BlockSpec(memory_space=pltpu.VMEM)
    scratch = list(scratch)
    if count:
        scratch += [pltpu.VMEM(v.shape, v.dtype) for v in far]
        scratch.append(pltpu.SemaphoreType.DMA((count,)))
    return pl.pallas_call(
        kernel,
        out_shape=out_shape,
        in_specs=[pl.BlockSpec(memory_space=pltpu.HBM)] * count
        + [near] * used
        + [pl.BlockSpec(memory_space=pl.ANY)] * waits,
        out_specs=jax.tree.map(lambda _: near, out_shape),
        scratch_shapes=scratch,
        compiler_params=pltpu.CompilerParams(vmem_limit_bytes=vmem * 2**20),
        cost_estimate=pl.CostEstimate(flops=flops, bytes_accessed=2_000_000, transcendentals=0),
    )(*far, *operands, *after)


def call_far(body, out_shape, operands, far=(), after=(), scratch=(), vmem=58, flops=0):
    outs, tree = jax.tree.flatten(out_shape)
    ins = (*far, *operands)
    waits, own = len(after), len(scratch)
    slots = len(outs) + 4

    def kernel(*refs):
        src, refs = refs[: len(ins)], refs[len(ins) + waits :]
        dst, refs = refs[: len(outs)], refs[len(outs) :]
        mine, refs = refs[:own], refs[own:]
        held, refs = refs[: len(ins)], refs[len(ins) :]
        made, (sem_in, sem_out) = refs[: len(outs)], refs[len(outs) :]
        copies = [pltpu.make_async_copy(a, b, sem_in.at[i]) for i, (a, b) in enumerate(zip(src, held))]
        for c in (*copies[len(far) :], *copies[: len(far)]):
            c.start()

        def loader(i):
            def load():
                copies[i].wait()
                return held[i]

            return load

        sent = {}

        def emit(i, start=None, size=None):
            a, b = made[i], dst[i]
            if start is not None:
                a, b = a.at[pl.ds(start, size)], b.at[pl.ds(start, size)]
            c = pltpu.make_async_copy(a, b, sem_out.at[sum(map(len, sent.values()))])
            c.start()
            sent.setdefault(i, []).append(c)

        for c in copies[len(far) :]:
            c.wait()
        body(emit, *[loader(i) for i in range(len(far))], *held[len(far) :], *made, *mine)
        for i in range(len(outs)):
            if i not in sent:
                emit(i)
        for parts in sent.values():
            for c in parts:
                c.wait()

    hbm = pl.BlockSpec(memory_space=pltpu.HBM)
    near = pl.BlockSpec(memory_space=pltpu.VMEM)
    results = pl.pallas_call(
        kernel,
        out_shape=tuple(outs),
        in_specs=[hbm] * len(ins) + [near] * waits,
        out_specs=(hbm,) * len(outs),
        scratch_shapes=[
            *scratch,
            *[pltpu.VMEM(v.shape, v.dtype) for v in ins],
            *[pltpu.VMEM(v.shape, v.dtype) for v in outs],
            pltpu.SemaphoreType.DMA((len(ins),)),
            pltpu.SemaphoreType.DMA((slots,)),
        ],
        compiler_params=pltpu.CompilerParams(vmem_limit_bytes=vmem * 2**20),
        cost_estimate=pl.CostEstimate(flops=flops, bytes_accessed=2_000_000, transcendentals=0),
    )(*ins, *after)
    return jax.tree.unflatten(tree, results)


def group_matrix(channels, lanes):
    size = channels // NORM_GROUPS
    group = iota((channels, lanes), 1) & (NORM_GROUPS - 1)
    channel = iota((channels, lanes), 0)
    return jnp.where((channel >= group * size) & (channel < (group + 1) * size), 1.0, 0.0).astype(F32)


def group_sums(rows):
    lanes = LANES
    g = group_matrix(rows.shape[1], lanes)
    keep = iota((8, lanes), 1) < NORM_GROUPS
    s = jnp.dot(rows, g, precision=HI, preferred_element_type=F32)
    s = jnp.where(keep, s, 0.0)
    return lax.dot_general(
        s, g, (((1,), (1,)), ((), ())), precision=HI, preferred_element_type=F32
    )


def stack_rows(rows, channels):
    r = iota((8, channels), 0)
    out = jnp.zeros((8, channels), F32)
    for k, v in enumerate(rows):
        out = out + jnp.where(r == k, v, 0.0)
    return out


def stats_kernel(batch, w, emit, x_load, g_load, top_ref, low_ref, pay_ref, west_ref, east_ref):
    sums = []
    step = 64
    t = step // w
    top, low = top_ref[...].astype(F32), low_ref[...].astype(F32)
    for k, load in enumerate((x_load, g_load)):
        ref = load()
        n, channels = ref.shape
        per = n // batch
        high = per // w
        for b in range(batch):
            at = k * batch + b

            def add(i, c, b=b, k=k, ref=ref, at=at):
                start = pl.multiple_of(b * per + i * step, 16)
                v = ref[pl.ds(start, step), :].astype(F32).reshape(t, w, channels)
                west_ref[at, pl.ds(i * t + 1, t)] = v[:, :1]
                east_ref[at, pl.ds(i * t + 1, t)] = v[:, w - 1 :]
                if k:
                    return c
                return c[0] + jnp.sum(v, axis=0), c[1] + jnp.sum(v * v, axis=0)

            zero = jnp.zeros((w, channels), F32)
            s, q = lax.fori_loop(0, per // step, add, (zero, zero))
            if not k:
                sums.append((jnp.sum(s, axis=0, keepdims=True), jnp.sum(q, axis=0, keepdims=True)))
            for v, h in ((top, 0), (low, high + 1)):
                west_ref[at, h] = v[at * w : at * w + 1]
                east_ref[at, h] = v[(at + 1) * w - 1 : (at + 1) * w]
    stacked = stack_rows([r[0] for r in sums] + [r[1] for r in sums], channels)
    lanes = pay_ref.shape[-1]
    res = jnp.dot(
        stacked, group_matrix(channels, lanes), precision=HI, preferred_element_type=F32
    )
    first = iota((8, lanes), 0) * NORM_GROUPS
    lane = iota((8, lanes), 1)
    mine = (lane >= first) & (lane < first + NORM_GROUPS)
    row = jnp.sum(jnp.where(mine, res, 0.0), axis=0, keepdims=True)
    pay_ref[...] = jnp.broadcast_to(row[None], pay_ref.shape)


def affine_rows(st_ref, gain_ref, bias_ref, batch, count):
    channels = gain_ref.shape[-1]
    lanes = st_ref.shape[-1]
    total = jnp.sum(st_ref[...], axis=0)
    first = iota((8, lanes), 0) * NORM_GROUPS
    lane = iota((8, lanes), 1)
    mine = (lane >= first) & (lane < first + NORM_GROUPS)
    spread = jnp.where(mine, total, 0.0)
    sums = lax.dot_general(
        spread,
        group_matrix(channels, lanes),
        (((1,), (1,)), ((), ())),
        precision=HI,
        preferred_element_type=F32,
    )
    gain, bias = gain_ref[...].reshape(1, channels), bias_ref[...].reshape(1, channels)
    a, s, r, t = [], [], [], []
    for b in range(batch):
        mean = sums[b : b + 1] / count
        var = sums[batch + b : batch + b + 1] / count - mean * mean
        inv = lax.rsqrt(var + EPS)
        r.append(inv)
        t.append(-mean * inv)
        a.append(inv * gain)
        s.append(bias - mean * inv * gain)
    return stack_rows(a + s + r + t, channels)


def put_shifted(ap, b, h, v, left, right):
    t, w, c = v.shape
    j = iota((t, w, c), 1)
    ap[0, b, pl.ds(h, t)] = jnp.where(j == 0, left, pltpu.roll(v, 1, 1))
    ap[1, b, pl.ds(h, t)] = v
    ap[2, b, pl.ds(h, t)] = jnp.where(j == w - 1, right, pltpu.roll(v, w - 1, 1))


def edge_masks():
    ri, rn = lax.axis_index("row"), lax.axis_size("row")
    ci, cn = lax.axis_index("col"), lax.axis_size("col")
    flags = (ri == 0, ri == rn - 1, ci == 0, ci == cn - 1)
    return tuple(jnp.where(f, 0.0, 1.0) for f in flags)


def fill(ap, part, batch, fn, src_ref, halo, visit=None):
    _, _, tall, w, c = ap.shape
    high = tall - 2
    up, down, west, east = edge_masks()
    left, right, top, low = halo
    top, low = top[...].astype(F32), low[...].astype(F32)
    t = 8
    first = part * batch
    for b in range(batch):

        def body(i, carry, b=b):
            start = pl.multiple_of(b * high * w + i * t * w, 16)
            v = src_ref[pl.ds(start, t * w), :].astype(F32).reshape(t, w, c)
            h = i * t
            put_shifted(
                ap,
                b,
                h + 1,
                fn(b, v),
                fn(b, left[first + b, pl.ds(h + 1, t)]) * west,
                fn(b, right[first + b, pl.ds(h + 1, t)]) * east,
            )
            return carry if visit is None else visit(carry, v)

        out = lax.fori_loop(0, high // t, body, jnp.zeros((w, c), F32))
        if visit is not None:
            yield out
        for line, h, edge in ((top, 0, up), (low, tall - 1, down)):
            at = first + b
            put_shifted(
                ap,
                b,
                h,
                fn(b, line[at * w : (at + 1) * w].reshape(1, w, c)) * edge,
                fn(b, left[at, h : h + 1]) * (west * edge),
                fn(b, right[at, h : h + 1]) * (east * edge),
            )


def fill_acts(ap, aff, batch, x_ref, halo):
    c = ap.shape[-1]

    def act(b, x):
        v = x * aff[b : b + 1].reshape(1, 1, c) + aff[batch + b : batch + b + 1].reshape(1, 1, c)
        return v / (1.0 + jnp.exp(-v))

    for _ in fill(ap, 0, batch, act, x_ref, halo):
        pass


def gather_taps(im, ap, flip):
    _, batch, tall, w, c = ap.shape
    per = (tall - 2) * w
    for b in range(batch):
        for tap in range(9):
            kh, kw = tap // 3, tap % 3
            if flip:
                kh, kw = 2 - kh, 2 - kw
            rows = ap[kw, b, kh : kh + tall - 2].reshape(per, c).astype(BF16)
            im[b * per : (b + 1) * per, tap * c : (tap + 1) * c] = rows


def dacts_kernel(batch, relative, share, emit, *refs):
    g_load, w_load = refs[:2]
    halo = refs[2:6]
    da_ref, gsum_ref, gp_ref, ap, gt, im, wt = refs[6:]
    g_ref = g_load()
    n, c = g_ref.shape
    _, _, tall, w, _ = ap.shape
    per = (tall - 2) * w
    totals = fill(
        ap, 1, batch, lambda b, v: v, g_ref, halo, lambda tot, v: tot + jnp.sum(v, axis=0)
    )
    totals = [jnp.sum(v, axis=0, keepdims=True) for v in totals]
    gsum_ref[...] = stack_rows([jnp.zeros((1, c), F32)] * (2 * batch) + totals, c)
    wide = gt.shape[0]
    step = LANES
    for i in range(n // step):
        v = g_ref[i * step : (i + 1) * step, :].astype(F32)
        v = jnp.concatenate([v, jnp.zeros((step, wide - c), F32)], axis=1)
        gt[:, i * step : (i + 1) * step] = jnp.transpose(v).astype(BF16)
    if relative:
        me = lax.axis_index("row") * 2 + (lax.axis_index("col") & 1)
        for q in range(4):
            other = (me ^ ((q % 2) * 2 + q // 2)) * share
            gp_ref[q * share : (q + 1) * share, :] = gt[pl.ds(pl.multiple_of(other, 16), share), :]
    else:
        gp_ref[...] = gt[:c, :]
    emit(1)
    emit(2)
    gather_taps(im, ap, True)
    w_ref = w_load()
    for tap in range(9):
        wt[:, tap * c : (tap + 1) * c] = w_ref[tap]
    for b in range(batch):
        da_ref[b * per : (b + 1) * per, :] = lax.dot_general(
            im[b * per : (b + 1) * per, : 9 * c],
            wt[...],
            (((1,), (1,)), ((), ())),
            preferred_element_type=F32,
        )
        emit(0, b * per, per)


def wgrad_kernel(batch, count, scale, emit, *refs):
    x_load, gp_load, gain_load, bias_load, st_ref = refs[:5]
    halo = refs[5:9]
    aff_ref, keep_ref, send_ref = refs[9:12]
    ap, part, im = refs[12:]
    aff = affine_rows(st_ref, gain_load(), bias_load(), batch, count)
    aff_ref[...] = aff
    emit(0)
    x_ref = x_load()
    n, channels = x_ref.shape
    _, rows, pieces, share, width = send_ref.shape
    fill_acts(ap, aff, batch, x_ref, halo)
    part[:, 9 * channels :] = jnp.zeros((channels, part.shape[1] - 9 * channels), F32)
    gather_taps(im, ap, False)
    gp = gp_load()
    part[:, : 9 * channels] = (
        jnp.dot(gp[...], im[...], preferred_element_type=F32) * scale
    )
    for r in range(rows):
        for p in range(pieces):
            lane = slice(p * width, (p + 1) * width)
            low = (rows + r) * share
            send_ref[0, r, p] = part[low : low + share, lane].astype(BF16)
    emit(2)
    for r in range(rows):
        for p in range(pieces):
            lane = slice(p * width, (p + 1) * width)
            keep_ref[r, p] = part[r * share : (r + 1) * share, lane]
        emit(1, r, 1)


def back_kernel(batch, emit, *refs):
    x_load, da_load, aff_ref, gsum_ref, dn_ref, sums_ref = refs
    n, c = dn_ref.shape
    per = n // batch
    rows = []
    aff = aff_ref[...]
    x_ref, da_ref = x_load(), da_load()
    for b in range(batch):
        a, s, r, o = (aff[k * batch + b : k * batch + b + 1] for k in range(4))

        def body(i, carry, b=b, a=a, s=s, r=r, o=o):
            rows_here = pl.ds(pl.multiple_of(b * per + i * 64, 16), 64)
            x = x_ref[rows_here, :].astype(F32)
            normed = x * a + s
            sig = 1.0 / (1.0 + jnp.exp(-normed))
            dn = da_ref[rows_here, :] * sig * (1.0 + normed * (1.0 - sig))
            dn_ref[rows_here, :] = dn
            xhat = x * r + o
            return (
                carry[0] + jnp.sum(dn.reshape(8, 8, c), axis=0),
                carry[1] + jnp.sum((dn * xhat).reshape(8, 8, c), axis=0),
            )

        zero = jnp.zeros((8, c), F32)
        rows.append(lax.fori_loop(0, per // 64, body, (zero, zero)))
        emit(0, b * per, per)
    sums_ref[...] = gsum_ref[...] + stack_rows(
        [jnp.sum(v[0], axis=0, keepdims=True) for v in rows]
        + [jnp.sum(v[1], axis=0, keepdims=True) for v in rows],
        c,
    )


def conv_kernel(batch, emit, *refs):
    x_load, w_load, cb_load, aff_ref = refs[:4]
    halo = refs[4:8]
    temb_ref, out_ref, done_ref, ap, im = refs[8:]
    x_ref = x_load()
    done_ref[...] = jnp.zeros_like(done_ref)
    _, _, tall, w, c = ap.shape
    per = (tall - 2) * w
    fill_acts(ap, aff_ref[...], batch, x_ref, halo)
    gather_taps(im, ap, False)
    w_ref = w_load()
    bias = cb_load()[...].reshape(1, c)
    w = w_ref[...].reshape(9 * c, c)
    for b in range(batch):
        acc = jnp.dot(im[b * per : (b + 1) * per, :], w, preferred_element_type=F32)
        here = slice(b * per, (b + 1) * per)
        out = x_ref[here, :].astype(F32) + acc + bias + temb_ref[b : b + 1, :]
        out_ref[here, :] = out.astype(BF16)
        emit(0, b * per, per)


def input_kernel(batch, count, scale, emit, *refs):
    x_load, g_load, dn_load, gain_load, aff_ref, part_ref, other_ref, emb_ref = refs[:8]
    out_ref, gain_out, bias_out, cb_out, tw_out, done_ref = refs[8:]
    done_ref[...] = jnp.zeros_like(done_ref)
    gain_ref = gain_load()
    n, c = out_ref.shape
    per = n // batch
    red = part_ref[...] + other_ref[...]
    aff = aff_ref[...]
    gain = gain_ref[...].reshape(1, c)
    m = group_sums(red * gain) / count
    total = lambda k: sum(red[k * batch + b : k * batch + b + 1] for b in range(batch)) * scale
    bias_out[...] = total(0).reshape(c)
    gain_out[...] = total(1).reshape(c)
    cb_out[...] = total(2).reshape(c)
    rest = red[2 * batch : 3 * batch] * scale
    parts = []
    for _ in range(3):
        parts.append(rest.astype(BF16))
        rest = rest - parts[-1].astype(F32)
    emb = emb_ref[...]
    tw_out[...] = sum(
        lax.dot_general(p, emb, (((0,), (0,)), ((), ())), preferred_element_type=F32)
        for p in reversed(parts)
    )
    emit(4)
    x_ref, g_ref, dn_ref = x_load(), g_load(), dn_load()
    for b in range(batch):
        a, r, o = (aff[k * batch + b : k * batch + b + 1] for k in (0, 2, 3))
        m1 = r * m[b : b + 1]
        m2 = r * m[batch + b : batch + b + 1]

        def body(i, _, b=b, a=a, r=r, o=o, m1=m1, m2=m2):
            here = pl.ds(pl.multiple_of(b * per + i * 64, 16), 64)
            xhat = x_ref[here, :].astype(F32) * r + o
            out_ref[here, :] = g_ref[here, :].astype(F32) + (dn_ref[here, :] * a - m1 - xhat * m2)
            return 0

        lax.fori_loop(0, per // 64, body, 0)
        emit(0, b * per, per)


def place():
    col = lax.axis_index("col")
    return col & 1, (col >> 1) & 1, col >> 2


def step_one(nz, keep_ref, got_ref, a_send, a_keep, b_send, b_keep, done_ref):
    _, xb, _ = place()
    half = nz // 2
    done_ref[...] = jnp.zeros_like(done_ref)
    total = lambda r, p: keep_ref[r, p] + got_ref[r, p].astype(F32)
    for x in range(2):
        for z in range(half):
            p = x * nz + z
            a_send[x, z] = total(1, p).astype(BF16)
            a_keep[x, z] = total(0, p)
    for r in range(2):
        for z in range(half):
            b_send[r, z] = total(r, (1 - xb) * nz + half + z).astype(BF16)
            b_keep[r, z] = total(r, xb * nz + half + z)


def step_two(nz, a_got, a_keep, b_got, b_keep, s, s_got, a_send, a_next, b_send, b_next, s_next):
    _, xb, _ = place()
    s_next[...] = s[...] + s_got[...]
    for z in range(nz // 2):
        a_send[z] = (a_keep[1 - xb, z] + a_got[1 - xb, z].astype(F32)).astype(BF16)
        a_next[z] = a_keep[xb, z] + a_got[xb, z].astype(F32)
        b_send[z] = (b_keep[1, z] + b_got[1, z].astype(F32)).astype(BF16)
        b_next[z] = b_keep[0, z] + b_got[0, z].astype(F32)


def step_three(nz, a_got, a_keep, b_got, b_keep, s, s_got, own_ref, s_next, *refs):
    s_next[...] = s[...] + s_got[...]
    sends, held = refs[: nz - 1], refs[nz - 1]
    _, _, zb = place()
    half = nz // 2
    for z in range(half):
        held[z] = a_keep[z] + a_got[z].astype(F32)
        held[half + z] = b_keep[z] + b_got[z].astype(F32)
    own_ref[...] = held[zb]
    for k in range(1, nz):
        sends[k - 1][...] = held[zb ^ k].astype(BF16)


def step_four(nz, own_ref, s, *refs):
    total, sums = own_ref[...], s[...]
    for k in range(nz - 1):
        total = total + refs[k][...].astype(F32)
        sums = sums + refs[nz - 1 + k][...]
    refs[-2][...] = total.astype(BF16)
    refs[-1][...] = sums


def step_five(nz, *refs):
    out = refs[-1]
    width = refs[0].shape[-1]
    _, xb, zb = place()
    for k, ref in enumerate(refs[:-1]):
        p = (xb ^ (k % 2)) * nz + (zb ^ (k // 2))
        out[:, pl.ds(pl.multiple_of(p * width, LANES), width)] = ref[...]


def step_six(mine_ref, other_ref, out_ref, full):
    core, _, _ = place()
    share = mine_ref.shape[0]
    c = out_ref.shape[-1]
    full[pl.ds(pl.multiple_of(core * share, 16), share), :] = mine_ref[...].astype(F32)
    full[pl.ds(pl.multiple_of((1 - core) * share, 16), share), :] = other_ref[...].astype(F32)
    for tap in range(out_ref.shape[0]):
        out_ref[tap] = full[:, tap * c : (tap + 1) * c]


def embed(timestep, embed_in, embed_out):
    half = embed_in.shape[0] // 2
    freqs = jnp.exp(-math.log(10000.0) * jnp.arange(half, dtype=F32) / half)
    angles = timestep.astype(F32)[:, None] * freqs[None, :]
    sinus = jnp.concatenate([jnp.cos(angles), jnp.sin(angles)], axis=1).astype(BF16)
    first_hidden = jax.nn.silu(jnp.dot(sinus, embed_in, preferred_element_type=F32)).astype(BF16)
    return jax.nn.silu(jnp.dot(first_hidden, embed_out, preferred_element_type=F32)).astype(BF16)


def partner(value, bit):
    size = lax.axis_size("row") * lax.axis_size("col")
    return lax.ppermute(value, AXES, [(i, i ^ bit) for i in range(size)])


def shift(value, down, right):
    rows, cols = lax.axis_size("row"), lax.axis_size("col")
    pairs = []
    for r in range(rows):
        for c in range(cols):
            to = (r + down, c + right)
            if 0 <= to[0] < rows and 0 <= to[1] < cols:
                pairs.append((r * cols + c, to[0] * cols + to[1]))
    return lax.ppermute(value, AXES, pairs)


def swap(value):
    return partner(value, lax.axis_size("col"))


def local(
    latent,
    timestep,
    group_norm_gain,
    group_norm_bias,
    conv_w,
    conv_b,
    embed_in,
    embed_out,
    time_w,
    cotangent,
):
    batch, high, wide, channels = latent.shape
    rows, cols = lax.axis_size("row"), lax.axis_size("col")
    devices = rows * cols
    n = batch * high * wide
    count = high * rows * wide * cols * (channels // NORM_GROUPS)
    scale = 1.0 / math.sqrt(batch * high * rows * wide * cols)
    x2 = latent.reshape(n, channels)
    g2 = cotangent.reshape(n, channels)
    w9 = conv_w.reshape(9, channels, channels)
    of = jax.ShapeDtypeStruct

    lanes = -(-2 * batch * NORM_GROUPS // LANES) * LANES
    column = of((2 * batch, high + 2, 1, channels), F32)
    row = lax.axis_index("row")

    def edge(at):
        lines = [lax.dynamic_slice_in_dim(v, at, 1, 1) for v in (latent, cotangent)]
        return jnp.concatenate(lines, axis=0).reshape(2 * batch * wide, channels)

    if rows == 2:
        top = swap(edge(jnp.where(row == 0, high - 1, 0)))
        low = top
    else:
        top, low = shift(edge(high - 1), 1, 0), shift(edge(0), -1, 0)
    pay, west, east = call_far(
        functools.partial(stats_kernel, batch, wide),
        (of((devices, 1, lanes), F32), column, column),
        (top, low),
        far=(x2, g2),
        vmem=64,
    )
    left, right = shift(east, 0, 1), shift(west, 0, -1)
    stats = lax.all_to_all(pay, AXES, 0, 0)
    halo = (left, right, top, low)

    neighbours = pltpu.VMEM((n, 9 * channels), BF16)
    shifted = pltpu.VMEM((3, batch, high + 2, wide, channels), F32)
    nz = cols // 4
    share = channels // (2 * rows)
    relative = rows == 2 and nz >= 2 and share % 16 == 0
    pieces = cols // 2 if relative else 1
    width = -(-9 * channels // (LANES * pieces)) * LANES
    padded = -(-channels // LANES) * LANES
    conv_flops = 2 * 9 * n * channels * channels
    if not relative:
        share = channels // 2
    keep_rows = rows if relative else 1
    dacts, gsum, flipped = call_far(
        functools.partial(dacts_kernel, batch, relative, share),
        (of((n, channels), F32), of((8, channels), F32), of((channels, n), BF16)),
        halo,
        far=(g2, w9),
        vmem=64,
        scratch=(
            shifted,
            pltpu.VMEM((padded, n), BF16),
            neighbours,
            pltpu.VMEM((channels, 9 * channels), BF16),
        ),
        flops=conv_flops,
    )
    aff, keep, send = call_far(
        functools.partial(wgrad_kernel, batch, count, scale),
        (
            of((8, channels), F32),
            of((keep_rows, pieces, share, width), F32),
            of((1, keep_rows, pieces, share, width), BF16),
        ),
        (stats, *halo),
        far=(x2, flipped, group_norm_gain, group_norm_bias),
        vmem=56,
        scratch=(shifted, pltpu.VMEM((channels, pieces * width), F32), neighbours),
        flops=conv_flops,
    )

    token = of((8, LANES), F32)
    if relative:
        half = nz // 2
        many = lambda k, dtype: of((*k, share, width), dtype)
        got = partner(send[0], 1)
        a_send, a_keep, b_send, b_keep, done = call(
            functools.partial(step_one, nz),
            (many((2, half), BF16), many((2, half), F32)) * 2 + (token,),
            (keep, got),
        )
        a_got, b_got = partner(a_send, cols), partner(b_send, 2)
        first = (done,)
    else:
        first = ()

    dn, sums = call_far(
        functools.partial(back_kernel, batch),
        (of((n, channels), F32), of((8, channels), F32)),
        (aff, gsum),
        far=(x2, dacts),
        vmem=58,
        after=first,
        flops=20 * n * channels,
    )
    emb = embed(timestep, embed_in, embed_out)
    temb = jnp.dot(emb, time_w, preferred_element_type=F32)

    if relative:
        s_shape = of(sums.shape, F32)
        a_send, a_keep, b_send, b_keep, sums = call(
            functools.partial(step_two, nz),
            (many((half,), BF16), many((half,), F32)) * 2 + (s_shape,),
            (a_got, a_keep, b_got, b_keep, sums, partner(sums, 1)),
        )
        a_got, b_got = partner(a_send, 2), partner(b_send, cols)
        own, sums, *sends = call(
            functools.partial(step_three, nz),
            (many((), F32), s_shape, *[many((), BF16)] * (nz - 1)),
            (a_got, a_keep, b_got, b_keep, sums, partner(sums, 2)),
            scratch=(pltpu.VMEM((nz, share, width), F32),),
        )
        gots = [partner(v, 4 * (k + 1)) for k, v in enumerate(sends)]
        gots += [partner(sums, 4 * k) for k in range(1, nz)]
        second = (sums,)
    else:
        second = ()


    block_out, done = call_far(
        functools.partial(conv_kernel, batch),
        (of((n, channels), BF16), token),
        (aff, *halo, temb),
        far=(x2, w9, conv_b),
        after=second,
        vmem=58,
        scratch=(shifted, neighbours),
        flops=conv_flops,
    )

    if relative:
        own, sums = call(
            functools.partial(step_four, nz),
            (many((), BF16), s_shape),
            (own, sums, *gots),
            after=(done,),
        )
        others = [partner(own, 2 * k) for k in range(1, pieces)]
    else:
        bit = 1
        while 2 * bit < devices:
            sums = sums + partner(sums, bit)
            bit *= 2

    vector = of((channels,), F32)
    input_grad, gain_grad, bias_grad, conv_b_grad, time_grad, done = call_far(
        functools.partial(input_kernel, batch, count, scale),
        (of((n, channels), F32), *[vector] * 3, of((channels, emb.shape[1]), F32), token),
        (aff, sums, partner(sums, cols if relative else bit), emb),
        far=(x2, g2, dn, group_norm_gain),
        vmem=60,
        flops=8 * n * channels,
    )

    if relative:
        mine = call(
            functools.partial(step_five, nz),
            of((share, pieces * width), BF16),
            (own, *others),
            after=(done,),
        )
        grad = call(
            step_six,
            of((9, 2 * share, channels), F32),
            (mine, partner(mine, 1)),
            scratch=(pltpu.VMEM((2 * share, pieces * width), F32),),
        )
    else:
        both = jnp.concatenate([keep[0, 0], send[0, 0, 0].astype(F32)], axis=0)
        both = lax.psum(both[:, : 9 * channels], AXES)
        mine = channels // rows
        grad = lax.dynamic_slice_in_dim(both, lax.axis_index("row") * mine, mine, 0)
        grad = jnp.transpose(grad.reshape(mine, 9, channels), (1, 0, 2))
    conv_w_grad = jnp.transpose(grad.reshape(3, 3, channels // rows, channels), (2, 0, 1, 3))
    return (
        block_out.reshape(latent.shape),
        input_grad.reshape(latent.shape),
        conv_w_grad,
        gain_grad,
        bias_grad,
        conv_b_grad,
        time_grad.T,
    )


def solution(mesh):
    return jax.shard_map(
        local,
        mesh=mesh,
        in_specs=(
            P(None, "row", "col", None),
            P(),
            P(),
            P(),
            P(),
            P(),
            P(),
            P(),
            P(),
            P(None, "row", "col", None),
        ),
        out_specs=(
            P(None, "row", "col", None),
            P(None, "row", "col", None),
            P("row", None, None, None),
            P(),
            P(),
            P(),
            P(),
        ),
        check_vma=False,
    )
```

```python
import functools
import math

import jax
import jax.numpy as jnp
from jax import lax
from jax.experimental import pallas as pl
from jax.experimental.pallas import tpu as pltpu
from jax.sharding import PartitionSpec as P

NORM_GROUPS = 32
EPS = 1e-05
LANES = 128
F32 = jnp.float32
BF16 = jnp.bfloat16
AXES = ("row", "col")
HI = lax.Precision.HIGHEST


def iota(shape, dim):
    return lax.broadcasted_iota(jnp.int32, shape, dim)


def call(body, out_shape, operands, far=(), after=(), scratch=(), vmem=20, flops=0):
    count, used, waits = len(far), len(operands), len(after)

    def kernel(*refs):
        ins = refs[:count]
        rest = refs[count : count + used] + refs[count + used + waits :]
        if not count:
            return body(*rest)
        holds, sems = rest[-1 - count : -1], rest[-1]
        copies = [
            pltpu.make_async_copy(ins[i], holds[i], sems.at[i]) for i in range(count)
        ]
        for c in copies:
            c.start()

        def loader(i):
            def load():
                copies[i].wait()
                return holds[i]

            return load

        body(*[loader(i) for i in range(count)], *rest[: -1 - count])

    near = pl.BlockSpec(memory_space=pltpu.VMEM)
    scratch = list(scratch)
    if count:
        scratch += [pltpu.VMEM(v.shape, v.dtype) for v in far]
        scratch.append(pltpu.SemaphoreType.DMA((count,)))
    return pl.pallas_call(
        kernel,
        out_shape=out_shape,
        in_specs=[pl.BlockSpec(memory_space=pltpu.HBM)] * count
        + [near] * used
        + [pl.BlockSpec(memory_space=pl.ANY)] * waits,
        out_specs=jax.tree.map(lambda _: near, out_shape),
        scratch_shapes=scratch,
        compiler_params=pltpu.CompilerParams(vmem_limit_bytes=vmem * 2**20),
        cost_estimate=pl.CostEstimate(flops=flops, bytes_accessed=2_000_000, transcendentals=0),
    )(*far, *operands, *after)


def call_far(body, out_shape, operands, far=(), after=(), scratch=(), vmem=58, flops=0):
    outs, tree = jax.tree.flatten(out_shape)
    ins = (*far, *operands)
    waits, own = len(after), len(scratch)
    slots = len(outs) + 4

    def kernel(*refs):
        src, refs = refs[: len(ins)], refs[len(ins) + waits :]
        dst, refs = refs[: len(outs)], refs[len(outs) :]
        mine, refs = refs[:own], refs[own:]
        held, refs = refs[: len(ins)], refs[len(ins) :]
        made, (sem_in, sem_out) = refs[: len(outs)], refs[len(outs) :]
        copies = [pltpu.make_async_copy(a, b, sem_in.at[i]) for i, (a, b) in enumerate(zip(src, held))]
        for c in (*copies[len(far) :], *copies[: len(far)]):
            c.start()

        def loader(i):
            def load():
                copies[i].wait()
                return held[i]

            return load

        sent = {}

        def emit(i, start=None, size=None):
            a, b = made[i], dst[i]
            if start is not None:
                a, b = a.at[pl.ds(start, size)], b.at[pl.ds(start, size)]
            c = pltpu.make_async_copy(a, b, sem_out.at[sum(map(len, sent.values()))])
            c.start()
            sent.setdefault(i, []).append(c)

        for c in copies[len(far) :]:
            c.wait()
        body(emit, *[loader(i) for i in range(len(far))], *held[len(far) :], *made, *mine)
        for i in range(len(outs)):
            if i not in sent:
                emit(i)
        for parts in sent.values():
            for c in parts:
                c.wait()

    hbm = pl.BlockSpec(memory_space=pltpu.HBM)
    near = pl.BlockSpec(memory_space=pltpu.VMEM)
    results = pl.pallas_call(
        kernel,
        out_shape=tuple(outs),
        in_specs=[hbm] * len(ins) + [near] * waits,
        out_specs=(hbm,) * len(outs),
        scratch_shapes=[
            *scratch,
            *[pltpu.VMEM(v.shape, v.dtype) for v in ins],
            *[pltpu.VMEM(v.shape, v.dtype) for v in outs],
            pltpu.SemaphoreType.DMA((len(ins),)),
            pltpu.SemaphoreType.DMA((slots,)),
        ],
        compiler_params=pltpu.CompilerParams(vmem_limit_bytes=vmem * 2**20),
        cost_estimate=pl.CostEstimate(flops=flops, bytes_accessed=2_000_000, transcendentals=0),
    )(*ins, *after)
    return jax.tree.unflatten(tree, results)


def group_matrix(channels, lanes):
    size = channels // NORM_GROUPS
    group = iota((channels, lanes), 1) & (NORM_GROUPS - 1)
    channel = iota((channels, lanes), 0)
    return jnp.where((channel >= group * size) & (channel < (group + 1) * size), 1.0, 0.0).astype(F32)


def group_sums(rows):
    lanes = LANES
    g = group_matrix(rows.shape[1], lanes)
    keep = iota((8, lanes), 1) < NORM_GROUPS
    s = jnp.dot(rows, g, precision=HI, preferred_element_type=F32)
    s = jnp.where(keep, s, 0.0)
    return lax.dot_general(
        s, g, (((1,), (1,)), ((), ())), precision=HI, preferred_element_type=F32
    )


def stack_rows(rows, channels):
    r = iota((8, channels), 0)
    out = jnp.zeros((8, channels), F32)
    for k, v in enumerate(rows):
        out = out + jnp.where(r == k, v, 0.0)
    return out


def stats_kernel(batch, w, emit, x_load, g_load, top_ref, low_ref, pay_ref, west_ref, east_ref):
    sums = []
    step = 64
    t = step // w
    top, low = top_ref[...].astype(F32), low_ref[...].astype(F32)
    for k, load in enumerate((x_load, g_load)):
        ref = load()
        n, channels = ref.shape
        per = n // batch
        high = per // w
        for b in range(batch):
            at = k * batch + b

            def add(i, c, b=b, k=k, ref=ref, at=at):
                start = pl.multiple_of(b * per + i * step, 16)
                v = ref[pl.ds(start, step), :].astype(F32).reshape(t, w, channels)
                west_ref[at, pl.ds(i * t + 1, t)] = v[:, :1]
                east_ref[at, pl.ds(i * t + 1, t)] = v[:, w - 1 :]
                if k:
                    return c
                return c[0] + jnp.sum(v, axis=0), c[1] + jnp.sum(v * v, axis=0)

            zero = jnp.zeros((w, channels), F32)
            s, q = lax.fori_loop(0, per // step, add, (zero, zero))
            if not k:
                sums.append((jnp.sum(s, axis=0, keepdims=True), jnp.sum(q, axis=0, keepdims=True)))
            for v, h in ((top, 0), (low, high + 1)):
                west_ref[at, h] = v[at * w : at * w + 1]
                east_ref[at, h] = v[(at + 1) * w - 1 : (at + 1) * w]
    stacked = stack_rows([r[0] for r in sums] + [r[1] for r in sums], channels)
    lanes = pay_ref.shape[-1]
    res = jnp.dot(
        stacked, group_matrix(channels, lanes), precision=HI, preferred_element_type=F32
    )
    first = iota((8, lanes), 0) * NORM_GROUPS
    lane = iota((8, lanes), 1)
    mine = (lane >= first) & (lane < first + NORM_GROUPS)
    row = jnp.sum(jnp.where(mine, res, 0.0), axis=0, keepdims=True)
    pay_ref[...] = jnp.broadcast_to(row[None], pay_ref.shape)


def affine_rows(st_ref, gain_ref, bias_ref, batch, count):
    channels = gain_ref.shape[-1]
    lanes = st_ref.shape[-1]
    total = jnp.sum(st_ref[...], axis=0)
    first = iota((8, lanes), 0) * NORM_GROUPS
    lane = iota((8, lanes), 1)
    mine = (lane >= first) & (lane < first + NORM_GROUPS)
    spread = jnp.where(mine, total, 0.0)
    sums = lax.dot_general(
        spread,
        group_matrix(channels, lanes),
        (((1,), (1,)), ((), ())),
        precision=HI,
        preferred_element_type=F32,
    )
    gain, bias = gain_ref[...].reshape(1, channels), bias_ref[...].reshape(1, channels)
    a, s, r, t = [], [], [], []
    for b in range(batch):
        mean = sums[b : b + 1] / count
        var = sums[batch + b : batch + b + 1] / count - mean * mean
        inv = lax.rsqrt(var + EPS)
        r.append(inv)
        t.append(-mean * inv)
        a.append(inv * gain)
        s.append(bias - mean * inv * gain)
    return stack_rows(a + s + r + t, channels)


def put_shifted(ap, b, h, v, sides):
    t, w, c = v.shape
    j = iota((t, w, c), 1)
    ap[0, b, pl.ds(h, t)] = jnp.where(j == 0, sides, pltpu.roll(v, 1, 1))
    ap[1, b, pl.ds(h, t)] = v
    ap[2, b, pl.ds(h, t)] = jnp.where(j == w - 1, sides, pltpu.roll(v, w - 1, 1))


def edge_masks():
    ri, rn = lax.axis_index("row"), lax.axis_size("row")
    ci, cn = lax.axis_index("col"), lax.axis_size("col")
    flags = (ri == 0, ri == rn - 1, ci == 0, ci == cn - 1)
    return tuple(jnp.where(f, 0.0, 1.0) for f in flags)


def fill(ap, part, batch, fn, src_ref, halo, visit=None):
    _, _, tall, w, c = ap.shape
    high = tall - 2
    up, down, west, east = edge_masks()
    left, right, top, low = halo
    top, low = top[...].astype(F32), low[...].astype(F32)
    t = 8
    first = part * batch

    def sides(b, l, r, scale):
        j = iota((l.shape[0], w, c), 1)
        return fn(b, jnp.where(j == 0, l, r)) * (jnp.where(j == 0, west, east) * scale)

    for b in range(batch):

        def body(i, carry, b=b):
            start = pl.multiple_of(b * high * w + i * t * w, 16)
            v = src_ref[pl.ds(start, t * w), :].astype(F32).reshape(t, w, c)
            h = i * t
            put_shifted(
                ap,
                b,
                h + 1,
                fn(b, v),
                sides(b, left[first + b, pl.ds(h + 1, t)], right[first + b, pl.ds(h + 1, t)], 1.0),
            )
            return carry if visit is None else visit(carry, v)

        out = lax.fori_loop(0, high // t, body, jnp.zeros((w, c), F32))
        if visit is not None:
            yield out
        for line, h, edge in ((top, 0, up), (low, tall - 1, down)):
            at = first + b
            put_shifted(
                ap,
                b,
                h,
                fn(b, line[at * w : (at + 1) * w].reshape(1, w, c)) * edge,
                sides(b, left[at, h : h + 1], right[at, h : h + 1], edge),
            )


def fill_acts(ap, aff, batch, x_ref, halo):
    c = ap.shape[-1]

    def act(b, x):
        v = x * aff[b : b + 1].reshape(1, 1, c) + aff[batch + b : batch + b + 1].reshape(1, 1, c)
        return v / (1.0 + jnp.exp(-v))

    for _ in fill(ap, 0, batch, act, x_ref, halo):
        pass


def gather_taps(im, b, ap, flip):
    _, _, tall, w, c = ap.shape
    for tap in range(9):
        kh, kw = tap // 3, tap % 3
        if flip:
            kh, kw = 2 - kh, 2 - kw
        rows = ap[kw, b, kh : kh + tall - 2].reshape((tall - 2) * w, c).astype(BF16)
        im[:, tap * c : (tap + 1) * c] = rows


def dacts_kernel(batch, relative, share, emit, *refs):
    g_load, w_load = refs[:2]
    halo = refs[2:6]
    da_ref, gsum_ref, gp_ref, ap, gt, im, wt = refs[6:]
    g_ref = g_load()
    n, c = g_ref.shape
    _, _, tall, w, _ = ap.shape
    per = (tall - 2) * w
    totals = fill(
        ap, 1, batch, lambda b, v: v, g_ref, halo, lambda tot, v: tot + jnp.sum(v, axis=0)
    )
    totals = [jnp.sum(v, axis=0, keepdims=True) for v in totals]
    gsum_ref[...] = stack_rows([jnp.zeros((1, c), F32)] * (2 * batch) + totals, c)
    wide = gt.shape[0]
    step = LANES
    for i in range(n // step):
        v = g_ref[i * step : (i + 1) * step, :].astype(F32)
        v = jnp.concatenate([v, jnp.zeros((step, wide - c), F32)], axis=1)
        gt[:, i * step : (i + 1) * step] = jnp.transpose(v).astype(BF16)
    if relative:
        me = lax.axis_index("row") * 2 + (lax.axis_index("col") & 1)
        for q in range(4):
            other = (me ^ ((q % 2) * 2 + q // 2)) * share
            gp_ref[q * share : (q + 1) * share, :] = gt[pl.ds(pl.multiple_of(other, 16), share), :]
    else:
        gp_ref[...] = gt[:c, :]
    emit(1)
    emit(2)
    w_ref = w_load()
    for tap in range(9):
        wt[:, tap * c : (tap + 1) * c] = w_ref[tap]
    for b in range(batch):
        gather_taps(im, b, ap, True)
        da_ref[b * per : (b + 1) * per, :] = lax.dot_general(
            im[...],
            wt[...],
            (((1,), (1,)), ((), ())),
            preferred_element_type=F32,
        )
        emit(0, b * per, per)


def wgrad_kernel(batch, count, scale, emit, *refs):
    x_load, gp_load, gain_load, bias_load, st_ref = refs[:5]
    halo = refs[5:9]
    aff_ref, keep_ref, send_ref = refs[9:12]
    ims = refs[12 : 12 + batch]
    ap, part = refs[12 + batch :]
    aff = affine_rows(st_ref, gain_load(), bias_load(), batch, count)
    aff_ref[...] = aff
    emit(0)
    x_ref = x_load()
    n, channels = x_ref.shape
    _, rows, pieces, share, width = send_ref.shape
    fill_acts(ap, aff, batch, x_ref, halo)
    part[:, 9 * channels :] = jnp.zeros((channels, part.shape[1] - 9 * channels), F32)
    per = n // batch
    total = jnp.zeros((channels, 9 * channels), F32)
    gp = gp_load()
    for b in range(batch):
        gather_taps(ims[b], b, ap, False)
        emit(3 + b)
        total = total + jnp.dot(
            gp[:, b * per : (b + 1) * per], ims[b][...], preferred_element_type=F32
        )
    part[:, : 9 * channels] = total * scale
    for r in range(rows):
        for p in range(pieces):
            lane = slice(p * width, (p + 1) * width)
            low = (rows + r) * share
            send_ref[0, r, p] = part[low : low + share, lane].astype(BF16)
    emit(2)
    for r in range(rows):
        for p in range(pieces):
            lane = slice(p * width, (p + 1) * width)
            keep_ref[r, p] = part[r * share : (r + 1) * share, lane]
        emit(1, r, 1)


def back_kernel(batch, emit, *refs):
    x_load, da_load, aff_ref, gsum_ref, dn_ref, sums_ref = refs
    n, c = dn_ref.shape
    per = n // batch
    rows = []
    aff = aff_ref[...]
    x_ref, da_ref = x_load(), da_load()
    for b in range(batch):
        a, s, r, o = (aff[k * batch + b : k * batch + b + 1] for k in range(4))

        def body(i, carry, b=b, a=a, s=s, r=r, o=o):
            rows_here = pl.ds(pl.multiple_of(b * per + i * 64, 16), 64)
            x = x_ref[rows_here, :].astype(F32)
            normed = x * a + s
            sig = 1.0 / (1.0 + jnp.exp(-normed))
            dn = da_ref[rows_here, :] * sig * (1.0 + normed * (1.0 - sig))
            dn_ref[rows_here, :] = dn
            xhat = x * r + o
            return (
                carry[0] + jnp.sum(dn.reshape(8, 8, c), axis=0),
                carry[1] + jnp.sum((dn * xhat).reshape(8, 8, c), axis=0),
            )

        zero = jnp.zeros((8, c), F32)
        rows.append(lax.fori_loop(0, per // 64, body, (zero, zero)))
        emit(0, b * per, per)
    sums_ref[...] = gsum_ref[...] + stack_rows(
        [jnp.sum(v[0], axis=0, keepdims=True) for v in rows]
        + [jnp.sum(v[1], axis=0, keepdims=True) for v in rows],
        c,
    )


def conv_kernel(batch, emit, *refs):
    w_load, x_load, cb_load = refs[:3]
    im_loads = refs[3 : 3 + batch]
    temb_ref, out_ref, done_ref = refs[3 + batch :]
    done_ref[...] = jnp.zeros_like(done_ref)
    n, c = out_ref.shape
    per = n // batch
    x_ref, w = x_load(), w_load()[...].reshape(9 * c, c)
    bias = cb_load()[...].reshape(1, c)
    for b in range(batch):
        acc = jnp.dot(im_loads[b]()[...], w, preferred_element_type=F32)
        here = slice(b * per, (b + 1) * per)
        out = x_ref[here, :].astype(F32) + acc + bias + temb_ref[b : b + 1, :]
        out_ref[here, :] = out.astype(BF16)
        emit(0, b * per, per)


def input_kernel(batch, count, scale, emit, *refs):
    x_load, g_load, dn_load, gain_load, aff_ref, part_ref, other_ref, emb_ref = refs[:8]
    out_ref, gain_out, bias_out, cb_out, tw_out, done_ref = refs[8:]
    done_ref[...] = jnp.zeros_like(done_ref)
    gain_ref = gain_load()
    n, c = out_ref.shape
    per = n // batch
    red = part_ref[...] + other_ref[...]
    aff = aff_ref[...]
    gain = gain_ref[...].reshape(1, c)
    m = group_sums(red * gain) / count
    total = lambda k: sum(red[k * batch + b : k * batch + b + 1] for b in range(batch)) * scale
    bias_out[...] = total(0).reshape(c)
    gain_out[...] = total(1).reshape(c)
    cb_out[...] = total(2).reshape(c)
    rest = red[2 * batch : 3 * batch] * scale
    parts = []
    for _ in range(3):
        parts.append(rest.astype(BF16))
        rest = rest - parts[-1].astype(F32)
    emb = emb_ref[...]
    tw_out[...] = sum(
        lax.dot_general(p, emb, (((0,), (0,)), ((), ())), preferred_element_type=F32)
        for p in reversed(parts)
    )
    emit(4)
    x_ref, g_ref, dn_ref = x_load(), g_load(), dn_load()
    for b in range(batch):
        a, r, o = (aff[k * batch + b : k * batch + b + 1] for k in (0, 2, 3))
        m1 = r * m[b : b + 1]
        m2 = r * m[batch + b : batch + b + 1]

        def body(i, _, b=b, a=a, r=r, o=o, m1=m1, m2=m2):
            here = pl.ds(pl.multiple_of(b * per + i * 64, 16), 64)
            xhat = x_ref[here, :].astype(F32) * r + o
            out_ref[here, :] = g_ref[here, :].astype(F32) + (dn_ref[here, :] * a - m1 - xhat * m2)
            return 0

        lax.fori_loop(0, per // 64, body, 0)
        emit(0, b * per, per)


def place():
    col = lax.axis_index("col")
    return col & 1, (col >> 1) & 1, col >> 2


def step_one(nz, keep_ref, got_ref, a_send, a_keep, b_send, b_keep, done_ref):
    _, xb, _ = place()
    half = nz // 2
    done_ref[...] = jnp.zeros_like(done_ref)
    total = lambda r, p: keep_ref[r, p] + got_ref[r, p].astype(F32)
    for x in range(2):
        for z in range(half):
            p = x * nz + z
            a_send[x, z] = total(1, p).astype(BF16)
            a_keep[x, z] = total(0, p)
    for r in range(2):
        for z in range(half):
            b_send[r, z] = total(r, (1 - xb) * nz + half + z).astype(BF16)
            b_keep[r, z] = total(r, xb * nz + half + z)


def step_two(nz, a_got, a_keep, b_got, b_keep, s, s_got, a_send, a_next, b_send, b_next, s_next):
    _, xb, _ = place()
    s_next[...] = s[...] + s_got[...]
    for z in range(nz // 2):
        a_send[z] = (a_keep[1 - xb, z] + a_got[1 - xb, z].astype(F32)).astype(BF16)
        a_next[z] = a_keep[xb, z] + a_got[xb, z].astype(F32)
        b_send[z] = (b_keep[1, z] + b_got[1, z].astype(F32)).astype(BF16)
        b_next[z] = b_keep[0, z] + b_got[0, z].astype(F32)


def step_three(nz, a_got, a_keep, b_got, b_keep, s, s_got, own_ref, s_next, *refs):
    sums = s[...] + s_got[...]
    high = sums.astype(BF16).astype(F32)
    low = (sums - high).astype(BF16).astype(F32)
    s_next[...] = high + low
    sends, held = refs[: nz - 1], refs[nz - 1]
    _, _, zb = place()
    half = nz // 2
    share, width = own_ref.shape
    rider = jnp.concatenate([high, low], axis=0)
    rider = jnp.concatenate([rider, jnp.zeros((16, width - rider.shape[1]), F32)], axis=1)
    for z in range(half):
        held[z] = a_keep[z] + a_got[z].astype(F32)
        held[half + z] = b_keep[z] + b_got[z].astype(F32)
    own_ref[...] = held[zb]
    for k in range(1, nz):
        sends[k - 1][:share, :] = held[zb ^ k].astype(BF16)
        sends[k - 1][share:, :] = rider.astype(BF16)


def step_four(nz, own_ref, s, *refs):
    total, sums = own_ref[...], s[...]
    share, c = total.shape[0], sums.shape[1]
    for k in range(nz - 1):
        total = total + refs[k][:share, :].astype(F32)
        rider = refs[k][share:, :].astype(F32)[:, :c]
        sums = sums + (rider[:8] + rider[8:])
    refs[-2][...] = total.astype(BF16)
    refs[-1][...] = sums


def step_five(nz, *refs):
    out = refs[-1]
    width = refs[0].shape[-1]
    _, xb, zb = place()
    for k, ref in enumerate(refs[:-1]):
        p = (xb ^ (k % 2)) * nz + (zb ^ (k // 2))
        out[:, pl.ds(pl.multiple_of(p * width, LANES), width)] = ref[...]


def step_six(mine_ref, other_ref, out_ref, full):
    core, _, _ = place()
    share = mine_ref.shape[0]
    c = out_ref.shape[-1]
    full[pl.ds(pl.multiple_of(core * share, 16), share), :] = mine_ref[...].astype(F32)
    full[pl.ds(pl.multiple_of((1 - core) * share, 16), share), :] = other_ref[...].astype(F32)
    for tap in range(out_ref.shape[0]):
        out_ref[tap] = full[:, tap * c : (tap + 1) * c]


def embed(timestep, embed_in, embed_out):
    half = embed_in.shape[0] // 2
    freqs = jnp.exp(-math.log(10000.0) * jnp.arange(half, dtype=F32) / half)
    angles = timestep.astype(F32)[:, None] * freqs[None, :]
    sinus = jnp.concatenate([jnp.cos(angles), jnp.sin(angles)], axis=1).astype(BF16)
    first_hidden = jax.nn.silu(jnp.dot(sinus, embed_in, preferred_element_type=F32)).astype(BF16)
    return jax.nn.silu(jnp.dot(first_hidden, embed_out, preferred_element_type=F32)).astype(BF16)


def partner(value, bit):
    size = lax.axis_size("row") * lax.axis_size("col")
    return lax.ppermute(value, AXES, [(i, i ^ bit) for i in range(size)])


def shift(value, down, right):
    rows, cols = lax.axis_size("row"), lax.axis_size("col")
    pairs = []
    for r in range(rows):
        for c in range(cols):
            to = (r + down, c + right)
            if 0 <= to[0] < rows and 0 <= to[1] < cols:
                pairs.append((r * cols + c, to[0] * cols + to[1]))
    return lax.ppermute(value, AXES, pairs)


def swap(value):
    return partner(value, lax.axis_size("col"))


def local(
    latent,
    timestep,
    group_norm_gain,
    group_norm_bias,
    conv_w,
    conv_b,
    embed_in,
    embed_out,
    time_w,
    cotangent,
):
    batch, high, wide, channels = latent.shape
    rows, cols = lax.axis_size("row"), lax.axis_size("col")
    devices = rows * cols
    n = batch * high * wide
    count = high * rows * wide * cols * (channels // NORM_GROUPS)
    scale = 1.0 / math.sqrt(batch * high * rows * wide * cols)
    x2 = latent.reshape(n, channels)
    g2 = cotangent.reshape(n, channels)
    w9 = conv_w.reshape(9, channels, channels)
    of = jax.ShapeDtypeStruct

    lanes = -(-2 * batch * NORM_GROUPS // LANES) * LANES
    column = of((2 * batch, high + 2, 1, channels), F32)
    row = lax.axis_index("row")

    def edge(at):
        lines = [lax.dynamic_slice_in_dim(v, at, 1, 1) for v in (latent, cotangent)]
        return jnp.concatenate(lines, axis=0).reshape(2 * batch * wide, channels)

    if rows == 2:
        top = swap(edge(jnp.where(row == 0, high - 1, 0)))
        low = top
    else:
        top, low = shift(edge(high - 1), 1, 0), shift(edge(0), -1, 0)
    pay, west, east = call_far(
        functools.partial(stats_kernel, batch, wide),
        (of((devices, 1, lanes), F32), column, column),
        (top, low),
        far=(x2, g2),
        vmem=64,
    )
    left, right = shift(east, 0, 1), shift(west, 0, -1)
    stats = lax.all_to_all(pay, AXES, 0, 0)
    halo = (left, right, top, low)

    per = n // batch
    neighbours = pltpu.VMEM((per, 9 * channels), BF16)
    shifted = pltpu.VMEM((3, batch, high + 2, wide, channels), F32)
    nz = cols // 4
    share = channels // (2 * rows)
    relative = rows == 2 and nz >= 2 and share % 16 == 0
    pieces = cols // 2 if relative else 1
    width = -(-9 * channels // (LANES * pieces)) * LANES
    width = max(width, -(-(channels + 1) // LANES) * LANES)
    padded = -(-channels // LANES) * LANES
    conv_flops = 2 * 9 * n * channels * channels
    if not relative:
        share = channels // 2
    keep_rows = rows if relative else 1
    dacts, gsum, flipped = call_far(
        functools.partial(dacts_kernel, batch, relative, share),
        (of((n, channels), F32), of((8, channels), F32), of((channels, n), BF16)),
        halo,
        far=(g2, w9),
        vmem=64,
        scratch=(
            shifted,
            pltpu.VMEM((padded, n), BF16),
            neighbours,
            pltpu.VMEM((channels, 9 * channels), BF16),
        ),
        flops=conv_flops,
    )
    aff, keep, send, *taps = call_far(
        functools.partial(wgrad_kernel, batch, count, scale),
        (
            of((8, channels), F32),
            of((keep_rows, pieces, share, width), F32),
            of((1, keep_rows, pieces, share, width), BF16),
            *[of((per, 9 * channels), BF16)] * batch,
        ),
        (stats, *halo),
        far=(x2, flipped, group_norm_gain, group_norm_bias),
        vmem=56,
        scratch=(shifted, pltpu.VMEM((channels, pieces * width), F32)),
        flops=conv_flops,
    )

    token = of((8, LANES), F32)
    if relative:
        half = nz // 2
        many = lambda k, dtype: of((*k, share, width), dtype)
        got = partner(send[0], 1)
        a_send, a_keep, b_send, b_keep, done = call(
            functools.partial(step_one, nz),
            (many((2, half), BF16), many((2, half), F32)) * 2 + (token,),
            (keep, got),
        )
        a_got, b_got = partner(a_send, cols), partner(b_send, 2)
        first = (done,)
    else:
        first = ()

    dn, sums = call_far(
        functools.partial(back_kernel, batch),
        (of((n, channels), F32), of((8, channels), F32)),
        (aff, gsum),
        far=(x2, dacts),
        vmem=58,
        after=first,
        flops=20 * n * channels,
    )
    emb = embed(timestep, embed_in, embed_out)
    temb = jnp.dot(emb, time_w, preferred_element_type=F32)

    if relative:
        s_shape = of(sums.shape, F32)
        a_send, a_keep, b_send, b_keep, sums = call(
            functools.partial(step_two, nz),
            (many((half,), BF16), many((half,), F32)) * 2 + (s_shape,),
            (a_got, a_keep, b_got, b_keep, sums, partner(sums, 1)),
        )
        a_got, b_got = partner(a_send, 2), partner(b_send, cols)
        own, sums, *sends = call(
            functools.partial(step_three, nz),
            (many((), F32), s_shape, *[of((share + 16, width), BF16)] * (nz - 1)),
            (a_got, a_keep, b_got, b_keep, sums, partner(sums, 2)),
            scratch=(pltpu.VMEM((nz, share, width), F32),),
        )
        gots = [partner(v, 4 * (k + 1)) for k, v in enumerate(sends)]
        second = (sums,)
    else:
        second = ()


    block_out, done = call_far(
        functools.partial(conv_kernel, batch),
        (of((n, channels), BF16), token),
        (temb,),
        far=(w9, x2, conv_b, *taps),
        after=second,
        flops=conv_flops,
    )

    if relative:
        own, sums = call(
            functools.partial(step_four, nz),
            (many((), BF16), s_shape),
            (own, sums, *gots),
            after=(done,),
        )
        others = [partner(own, 2 * k) for k in range(1, pieces)]
    else:
        bit = 1
        while 2 * bit < devices:
            sums = sums + partner(sums, bit)
            bit *= 2

    vector = of((channels,), F32)
    input_grad, gain_grad, bias_grad, conv_b_grad, time_grad, done = call_far(
        functools.partial(input_kernel, batch, count, scale),
        (of((n, channels), F32), *[vector] * 3, of((channels, emb.shape[1]), F32), token),
        (aff, sums, partner(sums, cols if relative else bit), emb),
        far=(x2, g2, dn, group_norm_gain),
        vmem=60,
        flops=8 * n * channels,
    )

    if relative:
        mine = call(
            functools.partial(step_five, nz),
            of((share, pieces * width), BF16),
            (own, *others),
            after=(done,),
        )
        grad = call(
            step_six,
            of((9, 2 * share, channels), F32),
            (mine, partner(mine, 1)),
            scratch=(pltpu.VMEM((2 * share, pieces * width), F32),),
        )
    else:
        both = jnp.concatenate([keep[0, 0], send[0, 0, 0].astype(F32)], axis=0)
        both = lax.psum(both[:, : 9 * channels], AXES)
        mine = channels // rows
        grad = lax.dynamic_slice_in_dim(both, lax.axis_index("row") * mine, mine, 0)
        grad = jnp.transpose(grad.reshape(mine, 9, channels), (1, 0, 2))
    conv_w_grad = jnp.transpose(grad.reshape(3, 3, channels // rows, channels), (2, 0, 1, 3))
    return (
        block_out.reshape(latent.shape),
        input_grad.reshape(latent.shape),
        conv_w_grad,
        gain_grad,
        bias_grad,
        conv_b_grad,
        time_grad.T,
    )


def solution(mesh):
    return jax.shard_map(
        local,
        mesh=mesh,
        in_specs=(
            P(None, "row", "col", None),
            P(),
            P(),
            P(),
            P(),
            P(),
            P(),
            P(),
            P(),
            P(None, "row", "col", None),
        ),
        out_specs=(
            P(None, "row", "col", None),
            P(None, "row", "col", None),
            P("row", None, None, None),
            P(),
            P(),
            P(),
            P(),
        ),
        check_vma=False,
    )
```

```python
import functools
import math

import jax
import jax.numpy as jnp
from jax import lax
from jax.experimental import pallas as pl
from jax.experimental.pallas import tpu as pltpu
from jax.sharding import PartitionSpec as P

NORM_GROUPS = 32
EPS = 1e-05
LANES = 128
F32 = jnp.float32
BF16 = jnp.bfloat16
AXES = ("row", "col")
HI = lax.Precision.HIGHEST


def iota(shape, dim):
    return lax.broadcasted_iota(jnp.int32, shape, dim)


def call(body, out_shape, operands, far=(), after=(), scratch=(), vmem=20, flops=0):
    count, used, waits = len(far), len(operands), len(after)

    def kernel(*refs):
        ins = refs[:count]
        rest = refs[count : count + used] + refs[count + used + waits :]
        if not count:
            return body(*rest)
        holds, sems = rest[-1 - count : -1], rest[-1]
        copies = [
            pltpu.make_async_copy(ins[i], holds[i], sems.at[i]) for i in range(count)
        ]
        for c in copies:
            c.start()

        def loader(i):
            def load():
                copies[i].wait()
                return holds[i]

            return load

        body(*[loader(i) for i in range(count)], *rest[: -1 - count])

    near = pl.BlockSpec(memory_space=pltpu.VMEM)
    scratch = list(scratch)
    if count:
        scratch += [pltpu.VMEM(v.shape, v.dtype) for v in far]
        scratch.append(pltpu.SemaphoreType.DMA((count,)))
    return pl.pallas_call(
        kernel,
        out_shape=out_shape,
        in_specs=[pl.BlockSpec(memory_space=pltpu.HBM)] * count
        + [near] * used
        + [pl.BlockSpec(memory_space=pl.ANY)] * waits,
        out_specs=jax.tree.map(lambda _: near, out_shape),
        scratch_shapes=scratch,
        compiler_params=pltpu.CompilerParams(vmem_limit_bytes=vmem * 2**20),
        cost_estimate=pl.CostEstimate(flops=flops, bytes_accessed=2_000_000, transcendentals=0),
    )(*far, *operands, *after)


def call_far(body, out_shape, operands, far=(), after=(), scratch=(), vmem=58, flops=0):
    outs, tree = jax.tree.flatten(out_shape)
    ins = (*far, *operands)
    waits, own = len(after), len(scratch)
    slots = len(outs) + 4

    def kernel(*refs):
        src, refs = refs[: len(ins)], refs[len(ins) + waits :]
        dst, refs = refs[: len(outs)], refs[len(outs) :]
        mine, refs = refs[:own], refs[own:]
        held, refs = refs[: len(ins)], refs[len(ins) :]
        made, (sem_in, sem_out) = refs[: len(outs)], refs[len(outs) :]
        copies = [pltpu.make_async_copy(a, b, sem_in.at[i]) for i, (a, b) in enumerate(zip(src, held))]
        for c in (*copies[len(far) :], *copies[: len(far)]):
            c.start()

        def loader(i):
            def load():
                copies[i].wait()
                return held[i]

            return load

        sent = {}

        def emit(i, start=None, size=None):
            a, b = made[i], dst[i]
            if start is not None:
                a, b = a.at[pl.ds(start, size)], b.at[pl.ds(start, size)]
            c = pltpu.make_async_copy(a, b, sem_out.at[sum(map(len, sent.values()))])
            c.start()
            sent.setdefault(i, []).append(c)

        for c in copies[len(far) :]:
            c.wait()
        body(emit, *[loader(i) for i in range(len(far))], *held[len(far) :], *made, *mine)
        for i in range(len(outs)):
            if i not in sent:
                emit(i)
        for parts in sent.values():
            for c in parts:
                c.wait()

    hbm = pl.BlockSpec(memory_space=pltpu.HBM)
    near = pl.BlockSpec(memory_space=pltpu.VMEM)
    results = pl.pallas_call(
        kernel,
        out_shape=tuple(outs),
        in_specs=[hbm] * len(ins) + [near] * waits,
        out_specs=(hbm,) * len(outs),
        scratch_shapes=[
            *scratch,
            *[pltpu.VMEM(v.shape, v.dtype) for v in ins],
            *[pltpu.VMEM(v.shape, v.dtype) for v in outs],
            pltpu.SemaphoreType.DMA((len(ins),)),
            pltpu.SemaphoreType.DMA((slots,)),
        ],
        compiler_params=pltpu.CompilerParams(vmem_limit_bytes=vmem * 2**20),
        cost_estimate=pl.CostEstimate(flops=flops, bytes_accessed=2_000_000, transcendentals=0),
    )(*ins, *after)
    return jax.tree.unflatten(tree, results)


def group_matrix(channels, lanes):
    size = channels // NORM_GROUPS
    group = iota((channels, lanes), 1) & (NORM_GROUPS - 1)
    channel = iota((channels, lanes), 0)
    return jnp.where((channel >= group * size) & (channel < (group + 1) * size), 1.0, 0.0).astype(F32)


def group_sums(rows):
    lanes = LANES
    g = group_matrix(rows.shape[1], lanes)
    keep = iota((8, lanes), 1) < NORM_GROUPS
    s = jnp.dot(rows, g, precision=HI, preferred_element_type=F32)
    s = jnp.where(keep, s, 0.0)
    return lax.dot_general(
        s, g, (((1,), (1,)), ((), ())), precision=HI, preferred_element_type=F32
    )


def stack_rows(rows, channels):
    r = iota((8, channels), 0)
    out = jnp.zeros((8, channels), F32)
    for k, v in enumerate(rows):
        out = out + jnp.where(r == k, v, 0.0)
    return out


def stats_kernel(batch, w, emit, x_load, g_load, top_ref, low_ref, pay_ref, west_ref, east_ref):
    sums = []
    step = 64
    t = step // w
    top, low = top_ref[...].astype(F32), low_ref[...].astype(F32)
    for k, load in enumerate((x_load, g_load)):
        ref = load()
        n, channels = ref.shape
        per = n // batch
        high = per // w
        for b in range(batch):
            at = k * batch + b

            def add(i, c, b=b, k=k, ref=ref, at=at):
                start = pl.multiple_of(b * per + i * step, 16)
                v = ref[pl.ds(start, step), :].astype(F32).reshape(t, w, channels)
                west_ref[at, pl.ds(i * t + 1, t)] = v[:, :1]
                east_ref[at, pl.ds(i * t + 1, t)] = v[:, w - 1 :]
                if k:
                    return c
                return c[0] + jnp.sum(v, axis=0), c[1] + jnp.sum(v * v, axis=0)

            zero = jnp.zeros((w, channels), F32)
            s, q = lax.fori_loop(0, per // step, add, (zero, zero))
            if not k:
                sums.append((jnp.sum(s, axis=0, keepdims=True), jnp.sum(q, axis=0, keepdims=True)))
            for v, h in ((top, 0), (low, high + 1)):
                west_ref[at, h] = v[at * w : at * w + 1]
                east_ref[at, h] = v[(at + 1) * w - 1 : (at + 1) * w]
    stacked = stack_rows([r[0] for r in sums] + [r[1] for r in sums], channels)
    lanes = pay_ref.shape[-1]
    res = jnp.dot(
        stacked, group_matrix(channels, lanes), precision=HI, preferred_element_type=F32
    )
    first = iota((8, lanes), 0) * NORM_GROUPS
    lane = iota((8, lanes), 1)
    mine = (lane >= first) & (lane < first + NORM_GROUPS)
    row = jnp.sum(jnp.where(mine, res, 0.0), axis=0, keepdims=True)
    pay_ref[...] = jnp.broadcast_to(row[None], pay_ref.shape)


def affine_rows(st_ref, gain_ref, bias_ref, batch, count):
    channels = gain_ref.shape[-1]
    lanes = st_ref.shape[-1]
    total = jnp.sum(st_ref[...], axis=0)
    first = iota((8, lanes), 0) * NORM_GROUPS
    lane = iota((8, lanes), 1)
    mine = (lane >= first) & (lane < first + NORM_GROUPS)
    spread = jnp.where(mine, total, 0.0)
    sums = lax.dot_general(
        spread,
        group_matrix(channels, lanes),
        (((1,), (1,)), ((), ())),
        precision=HI,
        preferred_element_type=F32,
    )
    gain, bias = gain_ref[...].reshape(1, channels), bias_ref[...].reshape(1, channels)
    a, s, r, t = [], [], [], []
    for b in range(batch):
        mean = sums[b : b + 1] / count
        var = sums[batch + b : batch + b + 1] / count - mean * mean
        inv = lax.rsqrt(var + EPS)
        r.append(inv)
        t.append(-mean * inv)
        a.append(inv * gain)
        s.append(bias - mean * inv * gain)
    return stack_rows(a + s + r + t, channels)


def put_shifted(ap, b, h, v, sides):
    t, w, c = v.shape
    j = iota((t, w, c), 1)
    ap[0, b, pl.ds(h, t)] = jnp.where(j == 0, sides, pltpu.roll(v, 1, 1))
    ap[1, b, pl.ds(h, t)] = v
    ap[2, b, pl.ds(h, t)] = jnp.where(j == w - 1, sides, pltpu.roll(v, w - 1, 1))


def edge_masks():
    ri, rn = lax.axis_index("row"), lax.axis_size("row")
    ci, cn = lax.axis_index("col"), lax.axis_size("col")
    flags = (ri == 0, ri == rn - 1, ci == 0, ci == cn - 1)
    return tuple(jnp.where(f, 0.0, 1.0) for f in flags)


def fill(ap, part, batch, fn, src_ref, halo, visit=None):
    _, _, tall, w, c = ap.shape
    high = tall - 2
    up, down, west, east = edge_masks()
    left, right, top, low = halo
    top, low = top[...].astype(F32), low[...].astype(F32)
    t = 8
    first = part * batch

    def sides(b, l, r, scale):
        j = iota((l.shape[0], w, c), 1)
        return fn(b, jnp.where(j == 0, l, r)) * (jnp.where(j == 0, west, east) * scale)

    for b in range(batch):

        def body(i, carry, b=b):
            start = pl.multiple_of(b * high * w + i * t * w, 16)
            v = src_ref[pl.ds(start, t * w), :].astype(F32).reshape(t, w, c)
            h = i * t
            put_shifted(
                ap,
                b,
                h + 1,
                fn(b, v),
                sides(b, left[first + b, pl.ds(h + 1, t)], right[first + b, pl.ds(h + 1, t)], 1.0),
            )
            return carry if visit is None else visit(carry, v)

        out = lax.fori_loop(0, high // t, body, jnp.zeros((w, c), F32))
        if visit is not None:
            yield out
        for line, h, edge in ((top, 0, up), (low, tall - 1, down)):
            at = first + b
            put_shifted(
                ap,
                b,
                h,
                fn(b, line[at * w : (at + 1) * w].reshape(1, w, c)) * edge,
                sides(b, left[at, h : h + 1], right[at, h : h + 1], edge),
            )


def fill_acts(ap, aff, batch, x_ref, halo):
    c = ap.shape[-1]

    def act(b, x):
        v = x * aff[b : b + 1].reshape(1, 1, c) + aff[batch + b : batch + b + 1].reshape(1, 1, c)
        return v / (1.0 + jnp.exp(-v))

    for _ in fill(ap, 0, batch, act, x_ref, halo):
        pass


def gather_taps(im, b, ap, flip):
    _, _, tall, w, c = ap.shape
    for tap in range(9):
        kh, kw = tap // 3, tap % 3
        if flip:
            kh, kw = 2 - kh, 2 - kw
        rows = ap[kw, b, kh : kh + tall - 2].reshape((tall - 2) * w, c).astype(BF16)
        im[:, tap * c : (tap + 1) * c] = rows


def dacts_kernel(batch, relative, share, emit, *refs):
    g_load, w_load = refs[:2]
    halo = refs[2:6]
    da_ref, gsum_ref, gp_ref, ap, gt, im, wt = refs[6:]
    g_ref = g_load()
    n, c = g_ref.shape
    _, _, tall, w, _ = ap.shape
    per = (tall - 2) * w
    totals = fill(
        ap, 1, batch, lambda b, v: v, g_ref, halo, lambda tot, v: tot + jnp.sum(v, axis=0)
    )
    totals = [jnp.sum(v, axis=0, keepdims=True) for v in totals]
    gsum_ref[...] = stack_rows([jnp.zeros((1, c), F32)] * (2 * batch) + totals, c)
    wide = gt.shape[0]
    step = LANES
    for i in range(n // step):
        v = g_ref[i * step : (i + 1) * step, :].astype(F32)
        v = jnp.concatenate([v, jnp.zeros((step, wide - c), F32)], axis=1)
        gt[:, i * step : (i + 1) * step] = jnp.transpose(v).astype(BF16)
    if relative:
        me = lax.axis_index("row") * 2 + (lax.axis_index("col") & 1)
        for q in range(4):
            other = (me ^ ((q % 2) * 2 + q // 2)) * share
            gp_ref[q * share : (q + 1) * share, :] = gt[pl.ds(pl.multiple_of(other, 16), share), :]
    else:
        gp_ref[...] = gt[:c, :]
    emit(1)
    emit(2)
    w_ref = w_load()
    for tap in range(9):
        wt[:, tap * c : (tap + 1) * c] = w_ref[tap]
    for b in range(batch):
        gather_taps(im, b, ap, True)
        da_ref[b * per : (b + 1) * per, :] = lax.dot_general(
            im[...],
            wt[...],
            (((1,), (1,)), ((), ())),
            preferred_element_type=F32,
        )
        emit(0, b * per, per)


def wgrad_kernel(batch, count, scale, emit, *refs):
    x_load, gp_load, gain_load, bias_load, st_ref = refs[:5]
    halo = refs[5:9]
    aff_ref, keep_ref, send_ref = refs[9:12]
    ims = refs[12 : 12 + batch]
    ap, part = refs[12 + batch :]
    aff = affine_rows(st_ref, gain_load(), bias_load(), batch, count)
    aff_ref[...] = aff
    emit(0)
    x_ref = x_load()
    n, channels = x_ref.shape
    _, rows, pieces, share, width = send_ref.shape
    fill_acts(ap, aff, batch, x_ref, halo)
    part[:, 9 * channels :] = jnp.zeros((channels, part.shape[1] - 9 * channels), F32)
    per = n // batch
    total = jnp.zeros((channels, 9 * channels), F32)
    gp = gp_load()
    for b in range(batch):
        gather_taps(ims[b], b, ap, False)
        emit(3 + b)
        total = total + jnp.dot(
            gp[:, b * per : (b + 1) * per], ims[b][...], preferred_element_type=F32
        )
    part[:, : 9 * channels] = total * scale
    for r in range(rows):
        for p in range(pieces):
            lane = slice(p * width, (p + 1) * width)
            low = (rows + r) * share
            send_ref[0, r, p] = part[low : low + share, lane].astype(BF16)
    emit(2)
    for r in range(rows):
        for p in range(pieces):
            lane = slice(p * width, (p + 1) * width)
            keep_ref[r, p] = part[r * share : (r + 1) * share, lane]
        emit(1, r, 1)


def back_kernel(batch, emit, *refs):
    x_load, da_load, aff_ref, gsum_ref, dn_ref, sums_ref = refs
    n, c = dn_ref.shape
    per = n // batch
    rows = []
    aff = aff_ref[...]
    x_ref, da_ref = x_load(), da_load()
    for b in range(batch):
        a, s, r, o = (aff[k * batch + b : k * batch + b + 1] for k in range(4))

        def body(i, carry, b=b, a=a, s=s, r=r, o=o):
            rows_here = pl.ds(pl.multiple_of(b * per + i * 64, 16), 64)
            x = x_ref[rows_here, :].astype(F32)
            normed = x * a + s
            sig = 1.0 / (1.0 + jnp.exp(-normed))
            dn = da_ref[rows_here, :] * sig * (1.0 + normed * (1.0 - sig))
            dn_ref[rows_here, :] = dn
            xhat = x * r + o
            return (
                carry[0] + jnp.sum(dn.reshape(8, 8, c), axis=0),
                carry[1] + jnp.sum((dn * xhat).reshape(8, 8, c), axis=0),
            )

        zero = jnp.zeros((8, c), F32)
        rows.append(lax.fori_loop(0, per // 64, body, (zero, zero)))
        emit(0, b * per, per)
    sums_ref[...] = gsum_ref[...] + stack_rows(
        [jnp.sum(v[0], axis=0, keepdims=True) for v in rows]
        + [jnp.sum(v[1], axis=0, keepdims=True) for v in rows],
        c,
    )


def conv_kernel(batch, emit, *refs):
    w_load = refs[0]
    im_loads = refs[1 : 1 + batch]
    x_load, cb_load = refs[1 + batch : 3 + batch]
    temb_ref, out_ref, done_ref = refs[3 + batch :]
    done_ref[...] = jnp.zeros_like(done_ref)
    n, c = out_ref.shape
    per = n // batch
    w = w_load()[...].reshape(9 * c, c)
    for b in range(batch):
        acc = jnp.dot(im_loads[b]()[...], w, preferred_element_type=F32)
        if b == 0:
            x_ref = x_load()
            bias = cb_load()[...].reshape(1, c)
        here = slice(b * per, (b + 1) * per)
        out = x_ref[here, :].astype(F32) + acc + bias + temb_ref[b : b + 1, :]
        out_ref[here, :] = out.astype(BF16)
        emit(0, b * per, per)


def input_kernel(batch, count, scale, emit, *refs):
    x_load, g_load, dn_load, gain_load, aff_ref, part_ref, other_ref, emb_ref = refs[:8]
    out_ref, gain_out, bias_out, cb_out, tw_out = refs[8:]
    gain_ref = gain_load()
    n, c = out_ref.shape
    per = n // batch
    red = part_ref[...] + other_ref[...]
    aff = aff_ref[...]
    gain = gain_ref[...].reshape(1, c)
    m = group_sums(red * gain) / count
    total = lambda k: sum(red[k * batch + b : k * batch + b + 1] for b in range(batch)) * scale
    bias_out[...] = total(0).reshape(c)
    gain_out[...] = total(1).reshape(c)
    cb_out[...] = total(2).reshape(c)
    rest = red[2 * batch : 3 * batch] * scale
    parts = []
    for _ in range(3):
        parts.append(rest.astype(BF16))
        rest = rest - parts[-1].astype(F32)
    emb = emb_ref[...]
    tw_out[...] = sum(
        lax.dot_general(p, emb, (((0,), (0,)), ((), ())), preferred_element_type=F32)
        for p in reversed(parts)
    )
    emit(4)
    x_ref, g_ref, dn_ref = x_load(), g_load(), dn_load()
    for b in range(batch):
        a, r, o = (aff[k * batch + b : k * batch + b + 1] for k in (0, 2, 3))
        m1 = r * m[b : b + 1]
        m2 = r * m[batch + b : batch + b + 1]

        def body(i, _, b=b, a=a, r=r, o=o, m1=m1, m2=m2):
            here = pl.ds(pl.multiple_of(b * per + i * 64, 16), 64)
            xhat = x_ref[here, :].astype(F32) * r + o
            out_ref[here, :] = g_ref[here, :].astype(F32) + (dn_ref[here, :] * a - m1 - xhat * m2)
            return 0

        lax.fori_loop(0, per // 64, body, 0)
        emit(0, b * per, per)


def place():
    col = lax.axis_index("col")
    return col & 1, (col >> 1) & 1, col >> 2


def step_one(nz, keep_ref, got_ref, a_send, a_keep, b_send, b_keep):
    _, xb, _ = place()
    half = nz // 2
    total = lambda r, p: keep_ref[r, p] + got_ref[r, p].astype(F32)
    for x in range(2):
        for z in range(half):
            p = x * nz + z
            a_send[x, z] = total(1, p).astype(BF16)
            a_keep[x, z] = total(0, p)
    for r in range(2):
        for z in range(half):
            b_send[r, z] = total(r, (1 - xb) * nz + half + z).astype(BF16)
            b_keep[r, z] = total(r, xb * nz + half + z)


def step_two(nz, a_got, a_keep, b_got, b_keep, s, s_got, a_send, a_next, b_send, b_next, s_next):
    _, xb, _ = place()
    s_next[...] = s[...] + s_got[...]
    for z in range(nz // 2):
        a_send[z] = (a_keep[1 - xb, z] + a_got[1 - xb, z].astype(F32)).astype(BF16)
        a_next[z] = a_keep[xb, z] + a_got[xb, z].astype(F32)
        b_send[z] = (b_keep[1, z] + b_got[1, z].astype(F32)).astype(BF16)
        b_next[z] = b_keep[0, z] + b_got[0, z].astype(F32)


def step_three(nz, a_got, a_keep, b_got, b_keep, s, s_got, own_ref, s_next, *refs):
    sums = s[...] + s_got[...]
    high = sums.astype(BF16).astype(F32)
    low = (sums - high).astype(BF16).astype(F32)
    s_next[...] = high + low
    sends, held = refs[: nz - 1], refs[nz - 1]
    _, _, zb = place()
    half = nz // 2
    share, width = own_ref.shape
    rider = jnp.concatenate([high, low], axis=0)
    rider = jnp.concatenate([rider, jnp.zeros((16, width - rider.shape[1]), F32)], axis=1)
    for z in range(half):
        held[z] = a_keep[z] + a_got[z].astype(F32)
        held[half + z] = b_keep[z] + b_got[z].astype(F32)
    own_ref[...] = held[zb]
    for k in range(1, nz):
        sends[k - 1][:share, :] = held[zb ^ k].astype(BF16)
        sends[k - 1][share:, :] = rider.astype(BF16)


def step_four(nz, own_ref, s, *refs):
    total, sums = own_ref[...], s[...]
    share, c = total.shape[0], sums.shape[1]
    for k in range(nz - 1):
        total = total + refs[k][:share, :].astype(F32)
        rider = refs[k][share:, :].astype(F32)[:, :c]
        sums = sums + (rider[:8] + rider[8:])
    refs[-2][...] = total.astype(BF16)
    refs[-1][...] = sums


def step_five(nz, *refs):
    out = refs[-1]
    width = refs[0].shape[-1]
    _, xb, zb = place()
    for k, ref in enumerate(refs[:-1]):
        p = (xb ^ (k % 2)) * nz + (zb ^ (k // 2))
        out[:, pl.ds(pl.multiple_of(p * width, LANES), width)] = ref[...]


def step_six(mine_ref, other_ref, out_ref, full):
    core, _, _ = place()
    share = mine_ref.shape[0]
    c = out_ref.shape[-1]
    full[pl.ds(pl.multiple_of(core * share, 16), share), :] = mine_ref[...].astype(F32)
    full[pl.ds(pl.multiple_of((1 - core) * share, 16), share), :] = other_ref[...].astype(F32)
    for tap in range(out_ref.shape[0]):
        out_ref[tap] = full[:, tap * c : (tap + 1) * c]


def embed(timestep, embed_in, embed_out):
    half = embed_in.shape[0] // 2
    freqs = jnp.exp(-math.log(10000.0) * jnp.arange(half, dtype=F32) / half)
    angles = timestep.astype(F32)[:, None] * freqs[None, :]
    sinus = jnp.concatenate([jnp.cos(angles), jnp.sin(angles)], axis=1).astype(BF16)
    first_hidden = jax.nn.silu(jnp.dot(sinus, embed_in, preferred_element_type=F32)).astype(BF16)
    return jax.nn.silu(jnp.dot(first_hidden, embed_out, preferred_element_type=F32)).astype(BF16)


def partner(value, bit):
    size = lax.axis_size("row") * lax.axis_size("col")
    return lax.ppermute(value, AXES, [(i, i ^ bit) for i in range(size)])


def shift(value, down, right):
    rows, cols = lax.axis_size("row"), lax.axis_size("col")
    pairs = []
    for r in range(rows):
        for c in range(cols):
            to = (r + down, c + right)
            if 0 <= to[0] < rows and 0 <= to[1] < cols:
                pairs.append((r * cols + c, to[0] * cols + to[1]))
    return lax.ppermute(value, AXES, pairs)


def swap(value):
    return partner(value, lax.axis_size("col"))


def local(
    latent,
    timestep,
    group_norm_gain,
    group_norm_bias,
    conv_w,
    conv_b,
    embed_in,
    embed_out,
    time_w,
    cotangent,
):
    batch, high, wide, channels = latent.shape
    rows, cols = lax.axis_size("row"), lax.axis_size("col")
    devices = rows * cols
    n = batch * high * wide
    count = high * rows * wide * cols * (channels // NORM_GROUPS)
    scale = 1.0 / math.sqrt(batch * high * rows * wide * cols)
    x2 = latent.reshape(n, channels)
    g2 = cotangent.reshape(n, channels)
    w9 = conv_w.reshape(9, channels, channels)
    of = jax.ShapeDtypeStruct

    lanes = -(-2 * batch * NORM_GROUPS // LANES) * LANES
    column = of((2 * batch, high + 2, 1, channels), F32)
    row = lax.axis_index("row")

    def edge(at):
        lines = [lax.dynamic_slice_in_dim(v, at, 1, 1) for v in (latent, cotangent)]
        return jnp.concatenate(lines, axis=0).reshape(2 * batch * wide, channels)

    if rows == 2:
        top = swap(edge(jnp.where(row == 0, high - 1, 0)))
        low = top
    else:
        top, low = shift(edge(high - 1), 1, 0), shift(edge(0), -1, 0)
    pay, west, east = call_far(
        functools.partial(stats_kernel, batch, wide),
        (of((devices, 1, lanes), F32), column, column),
        (top, low),
        far=(x2, g2),
        vmem=64,
    )
    left, right = shift(east, 0, 1), shift(west, 0, -1)
    stats = lax.all_to_all(pay, AXES, 0, 0)
    halo = (left, right, top, low)

    per = n // batch
    neighbours = pltpu.VMEM((per, 9 * channels), BF16)
    shifted = pltpu.VMEM((3, batch, high + 2, wide, channels), F32)
    nz = cols // 4
    share = channels // (2 * rows)
    relative = rows == 2 and nz >= 2 and share % 16 == 0
    pieces = cols // 2 if relative else 1
    width = -(-9 * channels // (LANES * pieces)) * LANES
    width = max(width, -(-(channels + 1) // LANES) * LANES)
    padded = -(-channels // LANES) * LANES
    conv_flops = 2 * 9 * n * channels * channels
    if not relative:
        share = channels // 2
    keep_rows = rows if relative else 1
    dacts, gsum, flipped = call_far(
        functools.partial(dacts_kernel, batch, relative, share),
        (of((n, channels), F32), of((8, channels), F32), of((channels, n), BF16)),
        halo,
        far=(g2, w9),
        vmem=64,
        scratch=(
            shifted,
            pltpu.VMEM((padded, n), BF16),
            neighbours,
            pltpu.VMEM((channels, 9 * channels), BF16),
        ),
        flops=conv_flops,
    )
    aff, keep, send, *taps = call_far(
        functools.partial(wgrad_kernel, batch, count, scale),
        (
            of((8, channels), F32),
            of((keep_rows, pieces, share, width), F32),
            of((1, keep_rows, pieces, share, width), BF16),
            *[of((per, 9 * channels), BF16)] * batch,
        ),
        (stats, *halo),
        far=(x2, flipped, group_norm_gain, group_norm_bias),
        vmem=56,
        scratch=(shifted, pltpu.VMEM((channels, pieces * width), F32)),
        flops=conv_flops,
    )

    dn, sums = call_far(
        functools.partial(back_kernel, batch),
        (of((n, channels), F32), of((8, channels), F32)),
        (aff, gsum),
        far=(x2, dacts),
        vmem=58,
        flops=conv_flops,
    )

    token = of((8, LANES), F32)
    if relative:
        half = nz // 2
        many = lambda k, dtype: of((*k, share, width), dtype)
        got = partner(send[0], 1)
        a_send, a_keep, b_send, b_keep = call(
            functools.partial(step_one, nz),
            (many((2, half), BF16), many((2, half), F32)) * 2,
            (keep, got),
            after=(sums,),
        )
        a_got, b_got = partner(a_send, cols), partner(b_send, 2)

    emb = embed(timestep, embed_in, embed_out)
    temb = jnp.dot(emb, time_w, preferred_element_type=F32)

    if relative:
        s_shape = of(sums.shape, F32)
        a_send, a_keep, b_send, b_keep, sums = call(
            functools.partial(step_two, nz),
            (many((half,), BF16), many((half,), F32)) * 2 + (s_shape,),
            (a_got, a_keep, b_got, b_keep, sums, partner(sums, 1)),
        )
        a_got, b_got = partner(a_send, 2), partner(b_send, cols)
        own, sums, *sends = call(
            functools.partial(step_three, nz),
            (many((), F32), s_shape, *[of((share + 16, width), BF16)] * (nz - 1)),
            (a_got, a_keep, b_got, b_keep, sums, partner(sums, 2)),
            scratch=(pltpu.VMEM((nz, share, width), F32),),
        )
        gots = [partner(v, 4 * (k + 1)) for k, v in enumerate(sends)]
        second = (sums,)
    else:
        second = ()


    block_out, done = call_far(
        functools.partial(conv_kernel, batch),
        (of((n, channels), BF16), token),
        (temb,),
        far=(w9, *taps, x2, conv_b),
        after=second,
        flops=conv_flops,
    )

    if relative:
        own, sums = call(
            functools.partial(step_four, nz),
            (many((), BF16), s_shape),
            (own, sums, *gots),
            after=(done,),
        )
        others = [partner(own, 2 * k) for k in range(1, pieces)]
    else:
        bit = 1
        while 2 * bit < devices:
            sums = sums + partner(sums, bit)
            bit *= 2

    other_sums = partner(sums, cols if relative else bit)
    if relative:
        mine = call(
            functools.partial(step_five, nz),
            of((share, pieces * width), BF16),
            (own, *others),
            after=(other_sums,),
        )
        last = (mine,)
    else:
        last = ()

    vector = of((channels,), F32)
    input_grad, gain_grad, bias_grad, conv_b_grad, time_grad = call_far(
        functools.partial(input_kernel, batch, count, scale),
        (of((n, channels), F32), *[vector] * 3, of((channels, emb.shape[1]), F32)),
        (aff, sums, other_sums, emb),
        far=(x2, g2, dn, group_norm_gain),
        vmem=60,
        after=last,
        flops=conv_flops,
    )

    if relative:
        grad = call(
            step_six,
            of((9, 2 * share, channels), F32),
            (mine, partner(mine, 1)),
            scratch=(pltpu.VMEM((2 * share, pieces * width), F32),),
        )
    else:
        both = jnp.concatenate([keep[0, 0], send[0, 0, 0].astype(F32)], axis=0)
        both = lax.psum(both[:, : 9 * channels], AXES)
        mine = channels // rows
        grad = lax.dynamic_slice_in_dim(both, lax.axis_index("row") * mine, mine, 0)
        grad = jnp.transpose(grad.reshape(mine, 9, channels), (1, 0, 2))
    conv_w_grad = jnp.transpose(grad.reshape(3, 3, channels // rows, channels), (2, 0, 1, 3))
    return (
        block_out.reshape(latent.shape),
        input_grad.reshape(latent.shape),
        conv_w_grad,
        gain_grad,
        bias_grad,
        conv_b_grad,
        time_grad.T,
    )


def solution(mesh):
    return jax.shard_map(
        local,
        mesh=mesh,
        in_specs=(
            P(None, "row", "col", None),
            P(),
            P(),
            P(),
            P(),
            P(),
            P(),
            P(),
            P(),
            P(None, "row", "col", None),
        ),
        out_specs=(
            P(None, "row", "col", None),
            P(None, "row", "col", None),
            P("row", None, None, None),
            P(),
            P(),
            P(),
            P(),
        ),
        check_vma=False,
    )
```

```python
import functools
import math

import jax
import jax.numpy as jnp
from jax import lax
from jax.experimental import pallas as pl
from jax.experimental.pallas import tpu as pltpu
from jax.sharding import PartitionSpec as P

NORM_GROUPS = 32
EPS = 1e-05
LANES = 128
F32 = jnp.float32
BF16 = jnp.bfloat16
AXES = ("row", "col")
HI = lax.Precision.HIGHEST


def iota(shape, dim):
    return lax.broadcasted_iota(jnp.int32, shape, dim)


def call(body, out_shape, operands, far=(), after=(), scratch=(), vmem=20, flops=0):
    count, used, waits = len(far), len(operands), len(after)

    def kernel(*refs):
        ins = refs[:count]
        rest = refs[count : count + used] + refs[count + used + waits :]
        if not count:
            return body(*rest)
        holds, sems = rest[-1 - count : -1], rest[-1]
        copies = [
            pltpu.make_async_copy(ins[i], holds[i], sems.at[i]) for i in range(count)
        ]
        for c in copies:
            c.start()

        def loader(i):
            def load():
                copies[i].wait()
                return holds[i]

            return load

        body(*[loader(i) for i in range(count)], *rest[: -1 - count])

    near = pl.BlockSpec(memory_space=pltpu.VMEM)
    scratch = list(scratch)
    if count:
        scratch += [pltpu.VMEM(v.shape, v.dtype) for v in far]
        scratch.append(pltpu.SemaphoreType.DMA((count,)))
    return pl.pallas_call(
        kernel,
        out_shape=out_shape,
        in_specs=[pl.BlockSpec(memory_space=pltpu.HBM)] * count
        + [near] * used
        + [pl.BlockSpec(memory_space=pl.ANY)] * waits,
        out_specs=jax.tree.map(lambda _: near, out_shape),
        scratch_shapes=scratch,
        compiler_params=pltpu.CompilerParams(vmem_limit_bytes=vmem * 2**20),
        cost_estimate=pl.CostEstimate(flops=flops, bytes_accessed=2_000_000, transcendentals=0),
    )(*far, *operands, *after)


def call_far(body, out_shape, operands, far=(), after=(), scratch=(), vmem=58, flops=0):
    outs, tree = jax.tree.flatten(out_shape)
    ins = (*far, *operands)
    waits, own = len(after), len(scratch)
    slots = len(outs) + 4

    def kernel(*refs):
        src, refs = refs[: len(ins)], refs[len(ins) + waits :]
        dst, refs = refs[: len(outs)], refs[len(outs) :]
        mine, refs = refs[:own], refs[own:]
        held, refs = refs[: len(ins)], refs[len(ins) :]
        made, (sem_in, sem_out) = refs[: len(outs)], refs[len(outs) :]
        copies = [pltpu.make_async_copy(a, b, sem_in.at[i]) for i, (a, b) in enumerate(zip(src, held))]
        for c in (*copies[len(far) :], *copies[: len(far)]):
            c.start()

        def loader(i):
            def load():
                copies[i].wait()
                return held[i]

            return load

        sent = {}

        def emit(i, start=None, size=None):
            a, b = made[i], dst[i]
            if start is not None:
                a, b = a.at[pl.ds(start, size)], b.at[pl.ds(start, size)]
            c = pltpu.make_async_copy(a, b, sem_out.at[sum(map(len, sent.values()))])
            c.start()
            sent.setdefault(i, []).append(c)

        for c in copies[len(far) :]:
            c.wait()
        body(emit, *[loader(i) for i in range(len(far))], *held[len(far) :], *made, *mine)
        for i in range(len(outs)):
            if i not in sent:
                emit(i)
        for parts in sent.values():
            for c in parts:
                c.wait()

    hbm = pl.BlockSpec(memory_space=pltpu.HBM)
    near = pl.BlockSpec(memory_space=pltpu.VMEM)
    results = pl.pallas_call(
        kernel,
        out_shape=tuple(outs),
        in_specs=[hbm] * len(ins) + [near] * waits,
        out_specs=(hbm,) * len(outs),
        scratch_shapes=[
            *scratch,
            *[pltpu.VMEM(v.shape, v.dtype) for v in ins],
            *[pltpu.VMEM(v.shape, v.dtype) for v in outs],
            pltpu.SemaphoreType.DMA((len(ins),)),
            pltpu.SemaphoreType.DMA((slots,)),
        ],
        compiler_params=pltpu.CompilerParams(vmem_limit_bytes=vmem * 2**20),
        cost_estimate=pl.CostEstimate(flops=flops, bytes_accessed=2_000_000, transcendentals=0),
    )(*ins, *after)
    return jax.tree.unflatten(tree, results)


def group_matrix(channels, lanes):
    size = channels // NORM_GROUPS
    group = iota((channels, lanes), 1) & (NORM_GROUPS - 1)
    channel = iota((channels, lanes), 0)
    return jnp.where((channel >= group * size) & (channel < (group + 1) * size), 1.0, 0.0).astype(F32)


def group_sums(rows):
    lanes = LANES
    g = group_matrix(rows.shape[1], lanes)
    keep = iota((8, lanes), 1) < NORM_GROUPS
    s = jnp.dot(rows, g, precision=HI, preferred_element_type=F32)
    s = jnp.where(keep, s, 0.0)
    return lax.dot_general(
        s, g, (((1,), (1,)), ((), ())), precision=HI, preferred_element_type=F32
    )


def stack_rows(rows, channels):
    r = iota((8, channels), 0)
    out = jnp.zeros((8, channels), F32)
    for k, v in enumerate(rows):
        out = out + jnp.where(r == k, v, 0.0)
    return out


def stats_kernel(batch, w, emit, x_load, g_load, top_ref, low_ref, pay_ref, west_ref, east_ref):
    sums = []
    step = 64
    t = step // w
    top, low = top_ref[...].astype(F32), low_ref[...].astype(F32)
    for k, load in enumerate((x_load, g_load)):
        ref = load()
        n, channels = ref.shape
        per = n // batch
        high = per // w
        for b in range(batch):
            at = k * batch + b

            def add(i, c, b=b, k=k, ref=ref, at=at):
                start = pl.multiple_of(b * per + i * step, 16)
                v = ref[pl.ds(start, step), :].astype(F32).reshape(t, w, channels)
                west_ref[at, pl.ds(i * t + 1, t)] = v[:, :1]
                east_ref[at, pl.ds(i * t + 1, t)] = v[:, w - 1 :]
                if k:
                    return c
                return c[0] + jnp.sum(v, axis=0), c[1] + jnp.sum(v * v, axis=0)

            zero = jnp.zeros((w, channels), F32)
            s, q = lax.fori_loop(0, per // step, add, (zero, zero))
            if not k:
                sums.append((jnp.sum(s, axis=0, keepdims=True), jnp.sum(q, axis=0, keepdims=True)))
            for v, h in ((top, 0), (low, high + 1)):
                west_ref[at, h] = v[at * w : at * w + 1]
                east_ref[at, h] = v[(at + 1) * w - 1 : (at + 1) * w]
    stacked = stack_rows([r[0] for r in sums] + [r[1] for r in sums], channels)
    lanes = pay_ref.shape[-1]
    res = jnp.dot(
        stacked, group_matrix(channels, lanes), precision=HI, preferred_element_type=F32
    )
    first = iota((8, lanes), 0) * NORM_GROUPS
    lane = iota((8, lanes), 1)
    mine = (lane >= first) & (lane < first + NORM_GROUPS)
    row = jnp.sum(jnp.where(mine, res, 0.0), axis=0, keepdims=True)
    pay_ref[...] = jnp.broadcast_to(row[None], pay_ref.shape)


def affine_rows(st_ref, gain_ref, bias_ref, batch, count):
    channels = gain_ref.shape[-1]
    lanes = st_ref.shape[-1]
    total = jnp.sum(st_ref[...], axis=0)
    first = iota((8, lanes), 0) * NORM_GROUPS
    lane = iota((8, lanes), 1)
    mine = (lane >= first) & (lane < first + NORM_GROUPS)
    spread = jnp.where(mine, total, 0.0)
    sums = lax.dot_general(
        spread,
        group_matrix(channels, lanes),
        (((1,), (1,)), ((), ())),
        precision=HI,
        preferred_element_type=F32,
    )
    gain, bias = gain_ref[...].reshape(1, channels), bias_ref[...].reshape(1, channels)
    a, s, r, t = [], [], [], []
    for b in range(batch):
        mean = sums[b : b + 1] / count
        var = sums[batch + b : batch + b + 1] / count - mean * mean
        inv = lax.rsqrt(var + EPS)
        r.append(inv)
        t.append(-mean * inv)
        a.append(inv * gain)
        s.append(bias - mean * inv * gain)
    return stack_rows(a + s + r + t, channels)


def put_shifted(ap, b, h, v, sides):
    t, w, c = v.shape
    j = iota((t, w, c), 1)
    ap[0, b, pl.ds(h, t)] = jnp.where(j == 0, sides, pltpu.roll(v, 1, 1))
    ap[1, b, pl.ds(h, t)] = v
    ap[2, b, pl.ds(h, t)] = jnp.where(j == w - 1, sides, pltpu.roll(v, w - 1, 1))


def edge_masks():
    ri, rn = lax.axis_index("row"), lax.axis_size("row")
    ci, cn = lax.axis_index("col"), lax.axis_size("col")
    flags = (ri == 0, ri == rn - 1, ci == 0, ci == cn - 1)
    return tuple(jnp.where(f, 0.0, 1.0) for f in flags)


def fill(ap, part, batch, fn, src_ref, halo, visit=None):
    _, _, tall, w, c = ap.shape
    high = tall - 2
    up, down, west, east = edge_masks()
    left, right, top, low = halo
    top, low = top[...].astype(F32), low[...].astype(F32)
    t = 8
    first = part * batch

    def sides(b, l, r, scale):
        j = iota((l.shape[0], w, c), 1)
        return fn(b, jnp.where(j == 0, l, r)) * (jnp.where(j == 0, west, east) * scale)

    for b in range(batch):

        def body(i, carry, b=b):
            start = pl.multiple_of(b * high * w + i * t * w, 16)
            v = src_ref[pl.ds(start, t * w), :].astype(F32).reshape(t, w, c)
            h = i * t
            put_shifted(
                ap,
                b,
                h + 1,
                fn(b, v),
                sides(b, left[first + b, pl.ds(h + 1, t)], right[first + b, pl.ds(h + 1, t)], 1.0),
            )
            return carry if visit is None else visit(carry, v)

        out = lax.fori_loop(0, high // t, body, jnp.zeros((w, c), F32))
        if visit is not None:
            yield out
        for line, h, edge in ((top, 0, up), (low, tall - 1, down)):
            at = first + b
            put_shifted(
                ap,
                b,
                h,
                fn(b, line[at * w : (at + 1) * w].reshape(1, w, c)) * edge,
                sides(b, left[at, h : h + 1], right[at, h : h + 1], edge),
            )


def fill_acts(ap, aff, batch, x_ref, halo):
    c = ap.shape[-1]

    def act(b, x):
        v = x * aff[b : b + 1].reshape(1, 1, c) + aff[batch + b : batch + b + 1].reshape(1, 1, c)
        return v / (1.0 + jnp.exp(-v))

    for _ in fill(ap, 0, batch, act, x_ref, halo):
        pass


def gather_taps(im, b, ap, flip):
    _, _, tall, w, c = ap.shape
    for tap in range(9):
        kh, kw = tap // 3, tap % 3
        if flip:
            kh, kw = 2 - kh, 2 - kw
        rows = ap[kw, b, kh : kh + tall - 2].reshape((tall - 2) * w, c).astype(BF16)
        im[:, tap * c : (tap + 1) * c] = rows


def dacts_kernel(batch, relative, share, emit, *refs):
    g_load, w_load = refs[:2]
    halo = refs[2:6]
    da_ref, gsum_ref, gp_ref, ap, gt, im, wt = refs[6:]
    g_ref = g_load()
    n, c = g_ref.shape
    _, _, tall, w, _ = ap.shape
    per = (tall - 2) * w
    totals = fill(
        ap, 1, batch, lambda b, v: v, g_ref, halo, lambda tot, v: tot + jnp.sum(v, axis=0)
    )
    totals = [jnp.sum(v, axis=0, keepdims=True) for v in totals]
    gsum_ref[...] = stack_rows([jnp.zeros((1, c), F32)] * (2 * batch) + totals, c)
    wide = gt.shape[0]
    step = LANES
    for i in range(n // step):
        v = g_ref[i * step : (i + 1) * step, :].astype(F32)
        v = jnp.concatenate([v, jnp.zeros((step, wide - c), F32)], axis=1)
        gt[:, i * step : (i + 1) * step] = jnp.transpose(v).astype(BF16)
    if relative:
        me = lax.axis_index("row") * 2 + (lax.axis_index("col") & 1)
        for q in range(4):
            other = (me ^ ((q % 2) * 2 + q // 2)) * share
            gp_ref[q * share : (q + 1) * share, :] = gt[pl.ds(pl.multiple_of(other, 16), share), :]
    else:
        gp_ref[...] = gt[:c, :]
    emit(1)
    emit(2)
    w_ref = w_load()
    for tap in range(9):
        wt[:, tap * c : (tap + 1) * c] = w_ref[tap]
    for b in range(batch):
        gather_taps(im, b, ap, True)
        da_ref[b * per : (b + 1) * per, :] = lax.dot_general(
            im[...],
            wt[...],
            (((1,), (1,)), ((), ())),
            preferred_element_type=F32,
        )
        emit(0, b * per, per)


def wgrad_kernel(batch, count, scale, emit, *refs):
    x_load, gp_load, gain_load, bias_load, st_ref = refs[:5]
    halo = refs[5:9]
    aff_ref, keep_ref, send_ref = refs[9:12]
    ims = refs[12 : 12 + batch]
    ap, part = refs[12 + batch :]
    aff = affine_rows(st_ref, gain_load(), bias_load(), batch, count)
    aff_ref[...] = aff
    emit(0)
    x_ref = x_load()
    n, channels = x_ref.shape
    _, rows, pieces, share, width = send_ref.shape
    fill_acts(ap, aff, batch, x_ref, halo)
    part[:, 9 * channels :] = jnp.zeros((channels, part.shape[1] - 9 * channels), F32)
    per = n // batch
    total = jnp.zeros((channels, 9 * channels), F32)
    gp = gp_load()
    for b in range(batch):
        gather_taps(ims[b], b, ap, False)
        emit(3 + b)
        total = total + jnp.dot(
            gp[:, b * per : (b + 1) * per], ims[b][...], preferred_element_type=F32
        )
    part[:, : 9 * channels] = total * scale
    for r in range(rows):
        for p in range(pieces):
            lane = slice(p * width, (p + 1) * width)
            low = (rows + r) * share
            send_ref[0, r, p] = part[low : low + share, lane].astype(BF16)
    emit(2)
    for r in range(rows):
        for p in range(pieces):
            lane = slice(p * width, (p + 1) * width)
            keep_ref[r, p] = part[r * share : (r + 1) * share, lane]
        emit(1, r, 1)


def back_kernel(batch, emit, *refs):
    x_load, da_load, aff_ref, gsum_ref, dn_ref, sums_ref = refs
    n, c = dn_ref.shape
    per = n // batch
    rows = []
    aff = aff_ref[...]
    x_ref, da_ref = x_load(), da_load()
    for b in range(batch):
        a, s, r, o = (aff[k * batch + b : k * batch + b + 1] for k in range(4))

        def body(i, carry, b=b, a=a, s=s, r=r, o=o):
            rows_here = pl.ds(pl.multiple_of(b * per + i * 64, 16), 64)
            x = x_ref[rows_here, :].astype(F32)
            normed = x * a + s
            sig = 1.0 / (1.0 + jnp.exp(-normed))
            dn = da_ref[rows_here, :] * sig * (1.0 + normed * (1.0 - sig))
            dn_ref[rows_here, :] = dn
            xhat = x * r + o
            return (
                carry[0] + jnp.sum(dn.reshape(8, 8, c), axis=0),
                carry[1] + jnp.sum((dn * xhat).reshape(8, 8, c), axis=0),
            )

        zero = jnp.zeros((8, c), F32)
        rows.append(lax.fori_loop(0, per // 64, body, (zero, zero)))
        emit(0, b * per, per)
    sums_ref[...] = gsum_ref[...] + stack_rows(
        [jnp.sum(v[0], axis=0, keepdims=True) for v in rows]
        + [jnp.sum(v[1], axis=0, keepdims=True) for v in rows],
        c,
    )


def conv_kernel(batch, emit, *refs):
    w_load = refs[0]
    im_loads = refs[1 : 1 + batch]
    x_load, cb_load = refs[1 + batch : 3 + batch]
    temb_ref, out_ref, done_ref = refs[3 + batch :]
    done_ref[...] = jnp.zeros_like(done_ref)
    n, c = out_ref.shape
    per = n // batch
    w = w_load()[...].reshape(9 * c, c)
    for b in range(batch):
        acc = jnp.dot(im_loads[b]()[...], w, preferred_element_type=F32)
        if b == 0:
            x_ref = x_load()
            bias = cb_load()[...].reshape(1, c)
        here = slice(b * per, (b + 1) * per)
        out = x_ref[here, :].astype(F32) + acc + bias + temb_ref[b : b + 1, :]
        out_ref[here, :] = out.astype(BF16)
        emit(0, b * per, per)


def input_kernel(batch, count, scale, emit, *refs):
    x_load, g_load, dn_load, gain_load, aff_ref, part_ref, other_ref, emb_ref = refs[:8]
    out_ref, gain_out, bias_out, cb_out, tw_out, done_ref = refs[8:]
    done_ref[...] = jnp.zeros_like(done_ref)
    gain_ref = gain_load()
    n, c = out_ref.shape
    per = n // batch
    red = part_ref[...] + other_ref[...]
    aff = aff_ref[...]
    gain = gain_ref[...].reshape(1, c)
    m = group_sums(red * gain) / count
    total = lambda k: sum(red[k * batch + b : k * batch + b + 1] for b in range(batch)) * scale
    bias_out[...] = total(0).reshape(c)
    gain_out[...] = total(1).reshape(c)
    cb_out[...] = total(2).reshape(c)
    rest = red[2 * batch : 3 * batch] * scale
    parts = []
    for _ in range(3):
        parts.append(rest.astype(BF16))
        rest = rest - parts[-1].astype(F32)
    emb = emb_ref[...]
    tw_out[...] = sum(
        lax.dot_general(p, emb, (((0,), (0,)), ((), ())), preferred_element_type=F32)
        for p in reversed(parts)
    )
    emit(4)
    x_ref, g_ref, dn_ref = x_load(), g_load(), dn_load()
    for b in range(batch):
        a, r, o = (aff[k * batch + b : k * batch + b + 1] for k in (0, 2, 3))
        m1 = r * m[b : b + 1]
        m2 = r * m[batch + b : batch + b + 1]

        def body(i, _, b=b, a=a, r=r, o=o, m1=m1, m2=m2):
            here = pl.ds(pl.multiple_of(b * per + i * 64, 16), 64)
            xhat = x_ref[here, :].astype(F32) * r + o
            out_ref[here, :] = g_ref[here, :].astype(F32) + (dn_ref[here, :] * a - m1 - xhat * m2)
            return 0

        lax.fori_loop(0, per // 64, body, 0)
        emit(0, b * per, per)


def place():
    col = lax.axis_index("col")
    return col & 1, (col >> 1) & 1, col >> 2


def step_one(nz, keep_ref, got_ref, a_send, a_keep, b_send, b_keep):
    _, xb, _ = place()
    half = nz // 2
    total = lambda r, p: keep_ref[r, p] + got_ref[r, p].astype(F32)
    for x in range(2):
        for z in range(half):
            p = x * nz + z
            a_send[x, z] = total(1, p).astype(BF16)
            a_keep[x, z] = total(0, p)
    for r in range(2):
        for z in range(half):
            b_send[r, z] = total(r, (1 - xb) * nz + half + z).astype(BF16)
            b_keep[r, z] = total(r, xb * nz + half + z)


def step_two(nz, a_got, a_keep, b_got, b_keep, s, s_got, a_send, a_next, b_send, b_next, s_next):
    _, xb, _ = place()
    s_next[...] = s[...] + s_got[...]
    for z in range(nz // 2):
        a_send[z] = (a_keep[1 - xb, z] + a_got[1 - xb, z].astype(F32)).astype(BF16)
        a_next[z] = a_keep[xb, z] + a_got[xb, z].astype(F32)
        b_send[z] = (b_keep[1, z] + b_got[1, z].astype(F32)).astype(BF16)
        b_next[z] = b_keep[0, z] + b_got[0, z].astype(F32)


def step_three(nz, a_got, a_keep, b_got, b_keep, s, s_got, own_ref, s_next, *refs):
    sums = s[...] + s_got[...]
    high = sums.astype(BF16).astype(F32)
    low = (sums - high).astype(BF16).astype(F32)
    s_next[...] = high + low
    sends, held = refs[: nz - 1], refs[nz - 1]
    _, _, zb = place()
    half = nz // 2
    share, width = own_ref.shape
    rider = jnp.concatenate([high, low], axis=0)
    rider = jnp.concatenate([rider, jnp.zeros((16, width - rider.shape[1]), F32)], axis=1)
    for z in range(half):
        held[z] = a_keep[z] + a_got[z].astype(F32)
        held[half + z] = b_keep[z] + b_got[z].astype(F32)
    own_ref[...] = held[zb]
    for k in range(1, nz):
        sends[k - 1][:share, :] = held[zb ^ k].astype(BF16)
        sends[k - 1][share:, :] = rider.astype(BF16)


def step_four(nz, own_ref, s, *refs):
    total, sums = own_ref[...], s[...]
    share, c = total.shape[0], sums.shape[1]
    for k in range(nz - 1):
        total = total + refs[k][:share, :].astype(F32)
        rider = refs[k][share:, :].astype(F32)[:, :c]
        sums = sums + (rider[:8] + rider[8:])
    refs[-2][...] = total.astype(BF16)
    refs[-1][...] = sums


def step_five(nz, *refs):
    out = refs[-1]
    width = refs[0].shape[-1]
    _, xb, zb = place()
    for k, ref in enumerate(refs[:-1]):
        p = (xb ^ (k % 2)) * nz + (zb ^ (k // 2))
        out[:, pl.ds(pl.multiple_of(p * width, LANES), width)] = ref[...]


def step_six(mine_ref, other_ref, out_ref, full):
    core, _, _ = place()
    share = mine_ref.shape[0]
    c = out_ref.shape[-1]
    full[pl.ds(pl.multiple_of(core * share, 16), share), :] = mine_ref[...].astype(F32)
    full[pl.ds(pl.multiple_of((1 - core) * share, 16), share), :] = other_ref[...].astype(F32)
    for tap in range(out_ref.shape[0]):
        out_ref[tap] = full[:, tap * c : (tap + 1) * c]


def embed(timestep, embed_in, embed_out):
    half = embed_in.shape[0] // 2
    freqs = jnp.exp(-math.log(10000.0) * jnp.arange(half, dtype=F32) / half)
    angles = timestep.astype(F32)[:, None] * freqs[None, :]
    sinus = jnp.concatenate([jnp.cos(angles), jnp.sin(angles)], axis=1).astype(BF16)
    first_hidden = jax.nn.silu(jnp.dot(sinus, embed_in, preferred_element_type=F32)).astype(BF16)
    return jax.nn.silu(jnp.dot(first_hidden, embed_out, preferred_element_type=F32)).astype(BF16)


def partner(value, bit):
    size = lax.axis_size("row") * lax.axis_size("col")
    return lax.ppermute(value, AXES, [(i, i ^ bit) for i in range(size)])


def shift(value, down, right):
    rows, cols = lax.axis_size("row"), lax.axis_size("col")
    pairs = []
    for r in range(rows):
        for c in range(cols):
            to = (r + down, c + right)
            if 0 <= to[0] < rows and 0 <= to[1] < cols:
                pairs.append((r * cols + c, to[0] * cols + to[1]))
    return lax.ppermute(value, AXES, pairs)


def swap(value):
    return partner(value, lax.axis_size("col"))


def local(
    latent,
    timestep,
    group_norm_gain,
    group_norm_bias,
    conv_w,
    conv_b,
    embed_in,
    embed_out,
    time_w,
    cotangent,
):
    batch, high, wide, channels = latent.shape
    rows, cols = lax.axis_size("row"), lax.axis_size("col")
    devices = rows * cols
    n = batch * high * wide
    count = high * rows * wide * cols * (channels // NORM_GROUPS)
    scale = 1.0 / math.sqrt(batch * high * rows * wide * cols)
    x2 = latent.reshape(n, channels)
    g2 = cotangent.reshape(n, channels)
    w9 = conv_w.reshape(9, channels, channels)
    of = jax.ShapeDtypeStruct

    lanes = -(-2 * batch * NORM_GROUPS // LANES) * LANES
    column = of((2 * batch, high + 2, 1, channels), F32)
    row = lax.axis_index("row")

    def edge(at):
        lines = [lax.dynamic_slice_in_dim(v, at, 1, 1) for v in (latent, cotangent)]
        return jnp.concatenate(lines, axis=0).reshape(2 * batch * wide, channels)

    if rows == 2:
        top = swap(edge(jnp.where(row == 0, high - 1, 0)))
        low = top
    else:
        top, low = shift(edge(high - 1), 1, 0), shift(edge(0), -1, 0)
    pay, west, east = call_far(
        functools.partial(stats_kernel, batch, wide),
        (of((devices, 1, lanes), F32), column, column),
        (top, low),
        far=(x2, g2),
        vmem=64,
    )
    left, right = shift(east, 0, 1), shift(west, 0, -1)
    stats = lax.all_to_all(pay, AXES, 0, 0)
    halo = (left, right, top, low)

    per = n // batch
    neighbours = pltpu.VMEM((per, 9 * channels), BF16)
    shifted = pltpu.VMEM((3, batch, high + 2, wide, channels), F32)
    nz = cols // 4
    share = channels // (2 * rows)
    relative = rows == 2 and nz >= 2 and share % 16 == 0
    pieces = cols // 2 if relative else 1
    width = -(-9 * channels // (LANES * pieces)) * LANES
    width = max(width, -(-(channels + 1) // LANES) * LANES)
    padded = -(-channels // LANES) * LANES
    conv_flops = 2 * 9 * n * channels * channels
    if not relative:
        share = channels // 2
    keep_rows = rows if relative else 1
    dacts, gsum, flipped = call_far(
        functools.partial(dacts_kernel, batch, relative, share),
        (of((n, channels), F32), of((8, channels), F32), of((channels, n), BF16)),
        halo,
        far=(g2, w9),
        vmem=64,
        scratch=(
            shifted,
            pltpu.VMEM((padded, n), BF16),
            neighbours,
            pltpu.VMEM((channels, 9 * channels), BF16),
        ),
        flops=conv_flops,
    )
    aff, keep, send, *taps = call_far(
        functools.partial(wgrad_kernel, batch, count, scale),
        (
            of((8, channels), F32),
            of((keep_rows, pieces, share, width), F32),
            of((1, keep_rows, pieces, share, width), BF16),
            *[of((per, 9 * channels), BF16)] * batch,
        ),
        (stats, *halo),
        far=(x2, flipped, group_norm_gain, group_norm_bias),
        vmem=56,
        scratch=(shifted, pltpu.VMEM((channels, pieces * width), F32)),
        flops=conv_flops,
    )

    dn, sums = call_far(
        functools.partial(back_kernel, batch),
        (of((n, channels), F32), of((8, channels), F32)),
        (aff, gsum),
        far=(x2, dacts),
        vmem=58,
        flops=conv_flops,
    )

    token = of((8, LANES), F32)
    if relative:
        half = nz // 2
        many = lambda k, dtype: of((*k, share, width), dtype)
        got = partner(send[0], 1)
        a_send, a_keep, b_send, b_keep = call(
            functools.partial(step_one, nz),
            (many((2, half), BF16), many((2, half), F32)) * 2,
            (keep, got),
            after=(sums,),
        )
        a_got, b_got = partner(a_send, cols), partner(b_send, 2)

    emb = embed(timestep, embed_in, embed_out)
    temb = jnp.dot(emb, time_w, preferred_element_type=F32)

    if relative:
        s_shape = of(sums.shape, F32)
        a_send, a_keep, b_send, b_keep, sums = call(
            functools.partial(step_two, nz),
            (many((half,), BF16), many((half,), F32)) * 2 + (s_shape,),
            (a_got, a_keep, b_got, b_keep, sums, partner(sums, 1)),
        )
        a_got, b_got = partner(a_send, 2), partner(b_send, cols)
        own, sums, *sends = call(
            functools.partial(step_three, nz),
            (many((), F32), s_shape, *[of((share + 16, width), BF16)] * (nz - 1)),
            (a_got, a_keep, b_got, b_keep, sums, partner(sums, 2)),
            scratch=(pltpu.VMEM((nz, share, width), F32),),
        )
        gots = [partner(v, 4 * (k + 1)) for k, v in enumerate(sends)]
        second = (sums,)
    else:
        second = ()


    block_out, done = call_far(
        functools.partial(conv_kernel, batch),
        (of((n, channels), BF16), token),
        (temb,),
        far=(w9, *taps, x2, conv_b),
        after=second,
        flops=conv_flops,
    )

    if relative:
        own, sums = call(
            functools.partial(step_four, nz),
            (many((), BF16), s_shape),
            (own, sums, *gots),
            after=(done,),
        )
        others = [partner(own, 2 * k) for k in range(1, pieces)]
    else:
        bit = 1
        while 2 * bit < devices:
            sums = sums + partner(sums, bit)
            bit *= 2

    vector = of((channels,), F32)
    input_grad, gain_grad, bias_grad, conv_b_grad, time_grad, done = call_far(
        functools.partial(input_kernel, batch, count, scale),
        (of((n, channels), F32), *[vector] * 3, of((channels, emb.shape[1]), F32), token),
        (aff, sums, partner(sums, cols if relative else bit), emb),
        far=(x2, g2, dn, group_norm_gain),
        vmem=60,
        flops=8 * n * channels,
    )

    if relative:
        mine = call(
            functools.partial(step_five, nz),
            of((share, pieces * width), BF16),
            (own, *others),
            after=(done,),
        )
        grad = call(
            step_six,
            of((9, 2 * share, channels), F32),
            (mine, partner(mine, 1)),
            scratch=(pltpu.VMEM((2 * share, pieces * width), F32),),
        )
    else:
        both = jnp.concatenate([keep[0, 0], send[0, 0, 0].astype(F32)], axis=0)
        both = lax.psum(both[:, : 9 * channels], AXES)
        mine = channels // rows
        grad = lax.dynamic_slice_in_dim(both, lax.axis_index("row") * mine, mine, 0)
        grad = jnp.transpose(grad.reshape(mine, 9, channels), (1, 0, 2))
    conv_w_grad = jnp.transpose(grad.reshape(3, 3, channels // rows, channels), (2, 0, 1, 3))
    return (
        block_out.reshape(latent.shape),
        input_grad.reshape(latent.shape),
        conv_w_grad,
        gain_grad,
        bias_grad,
        conv_b_grad,
        time_grad.T,
    )


def solution(mesh):
    return jax.shard_map(
        local,
        mesh=mesh,
        in_specs=(
            P(None, "row", "col", None),
            P(),
            P(),
            P(),
            P(),
            P(),
            P(),
            P(),
            P(),
            P(None, "row", "col", None),
        ),
        out_specs=(
            P(None, "row", "col", None),
            P(None, "row", "col", None),
            P("row", None, None, None),
            P(),
            P(),
            P(),
            P(),
        ),
        check_vma=False,
    )
```
